32 devices in a mesh: dp: 4 (over y, x), expert: 8 (over z, core).
Axes of the slice: x: 2, y: 2, z: 4, core: 2. Of those that a mesh axis runs over, the one named last changes fastest.
Arguments:
- layer_input: bfloat16 [4096, 1024], P(('dp', 'expert')), may hold values from -6 to 6
- cotangent: bfloat16 [4096, 1024], P(('dp', 'expert')), may hold values from -6 to 6
- lengths: int32 [32], P(('dp', 'expert')), may hold values from 64 to 128, as said below
- value_routes: int32 [4096, 4, 2], P(('dp', 'expert')), may hold values from 0 to 4, all different within a row
- output_routes: int32 [4096, 4, 2], P(('dp', 'expert')), may hold values from 0 to 4, all different within a row
- ffn_routes: int32 [4096, 16], P(('dp', 'expert')), may hold values from 0 to 386, all different within a row; in each aligned block of 128 rows (0 to 127, 128 to 255, ...) at most 8 rows name the same one
- att_gain: float32 [1024], replicated, may hold values from 0.1 to 1.9
- att_shift: float32 [1024], replicated, may hold values from -1.5 to 1.5
- query_weight: bfloat16 [1024, 512], replicated, may hold values from -0.1875 to 0.1875
- key_weight: bfloat16 [1024, 512], replicated, may hold values from -0.1875 to 0.1875
- value_weight: bfloat16 [1024, 2560], replicated, may hold values from -0.1875 to 0.1875
- output_weight: bfloat16 [2560, 1024], replicated, may hold values from -1.5 to 1.5
- value_selector: bfloat16 [1024, 20], replicated, may hold values from -0.09375 to 0.09375
- output_selector: bfloat16 [1024, 20], replicated, may hold values from -0.09375 to 0.09375
- ffn_gain: float32 [1024], replicated, may hold values from 0.1 to 1.9
- ffn_shift: float32 [1024], replicated, may hold values from -1.5 to 1.5
- ffn_selector: bfloat16 [1024, 387], replicated, may hold values from -0.09375 to 0.09375
- up_weight: bfloat16 [392, 1024, 128], P('expert'), may hold values from -0.1875 to 0.1875
- down_weight: bfloat16 [392, 128, 1024], P('expert'), may hold values from -0.5 to 0.5
Outputs:
- output: bfloat16 [4096, 1024], P(('dp', 'expert'))
- input_grad: float32 [4096, 1024], P(('dp', 'expert'))
- att_gain_grad: float32 [1024], P(('dp', 'expert'))
- att_shift_grad: float32 [1024], P(('dp', 'expert'))
- query_grad: float32 [1024, 512], P(('dp', 'expert'))
- key_grad: float32 [1024, 512], P(('dp', 'expert'))
- value_grad: float32 [1024, 2560], P(('dp', 'expert'))
- output_grad: float32 [2560, 1024], P(None, ('dp', 'expert'))
- value_selector_grad: float32 [1024, 20], P(('dp', 'expert'))
- output_selector_grad: float32 [1024, 20], P(('dp', 'expert'))
- ffn_gain_grad: float32 [1024], P(('dp', 'expert'))
- ffn_shift_grad: float32 [1024], P(('dp', 'expert'))
- ffn_selector_grad: float32 [1024, 387], P(('dp', 'expert'))
- up_grad: float32 [392, 1024, 128], P('expert', 'dp')
- down_grad: float32 [392, 128, 1024], P('expert', None, 'dp')
- expert_counts: float32 [387], replicated
The draws below stay inside these ranges and needn't reach their ends.
Inputs may be any that keep to these rules, and one draw needn't show every extreme that they name: `lengths`: at least 64; one sequence of every draw has length 128. `value_routes`: the 2 experts of a token in a head differ. `output_routes`: the 2 experts of a token in a head differ. `ffn_routes`: the 16 experts of a token differ; among the 128 rows of one device no expert is named by more than 8 rows, and in some device's rows some expert is named by exactly 8.
All inputs are finite; a program needn't handle non-finite values.
Results may differ from the reference program's by a relative error of at most 0.015.
Values may be sent and summed in bfloat16 or wider, within the bound.
No kernel may reach another device: no remote copies, remote signals or barrier semaphores. Data moves between devices by JAX's collectives and lax.ppermute only.
A program may use at most 256 MiB of HBM per device.

```python
import math
from functools import partial
import jax
import jax.numpy as jnp
import numpy as np
from jax import lax

D = 1024
HEADS = 4
DH = 128
EA = 5
TOP_A = 2
EXPERTS = 387
H = 128
TOP_F = 16
TOK_DEV = 128
SEQS = 32
TOKENS = 4096
E_PAD = 392
MOST = 8


def draw_lengths(key, part):
    drawn = jax.random.randint(jax.random.fold_in(key, 11), (SEQS,), TOK_DEV // 2, TOK_DEV + 1)
    longest = jax.random.randint(jax.random.fold_in(key, 12), (), 0, SEQS)
    return jnp.where(jnp.arange(SEQS) == longest, TOK_DEV, drawn).astype(jnp.int32)


def level_of(rng, extent, cuts, low, largest):
    loudness, own = 1.0, jax.random.fold_in(rng, 6)
    for dim, parts in cuts:
        steps = jnp.exp(jax.random.uniform(jax.random.fold_in(own, dim), (parts,), jnp.float32, low / len(cuts), largest / len(cuts)))
        loudness = loudness * jnp.repeat(steps, extent[dim] // parts).reshape([-1 if axis == dim else 1 for axis in range(len(extent))])
    return loudness


def distinct(stream_key, rows, number_of, top, lift):
    order = jax.random.permutation(jax.random.fold_in(stream_key, 1), number_of)
    pull = order
    for power in range(3):
        pull = pull * pull // number_of
    pull = pull * lift // number_of
    lots = jax.random.randint(jax.random.fold_in(stream_key, 2), (rows, number_of), 0, 4096) + pull
    fixed_rows = jax.random.permutation(jax.random.fold_in(stream_key, 3), rows)[jnp.arange(number_of) % rows]
    lots = jnp.where(jnp.arange(rows)[:, None] == fixed_rows[None, :], 1 << 14, lots)
    merit = lots * number_of + jnp.arange(number_of)
    return lax.top_k(merit.astype(jnp.int32), top)[1].astype(jnp.int32)


def routed_block(stream_key, own, number, rows, count, top, limit, lean):
    ranking = jax.random.permutation(stream_key, count)
    packed, usual = shares(count, rows * top, limit, lean, True), shares(count, rows * top, limit, lean, False)
    places = jnp.arange(count)

    def named(sizes, rotation):
        used = int((sizes > 0).sum())
        fixed = max(1, used // 4)
        shifted = fixed + (places - fixed + rotation * (used - fixed)) % max(1, count - fixed)
        return jnp.zeros((count,), jnp.int32).at[ranking[jnp.where(places < fixed, places, shifted)]].set(jnp.asarray(sizes, jnp.int32))

    sizes = jnp.where(number % 4 == 0, named(packed, number // 4), named(usual, number - number // 4 - 1))
    mixed = jax.random.permutation(jax.random.fold_in(own, 3), count)
    giver, sink = mixed[0:count // 2 * 2:2], mixed[1:count // 2 * 2:2]
    room = jnp.minimum(sizes[giver] - 1, limit - sizes[sink]) // 2
    room = jnp.where((giver == ranking[0]) | (sink == ranking[0]) | (sizes[sink] == 0), 0, jnp.maximum(room, 0))
    shifted = jax.random.randint(jax.random.fold_in(own, 4), (count // 2,), 0, 1 << 20) % (room + 1)
    sizes = sizes.at[giver].add(-shifted).at[sink].add(shifted)
    labels = jnp.searchsorted(jnp.cumsum(sizes), jnp.arange(rows * top), side="right").astype(jnp.int32)
    table = labels.reshape(top, rows).T
    table = table[jax.random.permutation(jax.random.fold_in(own, 1), rows)]
    rotation = jax.random.randint(jax.random.fold_in(own, 2), (rows, 1), 0, top)
    return jnp.take_along_axis(table, (jnp.arange(top)[None, :] + rotation) % top, axis=1)


def shares(number_of, total, limit, lean, full):
    portions = [(1 << 20) // math.isqrt(rank ** lean) + 1 for rank in range(1, number_of + 1)]
    largest = limit if full else min(limit, max(-(-total // number_of), total * portions[0] // sum(portions)))
    least = 1 if total - largest >= number_of - 1 else 0
    given, spare = [largest] + [least] * (number_of - 1), total - largest - least * (number_of - 1)
    while spare > 0:
        free = [i for i in range(1, number_of) if given[i] < largest] or [i for i in range(1, number_of) if given[i] < limit]
        mass, left = sum([portions[i] for i in free]), spare
        for i in free:
            extra = min(limit - given[i], max(1, left * portions[i] // mass), spare)
            given[i] = given[i] + extra
            spare = spare - extra
    return np.array(given)


def gaussian(key, extent, width, limit, cuts=(), held_as=jnp.bfloat16):
    values = jax.random.normal(key, extent, jnp.float32) * width
    if len(cuts) > 0:
        values = level_of(key, extent, cuts, -0.22, 0.18) * values
    return jnp.clip(values, min=-limit, max=limit).astype(held_as)


def setup_inputs(seed: int = 0) -> dict:
    keys = jax.random.split(jax.random.key(seed), 20)
    layer_input = gaussian(keys[0], (TOKENS, D), 1.0, 6.0, ((0, 32),))
    cotangent = gaussian(keys[1], (TOKENS, D), 1.0, 6.0, ((0, 32),))
    lengths = draw_lengths(jax.random.fold_in(keys[19], 71), 0)
    value_routes = distinct(keys[3], TOKENS * HEADS, EA, TOP_A, 0).reshape((TOKENS, HEADS, TOP_A))
    output_routes = distinct(keys[4], TOKENS * HEADS, EA, TOP_A, 0).reshape((TOKENS, HEADS, TOP_A))
    ffn_routes_keys = jax.random.split(jax.random.fold_in(keys[5], 1), TOKENS // TOK_DEV)
    ffn_routes_turns = jax.random.permutation(jax.random.fold_in(keys[5], 3), TOKENS // TOK_DEV)
    ffn_routes = jax.vmap(lambda own, number: routed_block(jax.random.fold_in(keys[5], 2), own, number, TOK_DEV, EXPERTS, TOP_F, MOST, 1))(ffn_routes_keys, ffn_routes_turns).reshape((TOKENS, TOP_F))
    att_gain = jnp.clip(1.0 + 0.18 * jax.random.normal(keys[6], (D,), jnp.float32), 0.1, 1.9)
    att_shift = gaussian(keys[7], (D,), 0.3, 1.5, (), jnp.float32)
    query_weight = gaussian(keys[8], (D, HEADS * DH), D ** -0.5, 0.1875)
    key_weight = gaussian(keys[9], (D, HEADS * DH), D ** -0.5, 0.1875)
    value_weight = gaussian(keys[10], (D, HEADS * EA * DH), D ** -0.5, 0.1875)
    output_weight = gaussian(keys[11], (HEADS * EA * DH, D), (HEADS * TOP_A * DH * 2 // TOK_DEV) ** -0.5, 1.5)
    value_selector = gaussian(keys[12], (D, HEADS * EA), (4 * D) ** -0.5, 0.09375)
    output_selector = gaussian(keys[13], (D, HEADS * EA), (4 * D) ** -0.5, 0.09375)
    ffn_gain = jnp.clip(1.0 + 0.18 * jax.random.normal(keys[14], (D,), jnp.float32), 0.1, 1.9)
    ffn_shift = gaussian(keys[15], (D,), 0.3, 1.5, (), jnp.float32)
    ffn_selector = gaussian(keys[16], (D, EXPERTS), (4 * D) ** -0.5, 0.09375)
    up_weight = gaussian(keys[17], (E_PAD, D, H), D ** -0.5, 0.1875, ((0, 8),))
    down_weight = gaussian(keys[18], (E_PAD, H, D), H ** -0.5, 0.5, ((0, 8),))
    return dict(layer_input=layer_input, cotangent=cotangent, lengths=lengths, value_routes=value_routes, output_routes=output_routes, ffn_routes=ffn_routes, att_gain=att_gain, att_shift=att_shift, query_weight=query_weight, key_weight=key_weight, value_weight=value_weight, output_weight=output_weight, value_selector=value_selector, output_selector=output_selector, ffn_gain=ffn_gain, ffn_shift=ffn_shift, ffn_selector=ffn_selector, up_weight=up_weight, down_weight=down_weight)


EPSILON = 1e-05
NEGATIVE = -1e+30
HIGHEST = lax.Precision.HIGHEST

@jax.custom_vjp
def low(v):
    return lax.optimization_barrier(v.astype(jnp.bfloat16)).astype(jnp.float32)

@jax.custom_vjp
def low_back(v):
    return v

def low_keep(v):
    return (low(v), None)

def low_pass(kept, grad):
    return (grad,)

def back_keep(v):
    return (v, None)

def back_low(kept, grad):
    return (low(grad),)
low.defvjp(low_keep, low_pass)
low_back.defvjp(back_keep, back_low)

def both_ways(values):
    return low(low_back(values))

def layer_norm(values, scaling, offset):
    centred = values - lax.optimization_barrier(jnp.mean(values, axis=-1, keepdims=True))
    inverse = lax.rsqrt(lax.optimization_barrier(jnp.mean(centred * centred, axis=-1, keepdims=True)) + EPSILON)
    return centred * inverse * scaling + offset

def gate_table(logits, routes, choices_count):
    chosen = jnp.any(routes[..., None] == jnp.arange(choices_count), axis=-2)
    return jnp.where(chosen, jax.nn.sigmoid(logits), 0.0)

def destinations(routes, is_valid):
    entries = routes.reshape(-1)
    live_entry = jnp.broadcast_to(is_valid[:, None], routes.shape).reshape(-1)
    onehot_table = ((entries[:, None] == jnp.arange(EXPERTS)[None, :]) & live_entry[:, None]).astype(jnp.int32)
    before = jnp.cumsum(onehot_table, axis=0) - onehot_table
    slot_rank = lax.optimization_barrier(jnp.sum(before * onehot_table, axis=1))
    return jnp.where(live_entry, entries * MOST + slot_rank, EXPERTS * MOST).astype(jnp.int32)

def block(weights, tokens, length, value_routes, output_routes, ffn_routes):
    att_gain, att_shift, query_weight, key_weight, value_weight, output_weight, value_selector, output_selector, ffn_gain, ffn_shift, ffn_selector, up_weight, down_weight = weights
    positions = jnp.arange(TOK_DEV)
    is_valid = positions < length
    validity = is_valid.astype(tokens.dtype)
    act_att = low(layer_norm(tokens, att_gain, att_shift))
    queries = both_ways(jnp.dot(act_att, query_weight, precision=HIGHEST)).reshape(TOK_DEV, HEADS, DH)
    key_rows = both_ways(jnp.dot(act_att, key_weight, precision=HIGHEST)).reshape(TOK_DEV, HEADS, DH)
    projected = low_back(jnp.dot(tokens, value_weight, precision=HIGHEST)).reshape(TOK_DEV, HEADS, EA, DH)
    value_logits = low_back(jnp.dot(act_att, value_selector, precision=HIGHEST)).reshape(TOK_DEV, HEADS, EA)
    output_logits = low_back(jnp.dot(act_att, output_selector, precision=HIGHEST)).reshape(TOK_DEV, HEADS, EA)
    value_gates = gate_table(value_logits, value_routes, EA)
    output_gates = gate_table(output_logits, output_routes, EA)
    values = both_ways(lax.optimization_barrier(jnp.sum(value_gates[..., None] * projected, axis=2)))
    causal = (positions[None, :] <= positions[:, None]) & is_valid[None, :]
    scaling = 1.0 / math.sqrt(DH)
    raw_scores = jnp.einsum('qhd,khd->hqk', queries, key_rows, precision=HIGHEST) * scaling
    scores = low_back(jnp.where(causal[None], raw_scores, NEGATIVE))
    row_peak = lax.optimization_barrier(jnp.max(scores, axis=-1, keepdims=True))
    exponent = jnp.exp(scores - row_peak)
    weights_p = exponent / lax.optimization_barrier(jnp.sum(exponent, axis=-1, keepdims=True))
    attended = low_back(jnp.einsum('hqk,khd->qhd', low(weights_p), values, precision=HIGHEST))
    mixed_rows = low(output_gates[..., None] * attended[:, :, None, :]).reshape(TOK_DEV, HEADS * EA * DH)
    residual = tokens + low_back(jnp.dot(mixed_rows, output_weight, precision=HIGHEST))
    act_ffn = low(layer_norm(residual, ffn_gain, ffn_shift))
    ffn_logits = low_back(jnp.dot(act_ffn, ffn_selector, precision=HIGHEST))
    ffn_gates = jax.nn.sigmoid(jnp.take_along_axis(ffn_logits, ffn_routes, axis=1)) * validity[:, None]
    target = destinations(ffn_routes, is_valid)
    copies = jnp.broadcast_to(low(residual)[:, None, :], (TOK_DEV, TOP_F, D)).reshape(TOK_DEV * TOP_F, D)
    buffer = jnp.zeros((EXPERTS * MOST, D), tokens.dtype).at[target].set(copies, mode='drop')
    buffer = low_back(buffer).reshape(EXPERTS, MOST, D)
    hidden_pre = low_back(jnp.einsum('emd,edh->emh', buffer, up_weight[:EXPERTS], precision=HIGHEST))
    hidden = low(jax.nn.gelu(hidden_pre))
    produced = both_ways(jnp.einsum('emh,ehd->emd', hidden, down_weight[:EXPERTS], precision=HIGHEST))
    produced = produced.reshape(EXPERTS * MOST, D)
    picked = produced[jnp.minimum(target, EXPERTS * MOST - 1)].reshape(TOK_DEV, TOP_F, D)
    return residual + lax.optimization_barrier(jnp.sum(ffn_gates[..., None] * picked, axis=1))

def reference(layer_input, cotangent, lengths, value_routes, output_routes, ffn_routes, att_gain, att_shift, query_weight, key_weight, value_weight, output_weight, value_selector, output_selector, ffn_gain, ffn_shift, ffn_selector, up_weight, down_weight):
    weights = tuple((item.astype(jnp.float32) for item in (att_gain, att_shift, query_weight, key_weight, value_weight, output_weight, value_selector, output_selector, ffn_gain, ffn_shift, ffn_selector, up_weight, down_weight)))
    group = math.gcd(SEQS, max(1, 2048 // TOK_DEV))
    steps_count = SEQS // group

    def forward(tokens_all, weight_set):

        def step(carry, pieces):
            return (carry, jax.vmap(partial(block, weight_set))(*pieces))
        pieces = (tokens_all.reshape(steps_count, group, TOK_DEV, D), lengths.reshape(steps_count, group), value_routes.reshape(steps_count, group, TOK_DEV, HEADS, TOP_A), output_routes.reshape(steps_count, group, TOK_DEV, HEADS, TOP_A), ffn_routes.reshape(steps_count, group, TOK_DEV, TOP_F))
        carry, result = lax.scan(jax.checkpoint(step), jnp.zeros((), jnp.float32), pieces)
        return result.reshape(TOKENS, D)
    final, backward = jax.vjp(forward, layer_input.astype(jnp.float32), weights)
    grad_input, weight_grads = backward(cotangent.astype(jnp.float32))
    live_all = (jnp.arange(TOK_DEV)[None, :] < lengths[:, None]).reshape(TOKENS)
    live_rows = jnp.broadcast_to(live_all[:, None], ffn_routes.shape).reshape(-1).astype(jnp.float32)
    expert_counts = jnp.zeros((EXPERTS,), jnp.float32).at[ffn_routes.reshape(-1)].add(live_rows)
    return (final.astype(jnp.bfloat16), grad_input, weight_grads[0], weight_grads[1], weight_grads[2], weight_grads[3], weight_grads[4], weight_grads[5], weight_grads[6], weight_grads[7], weight_grads[8], weight_grads[9], weight_grads[10], weight_grads[11], weight_grads[12], expert_counts)
```

```python
import math
from functools import partial

import jax
import jax.numpy as jnp
from jax import lax
from jax.experimental import pallas as pl
from jax.experimental.pallas import tpu as pltpu
from jax.sharding import PartitionSpec as P

EXPERTS = 387
MOST = 8
EPSILON = 1e-05
NEGATIVE = -1e30
f32 = jnp.float32
bf16 = jnp.bfloat16
VMEM_LIMIT = 56 * 1024 * 1024
GELU_A = math.sqrt(2.0 / math.pi)
GELU_B = 0.044715


def layer_norm(values, scaling, offset):
    centred = values - jnp.mean(values, axis=-1, keepdims=True)
    inverse = lax.rsqrt(jnp.mean(centred * centred, axis=-1, keepdims=True) + EPSILON)
    normed = centred * inverse
    return (normed * scaling + offset, normed, inverse)


def norm_backward(upstream, normed, inverse, scaling):
    scaled = upstream * scaling
    centre_term = jnp.mean(scaled, axis=-1, keepdims=True)
    slope_term = jnp.mean(scaled * normed, axis=-1, keepdims=True)
    return inverse * (scaled - centre_term - normed * slope_term)


def gate_table(logits, routes, choices_count):
    chosen = jnp.any(routes[..., None] == jnp.arange(choices_count), axis=-2)
    sigmas = jax.nn.sigmoid(logits)
    return (chosen, sigmas, jnp.where(chosen, sigmas, 0.0))


def general_path(
    layer_input,
    cotangent,
    lengths,
    value_routes,
    output_routes,
    ffn_routes,
    att_gain,
    att_shift,
    query_weight,
    key_weight,
    value_weight,
    output_weight,
    value_selector,
    output_selector,
    ffn_gain,
    ffn_shift,
    ffn_selector,
    up_weight,
    down_weight,
):
    f32 = jnp.float32
    bf16 = jnp.bfloat16
    seq_len, width = layer_input.shape
    heads = value_routes.shape[1]
    head_dim = query_weight.shape[1] // heads
    att_experts = value_selector.shape[1] // heads
    top_ffn = ffn_routes.shape[1]
    exp_local = up_weight.shape[0]
    owners = lax.axis_size("expert")
    padded_experts = exp_local * owners
    capacity = MOST
    scaling = 1.0 / math.sqrt(head_dim)
    positions = jnp.arange(seq_len)
    is_valid = positions < lengths[0]
    validity = is_valid.astype(f32)
    input_float = layer_input.astype(f32)
    norm_att, hat_att, inv_att = layer_norm(input_float, att_gain, att_shift)
    act_att = norm_att.astype(bf16)
    queries = (
        jnp.dot(act_att, query_weight, preferred_element_type=f32)
        .astype(bf16)
        .reshape(seq_len, heads, head_dim)
    )
    key_rows = (
        jnp.dot(act_att, key_weight, preferred_element_type=f32)
        .astype(bf16)
        .reshape(seq_len, heads, head_dim)
    )
    projected = jnp.dot(layer_input, value_weight, preferred_element_type=f32).reshape(
        seq_len, heads, att_experts, head_dim
    )
    value_logits = jnp.dot(act_att, value_selector, preferred_element_type=f32).reshape(
        seq_len, heads, att_experts
    )
    output_logits = jnp.dot(act_att, output_selector, preferred_element_type=f32).reshape(
        seq_len, heads, att_experts
    )
    value_pick, value_sig, value_gates = gate_table(value_logits, value_routes, att_experts)
    out_pick, out_sig, out_gates = gate_table(output_logits, output_routes, att_experts)
    values_low = jnp.sum(value_gates[..., None] * projected, axis=2).astype(bf16)
    causal = (positions[None, :] <= positions[:, None]) & is_valid[None, :]
    raw_scores = jnp.einsum("qhd,khd->hqk", queries, key_rows, preferred_element_type=f32) * scaling
    scores = jnp.where(causal[None], raw_scores, NEGATIVE)
    row_peak = jnp.max(scores, axis=-1, keepdims=True)
    log_total = row_peak + jnp.log(jnp.sum(jnp.exp(scores - row_peak), axis=-1, keepdims=True))
    weights_p = jnp.exp(scores - log_total)
    weights_low = weights_p.astype(bf16)
    attended = jnp.einsum("hqk,khd->qhd", weights_low, values_low, preferred_element_type=f32)
    mixed_rows = (out_gates[..., None] * attended[:, :, None, :]).reshape(seq_len, -1).astype(bf16)
    residual = input_float + jnp.dot(mixed_rows, output_weight, preferred_element_type=f32)
    norm_ffn, hat_ffn, inv_ffn = layer_norm(residual, ffn_gain, ffn_shift)
    act_ffn = norm_ffn.astype(bf16)
    ffn_logits = jnp.dot(act_ffn, ffn_selector, preferred_element_type=f32)
    ffn_sig = jax.nn.sigmoid(jnp.take_along_axis(ffn_logits, ffn_routes, axis=1))
    gate_weights = ffn_sig * validity[:, None]
    entries = ffn_routes.reshape(-1)
    live_entry = jnp.broadcast_to(is_valid[:, None], ffn_routes.shape).reshape(-1)
    onehot_table = (
        (entries[:, None] == jnp.arange(padded_experts)[None, :]) & live_entry[:, None]
    ).astype(jnp.int32)
    before = jnp.cumsum(onehot_table, axis=0) - onehot_table
    slot_rank = jnp.sum(before * onehot_table, axis=1)
    counts_local = jnp.sum(onehot_table, axis=0).astype(f32)
    target = jnp.where(live_entry, entries * capacity + slot_rank, padded_experts * capacity)
    fetch = jnp.minimum(target, padded_experts * capacity - 1)
    total_slots = padded_experts * capacity
    residual_low = residual.astype(bf16)
    copies = jnp.broadcast_to(residual_low[:, None, :], (seq_len, top_ffn, width)).reshape(
        -1, width
    )
    send_rows = jnp.zeros((total_slots, width), bf16).at[target].set(copies, mode="drop")
    received = lax.all_to_all(
        send_rows.reshape(owners, exp_local * capacity, width),
        "expert",
        split_axis=0,
        concat_axis=0,
        tiled=True,
    )
    received = received.reshape(owners, exp_local, capacity, width)
    hidden_pre = jnp.einsum("semd,edh->semh", received, up_weight, preferred_element_type=f32)
    hidden_act = jax.nn.gelu(hidden_pre).astype(bf16)
    expert_out = jnp.einsum(
        "semh,ehd->semd", hidden_act, down_weight, preferred_element_type=f32
    ).astype(bf16)
    returned = lax.all_to_all(
        expert_out.reshape(owners, exp_local * capacity, width),
        "expert",
        split_axis=0,
        concat_axis=0,
        tiled=True,
    )
    gathered = (
        returned.reshape(total_slots, width)[fetch].reshape(seq_len, top_ffn, width).astype(f32)
    )
    final = residual + jnp.einsum("tk,tkd->td", gate_weights, gathered)
    output = final.astype(bf16)
    counts_all = lax.psum(counts_local, ("dp", "expert"))
    grad_final = cotangent.astype(f32)
    grad_rows = (gate_weights[:, :, None] * grad_final[:, None, :]).astype(bf16).reshape(-1, width)
    grad_gate = validity[:, None] * jnp.einsum("tkd,td->tk", gathered, grad_final)
    send_grad = jnp.zeros((total_slots, width), bf16).at[target].set(grad_rows, mode="drop")
    grad_recv = lax.all_to_all(
        send_grad.reshape(owners, exp_local * capacity, width),
        "expert",
        split_axis=0,
        concat_axis=0,
        tiled=True,
    )
    grad_recv = grad_recv.reshape(owners, exp_local, capacity, width)
    down_local = jnp.einsum("semh,semd->ehd", hidden_act, grad_recv, preferred_element_type=f32)
    grad_act = jnp.einsum("semd,ehd->semh", grad_recv, down_weight, preferred_element_type=f32)
    gelu_value, gelu_back = jax.vjp(jax.nn.gelu, hidden_pre)
    grad_pre = gelu_back(grad_act)[0].astype(bf16)
    up_local = jnp.einsum("semd,semh->edh", received, grad_pre, preferred_element_type=f32)
    grad_in = jnp.einsum("semh,edh->semd", grad_pre, up_weight, preferred_element_type=f32).astype(
        bf16
    )
    grad_back = lax.all_to_all(
        grad_in.reshape(owners, exp_local * capacity, width),
        "expert",
        split_axis=0,
        concat_axis=0,
        tiled=True,
    )
    grad_copies = (
        grad_back.reshape(total_slots, width)[fetch].reshape(seq_len, top_ffn, width).astype(f32)
    )
    grad_residual = grad_final + jnp.einsum("t,tkd->td", validity, grad_copies)
    sig_grad = grad_gate * ffn_sig * (1.0 - ffn_sig)
    dense_select = jnp.sum(
        jnp.where(ffn_routes[:, :, None] == jnp.arange(EXPERTS), sig_grad[:, :, None], 0.0), axis=1
    ).astype(bf16)
    ffn_selector_local = jnp.einsum("td,te->de", act_ffn, dense_select, preferred_element_type=f32)
    grad_norm_ffn = jnp.einsum("te,de->td", dense_select, ffn_selector, preferred_element_type=f32)
    ffn_gain_local = jnp.sum(grad_norm_ffn * hat_ffn, axis=0)
    ffn_shift_local = jnp.sum(grad_norm_ffn, axis=0)
    grad_residual = grad_residual + norm_backward(grad_norm_ffn, hat_ffn, inv_ffn, ffn_gain)
    grad_att_low = grad_residual.astype(bf16)
    output_local = jnp.einsum("tc,td->cd", mixed_rows, grad_att_low, preferred_element_type=f32)
    grad_mixed = jnp.einsum("td,cd->tc", grad_att_low, output_weight, preferred_element_type=f32)
    grad_mixed = grad_mixed.reshape(seq_len, heads, att_experts, head_dim)
    grad_attended = jnp.sum(out_gates[..., None] * grad_mixed, axis=2).astype(bf16)
    grad_out_gates = jnp.sum(grad_mixed * attended[:, :, None, :], axis=-1)
    out_select = (
        jnp.where(out_pick, grad_out_gates * out_sig * (1.0 - out_sig), 0.0)
        .reshape(seq_len, -1)
        .astype(bf16)
    )
    grad_weights = jnp.einsum("qhd,khd->hqk", grad_attended, values_low, preferred_element_type=f32)
    row_delta = jnp.sum(weights_p * grad_weights, axis=-1, keepdims=True)
    grad_scores = (weights_p * (grad_weights - row_delta)).astype(bf16)
    grad_queries = (
        (jnp.einsum("hqk,khd->qhd", grad_scores, key_rows, preferred_element_type=f32) * scaling)
        .reshape(seq_len, -1)
        .astype(bf16)
    )
    grad_keys = (
        (jnp.einsum("hqk,qhd->khd", grad_scores, queries, preferred_element_type=f32) * scaling)
        .reshape(seq_len, -1)
        .astype(bf16)
    )
    grad_values = jnp.einsum(
        "hqk,qhd->khd", weights_low, grad_attended, preferred_element_type=f32
    ).astype(bf16)
    grad_values_float = grad_values.astype(f32)
    grad_projected = (
        (value_gates[..., None] * grad_values_float[:, :, None, :])
        .reshape(seq_len, -1)
        .astype(bf16)
    )
    grad_value_gates = jnp.sum(grad_values_float[:, :, None, :] * projected, axis=-1)
    value_select = (
        jnp.where(value_pick, grad_value_gates * value_sig * (1.0 - value_sig), 0.0)
        .reshape(seq_len, -1)
        .astype(bf16)
    )
    value_local = jnp.einsum("td,tc->dc", layer_input, grad_projected, preferred_element_type=f32)
    query_local = jnp.einsum("td,tc->dc", act_att, grad_queries, preferred_element_type=f32)
    key_local = jnp.einsum("td,tc->dc", act_att, grad_keys, preferred_element_type=f32)
    value_selector_local = jnp.einsum(
        "td,tc->dc", act_att, value_select, preferred_element_type=f32
    )
    output_selector_local = jnp.einsum("td,tc->dc", act_att, out_select, preferred_element_type=f32)
    grad_norm_att = jnp.einsum("tc,dc->td", grad_queries, query_weight, preferred_element_type=f32)
    grad_norm_att = grad_norm_att + jnp.einsum(
        "tc,dc->td", grad_keys, key_weight, preferred_element_type=f32
    )
    grad_norm_att = grad_norm_att + jnp.einsum(
        "tc,dc->td", value_select, value_selector, preferred_element_type=f32
    )
    grad_norm_att = grad_norm_att + jnp.einsum(
        "tc,dc->td", out_select, output_selector, preferred_element_type=f32
    )
    att_gain_local = jnp.sum(grad_norm_att * hat_att, axis=0)
    att_shift_local = jnp.sum(grad_norm_att, axis=0)
    input_grad = grad_residual + jnp.einsum(
        "tc,dc->td", grad_projected, value_weight, preferred_element_type=f32
    )
    input_grad = input_grad + norm_backward(grad_norm_att, hat_att, inv_att, att_gain)
    reduced = (
        lax.psum_scatter(att_gain_local, ("dp", "expert"), scatter_dimension=0, tiled=True),
        lax.psum_scatter(att_shift_local, ("dp", "expert"), scatter_dimension=0, tiled=True),
        lax.psum_scatter(query_local, ("dp", "expert"), scatter_dimension=0, tiled=True),
        lax.psum_scatter(key_local, ("dp", "expert"), scatter_dimension=0, tiled=True),
        lax.psum_scatter(value_local, ("dp", "expert"), scatter_dimension=0, tiled=True),
        lax.psum_scatter(output_local, ("dp", "expert"), scatter_dimension=1, tiled=True),
        lax.psum_scatter(value_selector_local, ("dp", "expert"), scatter_dimension=0, tiled=True),
        lax.psum_scatter(output_selector_local, ("dp", "expert"), scatter_dimension=0, tiled=True),
        lax.psum_scatter(ffn_gain_local, ("dp", "expert"), scatter_dimension=0, tiled=True),
        lax.psum_scatter(ffn_shift_local, ("dp", "expert"), scatter_dimension=0, tiled=True),
        lax.psum_scatter(ffn_selector_local, ("dp", "expert"), scatter_dimension=0, tiled=True),
    )
    up_grad, down_grad = (
        lax.psum_scatter(
            up_local.astype(jnp.bfloat16), "dp", scatter_dimension=1, tiled=True
        ).astype(jnp.float32),
        lax.psum_scatter(
            down_local.astype(jnp.bfloat16), "dp", scatter_dimension=2, tiled=True
        ).astype(jnp.float32),
    )
    return (
        output,
        input_grad,
        reduced[0],
        reduced[1],
        reduced[2],
        reduced[3],
        reduced[4],
        reduced[5],
        reduced[6],
        reduced[7],
        reduced[8],
        reduced[9],
        reduced[10],
        up_grad,
        down_grad,
        counts_all[:EXPERTS],
    )


def mm(a, b, ca, cb):
    return lax.dot_general(a, b, (((ca,), (cb,)), ((), ())), preferred_element_type=f32)


def iota(shape, dim):
    return lax.broadcasted_iota(jnp.int32, shape, dim)


def centre(values):
    centred = values - jnp.mean(values, axis=-1, keepdims=True)
    inverse = lax.rsqrt(jnp.mean(centred * centred, axis=-1, keepdims=True) + EPSILON)
    return centred * inverse, inverse


def centre_back(upstream, normed, inverse, gain):
    scaled = upstream * gain
    mean = jnp.mean(scaled, axis=-1, keepdims=True)
    slope = jnp.mean(scaled * normed, axis=-1, keepdims=True)
    return inverse * (scaled - mean - normed * slope)


def dest_of(ids, nz, s, x):
    return lax.rem(ids[0] + s, nz) * 2 + (ids[1] + x - 2 * ids[1] * x)


def call(body, outs, args, flops=0, scratch=(), smem=(), name=None):
    nbytes = sum(a.size * a.dtype.itemsize for a in args) + sum(
        math.prod(s) * jnp.dtype(d).itemsize for s, d in outs
    )
    return pl.pallas_call(
        body,
        out_shape=[jax.ShapeDtypeStruct(s, d) for s, d in outs],
        in_specs=[pl.BlockSpec(memory_space=pltpu.SMEM)] * len(smem)
        + [pl.BlockSpec(memory_space=pltpu.VMEM)] * len(args),
        out_specs=[pl.BlockSpec(memory_space=pltpu.VMEM)] * len(outs),
        scratch_shapes=list(scratch),
        compiler_params=pltpu.CompilerParams(vmem_limit_bytes=VMEM_LIMIT),
        cost_estimate=pl.CostEstimate(flops=flops, bytes_accessed=nbytes, transcendentals=0),
        name=name,
    )(*smem, *args)


def forward_body(
    length, li, vroutes, oroutes, froutes, att_gain, att_shift, wq, wk, wv, wo, selw,
    ffn_gain, ffn_shift, fsel,
    h1_o, xpack_o, q_o, k_o, v_o, p_o, a_o, o_o, gt_o, a1_o, a2_o, mixed,
):
    T, D = li.shape
    heads = vroutes.shape[1] // 2
    dh = wq.shape[1] // heads
    ea = wv.shape[1] // (heads * dh)
    he = heads * ea
    scaling = 1.0 / math.sqrt(dh)
    x = li[...].astype(f32)
    hat, _ = centre(x)
    a1 = (hat * att_gain[...] + att_shift[...]).astype(bf16)
    a1_o[...] = a1
    logits = mm(a1, selw[...], 1, 0)
    lane = iota((T, 128), 1)
    chosen = jnp.zeros((T, 128), jnp.bool_)
    for j in range(2 * heads):
        h = j // 2
        chosen |= lane == vroutes[:, j : j + 1] + h * ea
        chosen |= lane == oroutes[:, j : j + 1] + (he + h * ea)
    gt = jnp.where(chosen, jax.nn.sigmoid(logits), 0.0)
    gt_o[...] = gt
    q = mm(a1, wq[...], 1, 0).astype(bf16)
    k = mm(a1, wk[...], 1, 0).astype(bf16)
    q_o[...] = q
    k_o[...] = k
    n_live = length[0]
    row, col = iota((T, T), 0), iota((T, T), 1)
    causal = (col <= row) & (col < n_live)
    width = ea * dh
    for h in range(heads):
        proj = mm(li[...], wv[:, h * width : (h + 1) * width], 1, 0)
        p_o[:, h * width : (h + 1) * width] = proj
        v = jnp.zeros((T, dh), f32)
        for e in range(ea):
            v += gt[:, h * ea + e : h * ea + e + 1] * proj[:, e * dh : (e + 1) * dh]
        v = v.astype(bf16)
        v_o[:, h * dh : (h + 1) * dh] = v
        s = mm(q[:, h * dh : (h + 1) * dh], k[:, h * dh : (h + 1) * dh], 1, 1) * scaling
        s = jnp.where(causal, s, NEGATIVE)
        ex = jnp.exp(s - jnp.max(s, axis=-1, keepdims=True))
        a = ex / jnp.sum(ex, axis=-1, keepdims=True)
        a_o[h] = a
        o = mm(a.astype(bf16), v, 1, 0)
        o_o[:, h * dh : (h + 1) * dh] = o
        for e in range(ea):
            c = he + h * ea + e
            mixed[:, (h * ea + e) * dh : (h * ea + e + 1) * dh] = (gt[:, c : c + 1] * o).astype(bf16)
    h1 = x + mm(mixed[...], wo[...], 1, 0)
    h1_o[...] = h1
    hat2, _ = centre(h1)
    a2 = (hat2 * ffn_gain[...] + ffn_shift[...]).astype(bf16)
    a2_o[...] = a2
    sig = jax.nn.sigmoid(mm(a2, fsel[...], 1, 0))
    wide = iota(sig.shape, 1)
    g = jnp.zeros((T, 128), f32)
    for i in range(froutes.shape[1]):
        one = jnp.sum(jnp.where(wide == froutes[:, i : i + 1], sig, 0.0), axis=-1, keepdims=True)
        g = jnp.where(lane == i, one, g)
    g = g.T[:16]
    hi = g.astype(bf16)
    xpack_o[:T] = h1.astype(bf16)
    xpack_o[T:] = jnp.zeros((16, D), bf16)
    xpack_o[T:, :128] = hi
    xpack_o[T:, 128:256] = (g - hi.astype(f32)).astype(bf16)


def take_slices(v, n_p, S, e):
    D = v.shape[1]
    w = D // (n_p * S)
    return jnp.concatenate(
        [v[:, (b * S + e) * w : (b * S + e + 1) * w] for b in range(n_p)], axis=1
    )


def early_body(n_p, S, ids, li, a1, a2, o, gt, *rest):
    msgs, scratch = rest[:-1], rest[-1]
    hd = o.shape[1]
    for e in range(S):
        for i, v in enumerate((li, a1, a2)):
            scratch[e, :, i * 128 : (i + 1) * 128] = take_slices(v[...].astype(f32), n_p, S, e).astype(bf16)
    hi = gt[...].astype(bf16).astype(f32)
    both = (hi + pltpu.roll(gt[...] - hi, 64, 1)).astype(bf16)
    for s, m in enumerate(msgs):
        m[:, :hd] = o[...].astype(bf16)
        m[:, hd : hd + 128] = both
        m[:, hd + 128 : hd + 512] = scratch[dest_of(ids, S // 2, s, 1)]
        m[:, hd + 512 : hd + 896] = scratch[dest_of(ids, S // 2, s, 0)]


def gates_of(m, hd):
    both = m[:, hd : hd + 128].astype(f32)
    return both + pltpu.roll(both, 64, 1)


def codes_body(S, ids, *refs):
    c, (code_o, cnt_o) = refs[:S], refs[S:]
    ep = cnt_o.shape[1]
    T = c[0].shape[0] - 16
    strict = (iota((T, T), 0) < iota((T, T), 1)).astype(f32).astype(bf16)
    e_id = iota((ep, T), 0).astype(f32)
    cnt = jnp.zeros((8, ep), f32)
    start = ids[3].astype(f32)
    for k in range(S):
        r = c[k][T:, :T].astype(f32) * 32.0 + c[k][T:, T : 2 * T].astype(f32) - start
        mask = jnp.zeros((ep, T), f32)
        for i in range(r.shape[0]):
            mask += jnp.where(r[i : i + 1] == e_id, 1.0, 0.0)
        low = mask.astype(bf16)
        rank = mm(low, strict, 1, 0) + (MOST * (k % 2))
        cnt += mm(jnp.ones((8, T), bf16), low, 1, 1)
        code_o[k // 2, :, (k % 2) * T : (k % 2 + 1) * T] = jnp.where(mask > 0.5, rank, -1.0).astype(bf16)
    cnt_o[...] = cnt


def columns_body(S, n_p, *refs):
    x, out = refs[:S], refs[-1]
    T = x[0].shape[0] - 16
    wide = out.shape[3]
    for k in range(S):
        for s in range(n_p):
            out[s, k // 2, (k % 2) * T : (k % 2 + 1) * T, :] = x[k][:T, s * wide : (s + 1) * wide]
    if len(refs) > S + 1:
        for s in range(n_p):
            out[s, :, 2 * T :, :] = refs[S][...]


def gelu_both(u):
    t = jnp.tanh(GELU_A * (u + GELU_B * u * u * u))
    value = 0.5 * u * (1.0 + t)
    slope = 0.5 * (1.0 + t) + 0.5 * u * (1.0 - t * t) * (GELU_A * (1.0 + 3.0 * GELU_B * u * u))
    return value, slope


def experts_body(S, eb, ids, *refs):
    x, c = refs[:S], refs[S : 2 * S]
    code, up, down = refs[2 * S : 2 * S + 3]
    dx0, dx1, gy0, gy1, rdu = refs[2 * S + 3 : 2 * S + 8]
    ct, gts, dl, ps, xs, cs, gys, dxs = refs[2 * S + 8 :]
    step = pl.program_id(0)
    pairs = S // 2
    R = 2 * MOST
    T = x[0].shape[0] - 16
    D = x[0].shape[1]
    ep = ct.shape[1]
    rows = pairs * R

    @pl.when(step == 0)
    def _():
        e_id = iota((ep, T), 0).astype(f32)
        start = ids[3].astype(f32)
        dl[...] = jnp.zeros_like(dl)
        for pr in range(pairs):
            ct[pr] = code[pr].astype(f32)
        for k in range(S):
            r = c[k][T:, :T].astype(f32) * 32.0 + c[k][T:, T : 2 * T].astype(f32) - start
            g = x[k][T:, :T].astype(f32) + x[k][T:, T : 2 * T].astype(f32)
            dense = jnp.zeros((ep, T), f32)
            for i in range(r.shape[0]):
                dense += jnp.where(r[i : i + 1] == e_id, g[i : i + 1], 0.0)
            gts[:, k * T : (k + 1) * T] = dense

    slot = iota((R, 2 * T), 0).astype(f32)
    g_slot = [[None] * pairs for _ in range(eb)]
    onehot = [[None] * pairs for _ in range(eb)]
    for pr in range(pairs):
        blocks = []
        for j in range(eb):
            e = step * eb + j
            hot = jnp.where(ct[pr, pl.ds(e, 1), :] == slot, 1.0, 0.0)
            onehot[j][pr] = hot
            g_slot[j][pr] = jnp.sum(
                hot * gts[pl.ds(e, 1), pr * 2 * T : (pr + 1) * 2 * T], axis=-1, keepdims=True
            )
            blocks.append(hot.astype(bf16))
        block = jnp.concatenate(blocks, axis=0)
        ps[pr, pl.ds(pl.multiple_of(step * (eb * R), R), eb * R), :] = block
        for src, dst in ((x, xs), (c, cs)):
            both = jnp.concatenate([src[2 * pr][:T], src[2 * pr + 1][:T]], axis=0)
            got = mm(block, both, 1, 0).astype(bf16)
            for j in range(eb):
                dst[j * rows + pr * R : j * rows + (pr + 1) * R, :] = got[j * R : (j + 1) * R]
    for j in range(eb):
        e = step * eb + j
        g = jnp.concatenate(g_slot[j], axis=0)
        xj = xs[j * rows : (j + 1) * rows, :]
        cj = cs[j * rows : (j + 1) * rows, :].astype(f32)
        u = mm(xj, up[j], 1, 0)
        value, slope = gelu_both(u)
        r = value.astype(bf16)
        y = mm(r, down[j], 1, 0).astype(bf16).astype(f32)
        dgate = jnp.sum(cj * y, axis=-1, keepdims=True)
        gy = (g * y).astype(bf16)
        dr = mm((g * cj).astype(bf16), down[j], 1, 1)
        du = (dr * slope).astype(bf16)
        dx = mm(du, up[j], 1, 1).astype(bf16)
        gr = (g * r.astype(f32)).astype(bf16)
        for plane in range(rdu.shape[0]):
            rdu[plane, 0, j] = gr
            rdu[plane, 1, j] = du
        dlog = dgate * g * (1.0 - g)
        for pr in range(pairs):
            at = pl.ds(pl.multiple_of(step * (eb * R) + j * R, R), R)
            gys[pr, at, :] = gy[pr * R : (pr + 1) * R]
            dxs[pr, at, :] = dx[pr * R : (pr + 1) * R]
            dl[pl.ds(e, 1), pr * 2 * T : (pr + 1) * 2 * T] = jnp.sum(
                onehot[j][pr] * dlog[pr * R : (pr + 1) * R], axis=0, keepdims=True
            )

    @pl.when(step == pl.num_programs(0) - 1)
    def _():
        for pr in range(pairs):
            for src, d0, d1 in ((dxs, dx0, dx1), (gys, gy0, gy1)):
                got = mm(ps[pr], src[pr], 0, 0).astype(bf16)
                d0[pr, :T] = got[:T]
                d1[pr, :T] = got[T:]
            for x_i, d in ((0, dx0), (1, dx1)):
                k = 2 * pr + x_i
                part = dl[:, k * T : (k + 1) * T].astype(bf16)
                d[pr, T:] = jnp.zeros((16, D), bf16)
                for b in range(ep // 16):
                    d[pr, T:, b * T : (b + 1) * T] = part[16 * b : 16 * b + 16]


def join_body(nz, T, mine, recv, *outs):
    half = mine.shape[2] // 2
    for s in range(nz):
        outs[s][:T] = (mine[s, :T].astype(f32) + recv[s, :T].astype(f32)).astype(bf16)
        if outs[s].shape[0] > T:
            outs[s][T:, :half] = mine[s, T:, :half]
            outs[s][T:, half:] = recv[s, T:, :half]


def ffn_back_body(nz, ids, *refs):
    parts = refs[:nz]
    h1, c, fsel, gain, dh1_o, db_o, norms_o, dl_o, dlt = refs[nz:]
    T, D = h1.shape
    ep = dlt.shape[0] // (2 * nz)
    half = D // 2
    dxs = parts[0][:T].astype(f32)
    for m in parts[1:]:
        dxs += m[:T].astype(f32)
    for s in range(nz):
        for x in range(2):
            for b in range(ep // 16):
                at = pl.multiple_of(dest_of(ids, nz, s, x) * ep + 16 * b, 16)
                dlt[pl.ds(at, 16), :] = parts[s][T:, x * half + b * T : x * half + (b + 1) * T].astype(f32)
    dl = dlt[...].T
    dl_o[...] = dl
    da2 = mm(dl.astype(bf16), fsel[...], 1, 1)
    hat, inv = centre(h1[...])
    norms_o[...] = jnp.zeros_like(norms_o)
    norms_o[0:1] = jnp.sum(da2 * hat, axis=0, keepdims=True)
    norms_o[1:2] = jnp.sum(da2, axis=0, keepdims=True)
    dh1 = c[...].astype(f32) + dxs + centre_back(da2, hat, inv, gain[...])
    dh1_o[...] = dh1
    db_o[...] = dh1.astype(bf16)


def mid_body(n_p, S, nz, ids, db, dl, froutes, *refs):
    msgs, sl = refs[:nz], refs[nz]
    T = db.shape[0]
    low = db[...].astype(f32)
    for e in range(S):
        sl[e] = take_slices(low, n_p, S, e).astype(bf16)
    wide, lane = iota(dl.shape, 1), iota((T, 128), 1)
    few = jnp.zeros((T, 128), f32)
    for i in range(froutes.shape[1]):
        one = jnp.sum(jnp.where(wide == froutes[:, i : i + 1], dl[...], 0.0), axis=-1, keepdims=True)
        few = jnp.where(lane == i, one, few)
    few = few.T[:16].astype(bf16)
    for s, m in enumerate(msgs):
        m[:T, :128] = sl[dest_of(ids, nz, s, 1)]
        m[:T, 128:] = sl[dest_of(ids, nz, s, 0)]
        m[T:, :T] = few
        m[T:, T:] = jnp.zeros((16, 256 - T), bf16)


def attention_back_body(db, wo, gt, o, q, k, v, a, p, late_o, dp_o):
    T, D = db.shape
    heads = a.shape[0]
    dh = q.shape[1] // heads
    ea = p.shape[1] // (heads * dh)
    he, hd = heads * ea, heads * dh
    width = ea * dh
    scaling = 1.0 / math.sqrt(dh)
    lane = iota((T, 128), 1)
    dgates = jnp.zeros((T, 128), f32)
    gates = gt[...]
    for h in range(heads):
        hs = slice(h * dh, (h + 1) * dh)
        dz = mm(db[...], wo[h * width : (h + 1) * width, :], 1, 1)
        oh = o[:, hs]
        do = jnp.zeros((T, dh), f32)
        for e in range(ea):
            c = he + h * ea + e
            piece = dz[:, e * dh : (e + 1) * dh]
            do += gates[:, c : c + 1] * piece
            dgates = jnp.where(lane == c, jnp.sum(piece * oh, axis=-1, keepdims=True), dgates)
        do = do.astype(bf16)
        ah = a[h]
        dv = mm(ah.astype(bf16), do, 0, 0).astype(bf16)
        late_o[:, hs] = dv
        dvf = dv.astype(f32)
        for e in range(ea):
            c = h * ea + e
            es = slice(c * dh, (c + 1) * dh)
            dp_o[:, es] = (gates[:, c : c + 1] * dvf).astype(bf16)
            dgates = jnp.where(lane == c, jnp.sum(dvf * p[:, es], axis=-1, keepdims=True), dgates)
        da = mm(do, v[:, hs], 1, 1)
        ds = (ah * (da - jnp.sum(ah * da, axis=-1, keepdims=True))).astype(bf16)
        late_o[:, hd + h * dh : hd + (h + 1) * dh] = (mm(ds, k[:, hs], 1, 0) * scaling).astype(bf16)
        late_o[:, 2 * hd + h * dh : 2 * hd + (h + 1) * dh] = (mm(ds, q[:, hs], 0, 0) * scaling).astype(bf16)
    late_o[:, 3 * hd :] = (dgates * gates * (1.0 - gates)).astype(bf16)


def input_back_body(late, dp, wq, wk, wv, selw, li, gain, dh1, fnorms, ig_o, norms_o):
    hd = wq.shape[1]
    da1 = mm(late[:, hd : 2 * hd], wq[...], 1, 1)
    da1 += mm(late[:, 2 * hd : 3 * hd], wk[...], 1, 1)
    da1 += mm(late[:, 3 * hd :], selw[...], 1, 1)
    hat, inv = centre(li[...].astype(f32))
    norms_o[...] = fnorms[...]
    norms_o[2:3] = jnp.sum(da1 * hat, axis=0, keepdims=True)
    norms_o[3:4] = jnp.sum(da1, axis=0, keepdims=True)
    ig_o[...] = dh1[...] + mm(dp[...], wv[...], 1, 1) + centre_back(da1, hat, inv, gain[...])


def spread(values, gates, lo, heads, ea, dh):
    return jnp.concatenate(
        [
            (gates[:, lo + h * ea + e : lo + h * ea + e + 1] * values[:, h * dh : (h + 1) * dh]).astype(bf16)
            for h in range(heads)
            for e in range(ea)
        ],
        axis=1,
    )


def out_rows(acc, outs, ids, w):
    for s, ref in enumerate(outs):
        plane = ids[2] ^ s
        ref[...] = acc[pl.ds(pl.multiple_of(plane * w, 8), w), :].astype(ref.dtype)


def out_grads_body(S, n_p, heads, ea, w, ids, *refs):
    early, mid, cpack = refs[:S], refs[S : 2 * S], refs[2 * S : 3 * S]
    outs = refs[3 * S : 3 * S + n_p]
    acc, lhs, rhs, dlt = refs[3 * S + n_p :]
    T = early[0].shape[0]
    hd = early[0].shape[1] - 896
    dh = hd // heads
    EP = dlt.shape[0]
    e_id = iota((EP, T), 0).astype(f32)
    for k in range(S):
        x = k % 2
        ts = slice(k * T, (k + 1) * T)
        m = early[k]
        rhs[ts, :] = spread(m[:, :hd].astype(f32), gates_of(m, hd), heads * ea, heads, ea, dh)
        at = hd + 512 if x == 0 else hd + 128
        lhs[ts, 128:] = m[:, at + 256 : at + 384]
        n = mid[k]
        at = 128 if x == 0 else 0
        lhs[ts, :128] = n[:T, at : at + 128]
        route = cpack[k][T:, :T].astype(f32) * 32.0 + cpack[k][T:, T : 2 * T].astype(f32)
        few = n[T:, :T].astype(f32)
        dense = jnp.zeros((EP, T), f32)
        for i in range(16):
            dense += jnp.where(route[i : i + 1] == e_id, few[i : i + 1], 0.0)
        dlt[:, ts] = dense.astype(bf16)
    wide = rhs.shape[1]
    acc[:, :wide] = mm(lhs[:, :128], rhs[...], 0, 0)
    acc[:, wide:] = mm(dlt[...], lhs[:, 128:], 1, 0).T
    out_rows(acc, outs, ids, w)


def in_grads_body(S, n_p, heads, ea, w, ids, *refs):
    early, late = refs[:S], refs[S : 2 * S]
    outs = refs[2 * S : 2 * S + n_p]
    acc, lhs, rhs, qk = refs[2 * S + n_p :]
    T = early[0].shape[0]
    hd = early[0].shape[1] - 896
    dh = hd // heads
    for k in range(S):
        ts = slice(k * T, (k + 1) * T)
        m, n = early[k], late[k]
        rhs[ts, :] = spread(n[:, :hd].astype(f32), gates_of(m, hd), 0, heads, ea, dh)
        at = hd + 512 if k % 2 == 0 else hd + 128
        lhs[ts, :] = m[:, at : at + 256]
        qk[ts, :] = n[:, hd:]
    wide = rhs.shape[1]
    acc[:, :wide] = mm(lhs[:, :128], rhs[...], 0, 0)
    acc[:, wide:] = mm(lhs[:, 128:], qk[...], 0, 0)
    out_rows(acc, outs, ids, w)


def expert_grads_body(n_p, eb, cc, xc, rdu, up_o, down_o, ct, got):
    step = pl.program_id(0)
    _, pairs, T2, wide = cc.shape
    R = 2 * MOST
    rows = pairs * R

    @pl.when(step == 0)
    def _():
        for s in range(n_p):
            for pr in range(pairs):
                ct[s * pairs + pr] = xc[s, pr, T2:, :].astype(f32)

    slot = iota((R, T2), 0).astype(f32)
    for s in range(n_p):
        for pr in range(pairs):
            block = jnp.concatenate(
                [
                    jnp.where(ct[s * pairs + pr, pl.ds(step * eb + j, 1), :] == slot, 1.0, 0.0).astype(bf16)
                    for j in range(eb)
                ],
                axis=0,
            )
            both = jnp.concatenate([xc[s, pr, :T2], cc[s, pr]], axis=1)
            res = mm(block, both, 1, 0).astype(bf16)
            for j in range(eb):
                at = j * n_p * rows + s * rows + pr * R
                got[at : at + R, :] = res[j * R : (j + 1) * R]
    for j in range(eb):
        at = j * n_p * rows
        xj = got[at : at + n_p * rows, :wide]
        cj = got[at : at + n_p * rows, wide:]
        gr = jnp.concatenate([rdu[s, 0, j] for s in range(n_p)], axis=0)
        du = jnp.concatenate([rdu[s, 1, j] for s in range(n_p)], axis=0)
        up_o[j] = mm(xj, du, 0, 0)
        down_o[j] = mm(gr, cj, 0, 0)


def after(values, *deps):
    return lax.optimization_barrier((values, deps))[0]


class Links:
    def __init__(self):
        self.n_e = lax.axis_size("expert")
        self.nz = self.n_e // 2
        self.n_p = lax.axis_size("dp")
        self.me = lax.axis_index("expert")
        self.z, self.c = self.me // 2, self.me % 2
        self.p = lax.axis_index("dp")

    def core(self, v):
        return lax.ppermute(v, "expert", [(e, e ^ 1) for e in range(self.n_e)])

    def chip(self, v, s):
        return lax.ppermute(v, "expert", [(e, (e + 2 * s) % self.n_e) for e in range(self.n_e)])

    def plane(self, v, s):
        return lax.ppermute(v, "dp", [(p, p ^ s) for p in range(self.n_p)])

    def far(self, msgs):
        return [msgs[0]] + [self.chip(msgs[s], s) for s in range(1, self.nz)]

    def relay(self, got):
        return [v for a in got for v in (a, self.core(a))]

    def planes_of(self, msgs):
        return [msgs[0]] + [self.plane(msgs[s], s) for s in range(1, self.n_p)]


def fast_path(
    layer_input, cotangent, lengths, value_routes, output_routes, ffn_routes, att_gain, att_shift,
    query_weight, key_weight, value_weight, output_weight, value_selector, output_selector,
    ffn_gain, ffn_shift, ffn_selector, up_weight, down_weight,
):
    L = Links()
    S, nz, n_p = L.n_e, L.nz, L.n_p
    pairs = S // 2
    T, D = layer_input.shape
    heads = value_routes.shape[1]
    dh = query_weight.shape[1] // heads
    ea = value_selector.shape[1] // heads
    hd, he, wide = heads * dh, heads * ea, heads * ea * dh
    el, _, H = up_weight.shape
    ep = -(-el // 16) * 16
    EP = ep * S
    w = D // (n_p * S)
    Dp = D // n_p
    R = 2 * MOST
    eb = max(d for d in (7, 4, 2, 1) if el % d == 0)

    ids = jnp.stack([L.z, L.c, L.p, L.me * ep]).astype(jnp.int32)
    padded = (ffn_routes // el) * ep + ffn_routes % el
    selw = jnp.pad(jnp.concatenate([value_selector, output_selector], axis=1), ((0, 0), (0, 128 - 2 * he)))
    fsel = jnp.pad(ffn_selector, ((0, 0), (0, S * el - ffn_selector.shape[1])))
    fsel = jnp.pad(fsel.reshape(D, S, el), ((0, 0), (0, 0), (0, ep - el))).reshape(D, EP)
    v_routes, o_routes = value_routes.reshape(T, -1), output_routes.reshape(T, -1)
    padded, selw, fsel, v_routes, o_routes, ids = lax.optimization_barrier(
        (padded, selw, fsel, v_routes, o_routes, ids)
    )

    live = jnp.arange(T)[:, None] < lengths[0]
    rt = jnp.where(live, padded, EP).T
    tail = jnp.concatenate([rt // 32, rt % 32], axis=1).astype(bf16)
    cpack = jnp.concatenate([cotangent, jnp.pad(tail, ((0, 0), (0, D - 2 * T)))], axis=0)
    c_far = L.far([cpack] * nz)

    h1, xpack, q, k, v, proj, a, o, gt, a1, a2 = call(
        forward_body,
        [
            ((T, D), f32), ((T + 16, D), bf16), ((T, hd), bf16), ((T, hd), bf16), ((T, hd), bf16),
            ((T, wide), f32), ((heads, T, T), f32), ((T, hd), f32), ((T, 128), f32),
            ((T, D), bf16), ((T, D), bf16),
        ],
        [
            layer_input, v_routes, o_routes, padded,
            att_gain[None], att_shift[None], query_weight, key_weight, value_weight, output_weight,
            selw, ffn_gain[None], ffn_shift[None], fsel,
        ],
        flops=2 * T * D * (2 * hd + 2 * wide + EP),
        scratch=[pltpu.VMEM((T, wide), bf16)],
        smem=[lengths],
        name="forward",
    )
    x_far = L.far([xpack] * nz)
    x_sib = L.core(xpack)
    early = call(
        partial(early_body, n_p, S),
        [((T, hd + 896), bf16)] * nz,
        [layer_input, a1, a2, o, gt],
        scratch=[pltpu.VMEM((S, T, 384), bf16)],
        smem=[ids],
        name="early_slices",
    )
    c_msgs = L.relay(after(c_far, early))
    (ccols,) = call(
        partial(columns_body, S, n_p), [((n_p, pairs, 2 * T, Dp), bf16)], c_msgs, name="cotangent_columns"
    )
    cc_all = lax.all_to_all(ccols, "dp", 0, 0, tiled=True)
    code, cnt = call(
        partial(codes_body, S), [((pairs, ep, 2 * T), bf16), ((8, ep), f32)], after(c_msgs, ccols), smem=[ids], name="codes",

    )
    x_far = after(x_far, code)
    x_msgs = L.relay(x_far)
    x_msgs[1] = x_sib
    early_far = L.far(after(early, x_far))
    (xcols,) = call(
        partial(columns_body, S, n_p),
        [((n_p, pairs, 2 * T + ep, Dp), bf16)],
        [*after(x_msgs, cc_all), code],
        name="token_columns",
    )
    xc_all = lax.all_to_all(xcols, "dp", 0, 0, tiled=True)

    n_eb = el // eb
    whole = [pl.BlockSpec(memory_space=pltpu.VMEM)]
    dx0, dx1, gy0, gy1, rdu = pl.pallas_call(
        partial(experts_body, S, eb),
        grid=(n_eb,),
        out_shape=[
            jax.ShapeDtypeStruct((pairs, T + 16, D), bf16), jax.ShapeDtypeStruct((pairs, T + 16, D), bf16),
            jax.ShapeDtypeStruct((pairs, T, D), bf16), jax.ShapeDtypeStruct((pairs, T, D), bf16),
            jax.ShapeDtypeStruct((n_p, 2, el, pairs * R, H), bf16),
        ],
        in_specs=[pl.BlockSpec(memory_space=pltpu.SMEM)]
        + whole * (2 * S + 1)
        + [
            pl.BlockSpec((eb, D, H), lambda i: (i, 0, 0)),
            pl.BlockSpec((eb, H, D), lambda i: (i, 0, 0)),
        ],
        out_specs=whole * 4 + [pl.BlockSpec((n_p, 2, eb, pairs * R, H), lambda i: (0, 0, i, 0, 0))],
        scratch_shapes=[
            pltpu.VMEM((pairs, ep, 2 * T), f32), pltpu.VMEM((ep, S * T), f32), pltpu.VMEM((ep, S * T), f32),
            pltpu.VMEM((pairs, el * R, 2 * T), bf16),
            pltpu.VMEM((eb * pairs * R, D), bf16), pltpu.VMEM((eb * pairs * R, D), bf16),
            pltpu.VMEM((pairs, el * R, D), bf16), pltpu.VMEM((pairs, el * R, D), bf16),
        ],
        compiler_params=pltpu.CompilerParams(vmem_limit_bytes=VMEM_LIMIT),
        cost_estimate=pl.CostEstimate(
            flops=12 * el * pairs * R * D * H, bytes_accessed=4 * el * D * H + 14 * S * T * D, transcendentals=0
        ),
        name="experts",
    )(after(ids, xcols), *x_msgs, *c_msgs, code, up_weight, down_weight)

    def home(mine, other, name):
        joined = call(
            partial(join_body, nz, T), [(mine.shape[1:], bf16)] * nz, [mine, L.core(other)], name=name
        )
        return joined

    def go_home(joined):
        return [joined[0]] + [L.chip(joined[s], -s) for s in range(1, nz)]

    dx0, dx1, xc_all, early_far = lax.optimization_barrier((dx0, dx1, xc_all, early_far))
    dx_join = home(dx0, dx1, "join_dx")
    rdu_all = lax.all_to_all(after(rdu, dx_join), "dp", 0, 0, tiled=True)
    dx_parts = go_home(dx_join)
    gy_join = home(*after((gy0, gy1), dx_join), "join_out")
    dx_parts, gy_join = lax.optimization_barrier((dx_parts, gy_join))
    early_msgs = L.relay(after(early_far, dx_parts))

    dh1, db, fnorms, dl = call(
        partial(ffn_back_body, nz),
        [((T, D), f32), ((T, D), bf16), ((8, D), f32), ((T, EP), f32)],
        [*dx_parts, h1, cotangent, fsel, ffn_gain[None]],
        flops=2 * T * D * EP,
        scratch=[pltpu.VMEM((EP, T), f32)],
        smem=[ids],
        name="ffn_back",
    )
    mid = call(
        partial(mid_body, n_p, S, nz),
        [((T + 16, 256), bf16)] * nz,
        [after(db, early_msgs), dl, padded],
        scratch=[pltpu.VMEM((S, T, 128), bf16)],
        smem=[ids],
        name="mid_slices",
    )
    mid_far = L.far(mid)
    late, dp = call(
        attention_back_body,
        [((T, 3 * hd + 128), bf16), ((T, wide), bf16)],
        [after(db, mid), output_weight, gt, o, q, k, v, a, proj],
        flops=2 * T * D * wide,
        name="attention_back",
    )
    late_far = L.far([late] * nz)
    input_grad, norms = call(
        input_back_body,
        [((T, D), f32), ((8, D), f32)],
        [late, dp, query_weight, key_weight, value_weight, selw, layer_input, att_gain[None], dh1, fnorms],
        flops=2 * T * D * (wide + 2 * hd),
        name="input_back",
    )
    n_all = n_p * S
    small = jnp.concatenate(
        [
            norms[:4].reshape(4, n_all, w).transpose(1, 0, 2),
            jnp.broadcast_to(cnt[:1, : 2 * w].reshape(1, 2, w), (n_all, 2, w)),
        ],
        axis=1,
    )
    small = lax.all_to_all(after(small, rdu_all), ("dp", "expert"), 0, 0, tiled=True)
    mid_msgs = L.relay(after(mid_far, late))
    grads_a = call(
        partial(out_grads_body, S, n_p, heads, ea, w),
        [((w, wide + EP), f32)] + [((w, wide + EP), bf16)] * (n_p - 1),
        [*early_msgs, *mid_msgs, *c_msgs],
        flops=2 * S * T * 128 * (wide + EP),
        scratch=[
            pltpu.VMEM((128, wide + EP), f32), pltpu.VMEM((S * T, 256), bf16), pltpu.VMEM((S * T, wide), bf16),
            pltpu.VMEM((EP, S * T), bf16),
        ],
        smem=[ids],
        name="out_grads",
    )
    a_parts = L.planes_of(grads_a)
    up_grad, down_grad = pl.pallas_call(
        partial(expert_grads_body, n_p, eb),
        grid=(n_eb,),
        in_specs=whole * 2 + [pl.BlockSpec((n_p, 2, eb, pairs * R, H), lambda i: (0, 0, i, 0, 0))],
        out_specs=[
            pl.BlockSpec((eb, Dp, H), lambda i: (i, 0, 0)),
            pl.BlockSpec((eb, H, Dp), lambda i: (i, 0, 0)),
        ],
        scratch_shapes=[
            pltpu.VMEM((n_p * pairs, ep, 2 * T), f32),
            pltpu.VMEM((eb * n_p * pairs * R, 2 * Dp), bf16),
        ],
        out_shape=[jax.ShapeDtypeStruct((el, Dp, H), f32), jax.ShapeDtypeStruct((el, H, Dp), f32)],
        compiler_params=pltpu.CompilerParams(vmem_limit_bytes=VMEM_LIMIT),
        cost_estimate=pl.CostEstimate(
            flops=16 * el * pairs * R * Dp * H, bytes_accessed=12 * el * D * H // 4, transcendentals=0
        ),
        name="expert_grads",
    )(cc_all, xc_all, after(rdu_all, grads_a, input_grad))

    late_far, a_parts, up_grad = lax.optimization_barrier((late_far, a_parts, up_grad))
    sum_a = sum(m.astype(f32) for m in a_parts)
    late_msgs = L.relay(late_far)
    gy_parts = go_home(after(gy_join, late_far))
    output = (h1 + sum(m.astype(f32) for m in gy_parts)).astype(bf16)

    grads_b = call(
        partial(in_grads_body, S, n_p, heads, ea, w),
        [((w, wide + 2 * hd + 128), f32)] + [((w, wide + 2 * hd + 128), bf16)] * (n_p - 1),
        [*early_msgs, *late_msgs],
        flops=2 * S * T * 128 * (wide + 2 * hd),
        scratch=[
            pltpu.VMEM((128, wide + 2 * hd + 128), f32), pltpu.VMEM((S * T, 256), bf16),
            pltpu.VMEM((S * T, wide), bf16), pltpu.VMEM((S * T, 2 * hd + 128), bf16),
        ],
        smem=[ids],
        name="in_grads",
    )
    sum_b = sum(m.astype(f32) for m in L.planes_of(grads_b))

    counts = jnp.sum(small[:, 4:].reshape(n_p, S, 2 * w), axis=0)[:, :el].reshape(-1)[:EXPERTS]
    vectors = jnp.sum(small[:, :4], axis=0)
    fgrad = sum_a[:, wide:].reshape(w, S, ep)[:, :, :el].reshape(w, S * el)[:, :EXPERTS]
    sel = sum_b[:, wide + 2 * hd :]
    return (
        output, input_grad, vectors[2], vectors[3], sum_b[:, wide : wide + hd],
        sum_b[:, wide + hd : wide + 2 * hd], sum_b[:, :wide], sum_a[:, :wide].T,
        sel[:, :he], sel[:, he : 2 * he], vectors[0], vectors[1], fgrad, up_grad, down_grad, counts,
    )


def solution(mesh):
    path = fast_path if mesh.shape["expert"] == 8 and mesh.shape["dp"] == 4 else general_path
    placed = (
        P(("dp", "expert"), None),
        P(("dp", "expert"), None),
        P(("dp", "expert")),
        P(("dp", "expert"), None, None),
        P(("dp", "expert"), None, None),
        P(("dp", "expert"), None),
        P(),
        P(),
        P(),
        P(),
        P(),
        P(),
        P(),
        P(),
        P(),
        P(),
        P(),
        P("expert", None, None),
        P("expert", None, None),
    )
    return jax.shard_map(
        path,
        mesh=mesh,
        in_specs=placed,
        out_specs=(
            P(("dp", "expert"), None),
            P(("dp", "expert"), None),
            P(("dp", "expert")),
            P(("dp", "expert")),
            P(("dp", "expert"), None),
            P(("dp", "expert"), None),
            P(("dp", "expert"), None),
            P(None, ("dp", "expert")),
            P(("dp", "expert"), None),
            P(("dp", "expert"), None),
            P(("dp", "expert")),
            P(("dp", "expert")),
            P(("dp", "expert"), None),
            P("expert", "dp", None),
            P("expert", None, "dp"),
            P(),
        ),
        check_vma=False,
    )
```

```python
import math
from functools import partial

import jax
import jax.numpy as jnp
from jax import lax
from jax.experimental import pallas as pl
from jax.experimental.pallas import tpu as pltpu
from jax.sharding import PartitionSpec as P

EXPERTS = 387
MOST = 8
EPSILON = 1e-05
NEGATIVE = -1e30
f32 = jnp.float32
bf16 = jnp.bfloat16
VMEM_LIMIT = 56 * 1024 * 1024
GELU_A = math.sqrt(2.0 / math.pi)
GELU_B = 0.044715


def layer_norm(values, scaling, offset):
    centred = values - jnp.mean(values, axis=-1, keepdims=True)
    inverse = lax.rsqrt(jnp.mean(centred * centred, axis=-1, keepdims=True) + EPSILON)
    normed = centred * inverse
    return (normed * scaling + offset, normed, inverse)


def norm_backward(upstream, normed, inverse, scaling):
    scaled = upstream * scaling
    centre_term = jnp.mean(scaled, axis=-1, keepdims=True)
    slope_term = jnp.mean(scaled * normed, axis=-1, keepdims=True)
    return inverse * (scaled - centre_term - normed * slope_term)


def gate_table(logits, routes, choices_count):
    chosen = jnp.any(routes[..., None] == jnp.arange(choices_count), axis=-2)
    sigmas = jax.nn.sigmoid(logits)
    return (chosen, sigmas, jnp.where(chosen, sigmas, 0.0))


def general_path(
    layer_input,
    cotangent,
    lengths,
    value_routes,
    output_routes,
    ffn_routes,
    att_gain,
    att_shift,
    query_weight,
    key_weight,
    value_weight,
    output_weight,
    value_selector,
    output_selector,
    ffn_gain,
    ffn_shift,
    ffn_selector,
    up_weight,
    down_weight,
):
    f32 = jnp.float32
    bf16 = jnp.bfloat16
    seq_len, width = layer_input.shape
    heads = value_routes.shape[1]
    head_dim = query_weight.shape[1] // heads
    att_experts = value_selector.shape[1] // heads
    top_ffn = ffn_routes.shape[1]
    exp_local = up_weight.shape[0]
    owners = lax.axis_size("expert")
    padded_experts = exp_local * owners
    capacity = MOST
    scaling = 1.0 / math.sqrt(head_dim)
    positions = jnp.arange(seq_len)
    is_valid = positions < lengths[0]
    validity = is_valid.astype(f32)
    input_float = layer_input.astype(f32)
    norm_att, hat_att, inv_att = layer_norm(input_float, att_gain, att_shift)
    act_att = norm_att.astype(bf16)
    queries = (
        jnp.dot(act_att, query_weight, preferred_element_type=f32)
        .astype(bf16)
        .reshape(seq_len, heads, head_dim)
    )
    key_rows = (
        jnp.dot(act_att, key_weight, preferred_element_type=f32)
        .astype(bf16)
        .reshape(seq_len, heads, head_dim)
    )
    projected = jnp.dot(layer_input, value_weight, preferred_element_type=f32).reshape(
        seq_len, heads, att_experts, head_dim
    )
    value_logits = jnp.dot(act_att, value_selector, preferred_element_type=f32).reshape(
        seq_len, heads, att_experts
    )
    output_logits = jnp.dot(act_att, output_selector, preferred_element_type=f32).reshape(
        seq_len, heads, att_experts
    )
    value_pick, value_sig, value_gates = gate_table(value_logits, value_routes, att_experts)
    out_pick, out_sig, out_gates = gate_table(output_logits, output_routes, att_experts)
    values_low = jnp.sum(value_gates[..., None] * projected, axis=2).astype(bf16)
    causal = (positions[None, :] <= positions[:, None]) & is_valid[None, :]
    raw_scores = jnp.einsum("qhd,khd->hqk", queries, key_rows, preferred_element_type=f32) * scaling
    scores = jnp.where(causal[None], raw_scores, NEGATIVE)
    row_peak = jnp.max(scores, axis=-1, keepdims=True)
    log_total = row_peak + jnp.log(jnp.sum(jnp.exp(scores - row_peak), axis=-1, keepdims=True))
    weights_p = jnp.exp(scores - log_total)
    weights_low = weights_p.astype(bf16)
    attended = jnp.einsum("hqk,khd->qhd", weights_low, values_low, preferred_element_type=f32)
    mixed_rows = (out_gates[..., None] * attended[:, :, None, :]).reshape(seq_len, -1).astype(bf16)
    residual = input_float + jnp.dot(mixed_rows, output_weight, preferred_element_type=f32)
    norm_ffn, hat_ffn, inv_ffn = layer_norm(residual, ffn_gain, ffn_shift)
    act_ffn = norm_ffn.astype(bf16)
    ffn_logits = jnp.dot(act_ffn, ffn_selector, preferred_element_type=f32)
    ffn_sig = jax.nn.sigmoid(jnp.take_along_axis(ffn_logits, ffn_routes, axis=1))
    gate_weights = ffn_sig * validity[:, None]
    entries = ffn_routes.reshape(-1)
    live_entry = jnp.broadcast_to(is_valid[:, None], ffn_routes.shape).reshape(-1)
    onehot_table = (
        (entries[:, None] == jnp.arange(padded_experts)[None, :]) & live_entry[:, None]
    ).astype(jnp.int32)
    before = jnp.cumsum(onehot_table, axis=0) - onehot_table
    slot_rank = jnp.sum(before * onehot_table, axis=1)
    counts_local = jnp.sum(onehot_table, axis=0).astype(f32)
    target = jnp.where(live_entry, entries * capacity + slot_rank, padded_experts * capacity)
    fetch = jnp.minimum(target, padded_experts * capacity - 1)
    total_slots = padded_experts * capacity
    residual_low = residual.astype(bf16)
    copies = jnp.broadcast_to(residual_low[:, None, :], (seq_len, top_ffn, width)).reshape(
        -1, width
    )
    send_rows = jnp.zeros((total_slots, width), bf16).at[target].set(copies, mode="drop")
    received = lax.all_to_all(
        send_rows.reshape(owners, exp_local * capacity, width),
        "expert",
        split_axis=0,
        concat_axis=0,
        tiled=True,
    )
    received = received.reshape(owners, exp_local, capacity, width)
    hidden_pre = jnp.einsum("semd,edh->semh", received, up_weight, preferred_element_type=f32)
    hidden_act = jax.nn.gelu(hidden_pre).astype(bf16)
    expert_out = jnp.einsum(
        "semh,ehd->semd", hidden_act, down_weight, preferred_element_type=f32
    ).astype(bf16)
    returned = lax.all_to_all(
        expert_out.reshape(owners, exp_local * capacity, width),
        "expert",
        split_axis=0,
        concat_axis=0,
        tiled=True,
    )
    gathered = (
        returned.reshape(total_slots, width)[fetch].reshape(seq_len, top_ffn, width).astype(f32)
    )
    final = residual + jnp.einsum("tk,tkd->td", gate_weights, gathered)
    output = final.astype(bf16)
    counts_all = lax.psum(counts_local, ("dp", "expert"))
    grad_final = cotangent.astype(f32)
    grad_rows = (gate_weights[:, :, None] * grad_final[:, None, :]).astype(bf16).reshape(-1, width)
    grad_gate = validity[:, None] * jnp.einsum("tkd,td->tk", gathered, grad_final)
    send_grad = jnp.zeros((total_slots, width), bf16).at[target].set(grad_rows, mode="drop")
    grad_recv = lax.all_to_all(
        send_grad.reshape(owners, exp_local * capacity, width),
        "expert",
        split_axis=0,
        concat_axis=0,
        tiled=True,
    )
    grad_recv = grad_recv.reshape(owners, exp_local, capacity, width)
    down_local = jnp.einsum("semh,semd->ehd", hidden_act, grad_recv, preferred_element_type=f32)
    grad_act = jnp.einsum("semd,ehd->semh", grad_recv, down_weight, preferred_element_type=f32)
    gelu_value, gelu_back = jax.vjp(jax.nn.gelu, hidden_pre)
    grad_pre = gelu_back(grad_act)[0].astype(bf16)
    up_local = jnp.einsum("semd,semh->edh", received, grad_pre, preferred_element_type=f32)
    grad_in = jnp.einsum("semh,edh->semd", grad_pre, up_weight, preferred_element_type=f32).astype(
        bf16
    )
    grad_back = lax.all_to_all(
        grad_in.reshape(owners, exp_local * capacity, width),
        "expert",
        split_axis=0,
        concat_axis=0,
        tiled=True,
    )
    grad_copies = (
        grad_back.reshape(total_slots, width)[fetch].reshape(seq_len, top_ffn, width).astype(f32)
    )
    grad_residual = grad_final + jnp.einsum("t,tkd->td", validity, grad_copies)
    sig_grad = grad_gate * ffn_sig * (1.0 - ffn_sig)
    dense_select = jnp.sum(
        jnp.where(ffn_routes[:, :, None] == jnp.arange(EXPERTS), sig_grad[:, :, None], 0.0), axis=1
    ).astype(bf16)
    ffn_selector_local = jnp.einsum("td,te->de", act_ffn, dense_select, preferred_element_type=f32)
    grad_norm_ffn = jnp.einsum("te,de->td", dense_select, ffn_selector, preferred_element_type=f32)
    ffn_gain_local = jnp.sum(grad_norm_ffn * hat_ffn, axis=0)
    ffn_shift_local = jnp.sum(grad_norm_ffn, axis=0)
    grad_residual = grad_residual + norm_backward(grad_norm_ffn, hat_ffn, inv_ffn, ffn_gain)
    grad_att_low = grad_residual.astype(bf16)
    output_local = jnp.einsum("tc,td->cd", mixed_rows, grad_att_low, preferred_element_type=f32)
    grad_mixed = jnp.einsum("td,cd->tc", grad_att_low, output_weight, preferred_element_type=f32)
    grad_mixed = grad_mixed.reshape(seq_len, heads, att_experts, head_dim)
    grad_attended = jnp.sum(out_gates[..., None] * grad_mixed, axis=2).astype(bf16)
    grad_out_gates = jnp.sum(grad_mixed * attended[:, :, None, :], axis=-1)
    out_select = (
        jnp.where(out_pick, grad_out_gates * out_sig * (1.0 - out_sig), 0.0)
        .reshape(seq_len, -1)
        .astype(bf16)
    )
    grad_weights = jnp.einsum("qhd,khd->hqk", grad_attended, values_low, preferred_element_type=f32)
    row_delta = jnp.sum(weights_p * grad_weights, axis=-1, keepdims=True)
    grad_scores = (weights_p * (grad_weights - row_delta)).astype(bf16)
    grad_queries = (
        (jnp.einsum("hqk,khd->qhd", grad_scores, key_rows, preferred_element_type=f32) * scaling)
        .reshape(seq_len, -1)
        .astype(bf16)
    )
    grad_keys = (
        (jnp.einsum("hqk,qhd->khd", grad_scores, queries, preferred_element_type=f32) * scaling)
        .reshape(seq_len, -1)
        .astype(bf16)
    )
    grad_values = jnp.einsum(
        "hqk,qhd->khd", weights_low, grad_attended, preferred_element_type=f32
    ).astype(bf16)
    grad_values_float = grad_values.astype(f32)
    grad_projected = (
        (value_gates[..., None] * grad_values_float[:, :, None, :])
        .reshape(seq_len, -1)
        .astype(bf16)
    )
    grad_value_gates = jnp.sum(grad_values_float[:, :, None, :] * projected, axis=-1)
    value_select = (
        jnp.where(value_pick, grad_value_gates * value_sig * (1.0 - value_sig), 0.0)
        .reshape(seq_len, -1)
        .astype(bf16)
    )
    value_local = jnp.einsum("td,tc->dc", layer_input, grad_projected, preferred_element_type=f32)
    query_local = jnp.einsum("td,tc->dc", act_att, grad_queries, preferred_element_type=f32)
    key_local = jnp.einsum("td,tc->dc", act_att, grad_keys, preferred_element_type=f32)
    value_selector_local = jnp.einsum(
        "td,tc->dc", act_att, value_select, preferred_element_type=f32
    )
    output_selector_local = jnp.einsum("td,tc->dc", act_att, out_select, preferred_element_type=f32)
    grad_norm_att = jnp.einsum("tc,dc->td", grad_queries, query_weight, preferred_element_type=f32)
    grad_norm_att = grad_norm_att + jnp.einsum(
        "tc,dc->td", grad_keys, key_weight, preferred_element_type=f32
    )
    grad_norm_att = grad_norm_att + jnp.einsum(
        "tc,dc->td", value_select, value_selector, preferred_element_type=f32
    )
    grad_norm_att = grad_norm_att + jnp.einsum(
        "tc,dc->td", out_select, output_selector, preferred_element_type=f32
    )
    att_gain_local = jnp.sum(grad_norm_att * hat_att, axis=0)
    att_shift_local = jnp.sum(grad_norm_att, axis=0)
    input_grad = grad_residual + jnp.einsum(
        "tc,dc->td", grad_projected, value_weight, preferred_element_type=f32
    )
    input_grad = input_grad + norm_backward(grad_norm_att, hat_att, inv_att, att_gain)
    reduced = (
        lax.psum_scatter(att_gain_local, ("dp", "expert"), scatter_dimension=0, tiled=True),
        lax.psum_scatter(att_shift_local, ("dp", "expert"), scatter_dimension=0, tiled=True),
        lax.psum_scatter(query_local, ("dp", "expert"), scatter_dimension=0, tiled=True),
        lax.psum_scatter(key_local, ("dp", "expert"), scatter_dimension=0, tiled=True),
        lax.psum_scatter(value_local, ("dp", "expert"), scatter_dimension=0, tiled=True),
        lax.psum_scatter(output_local, ("dp", "expert"), scatter_dimension=1, tiled=True),
        lax.psum_scatter(value_selector_local, ("dp", "expert"), scatter_dimension=0, tiled=True),
        lax.psum_scatter(output_selector_local, ("dp", "expert"), scatter_dimension=0, tiled=True),
        lax.psum_scatter(ffn_gain_local, ("dp", "expert"), scatter_dimension=0, tiled=True),
        lax.psum_scatter(ffn_shift_local, ("dp", "expert"), scatter_dimension=0, tiled=True),
        lax.psum_scatter(ffn_selector_local, ("dp", "expert"), scatter_dimension=0, tiled=True),
    )
    up_grad, down_grad = (
        lax.psum_scatter(
            up_local.astype(jnp.bfloat16), "dp", scatter_dimension=1, tiled=True
        ).astype(jnp.float32),
        lax.psum_scatter(
            down_local.astype(jnp.bfloat16), "dp", scatter_dimension=2, tiled=True
        ).astype(jnp.float32),
    )
    return (
        output,
        input_grad,
        reduced[0],
        reduced[1],
        reduced[2],
        reduced[3],
        reduced[4],
        reduced[5],
        reduced[6],
        reduced[7],
        reduced[8],
        reduced[9],
        reduced[10],
        up_grad,
        down_grad,
        counts_all[:EXPERTS],
    )


def mm(a, b, ca, cb):
    return lax.dot_general(a, b, (((ca,), (cb,)), ((), ())), preferred_element_type=f32)


def iota(shape, dim):
    return lax.broadcasted_iota(jnp.int32, shape, dim)


def centre(values):
    centred = values - jnp.mean(values, axis=-1, keepdims=True)
    inverse = lax.rsqrt(jnp.mean(centred * centred, axis=-1, keepdims=True) + EPSILON)
    return centred * inverse, inverse


def centre_back(upstream, normed, inverse, gain):
    scaled = upstream * gain
    mean = jnp.mean(scaled, axis=-1, keepdims=True)
    slope = jnp.mean(scaled * normed, axis=-1, keepdims=True)
    return inverse * (scaled - mean - normed * slope)


def device_of(ids, s, x):
    return 2 * s + (ids[1] + x - 2 * ids[1] * x)


SHORT = pl.CostEstimate(flops=1, bytes_accessed=1, transcendentals=0)


LONG = pl.CostEstimate(flops=1, bytes_accessed=1 << 28, transcendentals=0)


def call(body, outs, args, scratch=(), smem=(), name=None, cost=SHORT):
    return pl.pallas_call(
        body,
        out_shape=[jax.ShapeDtypeStruct(s, d) for s, d in outs],
        in_specs=[pl.BlockSpec(memory_space=pltpu.SMEM)] * len(smem)
        + [pl.BlockSpec(memory_space=pltpu.VMEM)] * len(args),
        out_specs=[pl.BlockSpec(memory_space=pltpu.VMEM)] * len(outs),
        scratch_shapes=list(scratch),
        compiler_params=pltpu.CompilerParams(vmem_limit_bytes=VMEM_LIMIT),
        cost_estimate=cost,
        name=name,
    )(*smem, *args)


def forward_body(
    length, li, vroutes, oroutes, froutes, att_gain, att_shift, wq, wk, wv, wo, selw,
    ffn_gain, ffn_shift, fsel,
    h1_o, xpack_o, q_o, k_o, v_o, p_o, a_o, o_o, gt_o, a1_o, a2_o, mixed,
):
    T, D = li.shape
    heads = vroutes.shape[1] // 2
    dh = wq.shape[1] // heads
    ea = wv.shape[1] // (heads * dh)
    he = heads * ea
    scaling = 1.0 / math.sqrt(dh)
    x = li[...].astype(f32)
    hat, inv = centre(x)
    mean = jnp.mean(x, axis=-1, keepdims=True)
    a1 = (hat * att_gain[...] + att_shift[...]).astype(bf16)
    a1_o[...] = a1
    logits = mm(a1, selw[...], 1, 0)
    lane = iota((T, 128), 1)
    chosen = jnp.zeros((T, 128), jnp.bool_)
    for j in range(2 * heads):
        h = j // 2
        chosen |= lane == vroutes[:, j : j + 1] + h * ea
        chosen |= lane == oroutes[:, j : j + 1] + (he + h * ea)
    gt = jnp.where(chosen, jax.nn.sigmoid(logits), 0.0)
    gt_o[...] = jnp.where(lane == 2 * he, mean, jnp.where(lane == 2 * he + 1, inv, gt))
    q = mm(a1, wq[...], 1, 0).astype(bf16)
    k = mm(a1, wk[...], 1, 0).astype(bf16)
    q_o[...] = q
    k_o[...] = k
    n_live = length[0]
    row, col = iota((T, T), 0), iota((T, T), 1)
    causal = (col <= row) & (col < n_live)
    width = ea * dh
    for h in range(heads):
        proj = mm(li[...], wv[:, h * width : (h + 1) * width], 1, 0)
        p_o[:, h * width : (h + 1) * width] = proj
        v = jnp.zeros((T, dh), f32)
        for e in range(ea):
            v += gt[:, h * ea + e : h * ea + e + 1] * proj[:, e * dh : (e + 1) * dh]
        v = v.astype(bf16)
        v_o[:, h * dh : (h + 1) * dh] = v
        s = mm(q[:, h * dh : (h + 1) * dh], k[:, h * dh : (h + 1) * dh], 1, 1) * scaling
        s = jnp.where(causal, s, NEGATIVE)
        ex = jnp.exp(s - jnp.max(s, axis=-1, keepdims=True))
        a = ex / jnp.sum(ex, axis=-1, keepdims=True)
        a_o[h] = a
        o = mm(a.astype(bf16), v, 1, 0)
        o_o[:, h * dh : (h + 1) * dh] = o
        for e in range(ea):
            c = he + h * ea + e
            mixed[:, (h * ea + e) * dh : (h * ea + e + 1) * dh] = (gt[:, c : c + 1] * o).astype(bf16)
    h1 = x + mm(mixed[...], wo[...], 1, 0)
    h1_o[...] = h1
    hat2, _ = centre(h1)
    a2 = (hat2 * ffn_gain[...] + ffn_shift[...]).astype(bf16)
    a2_o[...] = a2
    sig = jax.nn.sigmoid(mm(a2, fsel[...], 1, 0))
    wide = iota(sig.shape, 1)
    g = jnp.zeros((T, 128), f32)
    for i in range(froutes.shape[1]):
        one = jnp.sum(jnp.where(wide == froutes[:, i : i + 1], sig, 0.0), axis=-1, keepdims=True)
        g = jnp.where(lane == i, one, g)
    g = g.T[:16]
    hi = g.astype(bf16)
    low = h1.astype(bf16)
    for s in range(xpack_o.shape[0]):
        xpack_o[s, :T] = low
        xpack_o[s, T:] = jnp.zeros((16, D), bf16)
        xpack_o[s, T:, :128] = hi
        xpack_o[s, T:, 128:256] = (g - hi.astype(f32)).astype(bf16)


def take_slices(v, n_p, S, e):
    D = v.shape[1]
    w = D // (n_p * S)
    return jnp.concatenate(
        [v[:, (b * S + e) * w : (b * S + e + 1) * w] for b in range(n_p)], axis=1
    )


def views(mine, theirs):
    return [r.at[s] for s in range(mine.shape[0]) for r in (mine, theirs)]


def views_from(ids, mine, theirs):
    return [r.at[ids[0] ^ s] for s in range(mine.shape[0]) for r in (mine, theirs)]


def early_body(n_p, S, ids, li, a1, a2, o, gt, *rest):
    msgs, scratch = rest
    msgs = [msgs.at[s] for s in range(S // 2)]
    hd = o.shape[1]
    for e in range(S):
        for i, v in enumerate((li, a1, a2)):
            scratch[e, :, i * 128 : (i + 1) * 128] = take_slices(v[...].astype(f32), n_p, S, e).astype(bf16)
    hi = gt[...].astype(bf16).astype(f32)
    both = (hi + pltpu.roll(gt[...] - hi, 64, 1)).astype(bf16)
    for s, m in enumerate(msgs):
        m[:, :hd] = o[...].astype(bf16)
        m[:, hd : hd + 128] = both
        m[:, hd + 128 : hd + 512] = scratch[device_of(ids, s, 1)]
        m[:, hd + 512 : hd + 896] = scratch[device_of(ids, s, 0)]


def codes_body(S, ids, *refs):
    c, (code_o, cnt_o) = views_from(ids, *refs[:2]), refs[2:]
    ep = cnt_o.shape[1]
    T = c[0].shape[0] - 16
    strict = (iota((T, T), 0) < iota((T, T), 1)).astype(f32).astype(bf16)
    e_id = iota((ep, T), 0).astype(f32)
    cnt = jnp.zeros((8, ep), f32)
    start = ids[3].astype(f32)
    for k in range(S):
        r = c[k][T:, :T].astype(f32) * 32.0 + c[k][T:, T : 2 * T].astype(f32) - start
        mask = jnp.zeros((ep, T), f32)
        for i in range(r.shape[0]):
            mask += jnp.where(r[i : i + 1] == e_id, 1.0, 0.0)
        low = mask.astype(bf16)
        rank = mm(low, strict, 1, 0) + (MOST * (k % 2))
        cnt += mm(jnp.ones((8, T), bf16), low, 1, 1)
        code_o[k // 2, :, (k % 2) * T : (k % 2 + 1) * T] = jnp.where(mask > 0.5, rank, -1.0).astype(bf16)
    cnt_o[...] = cnt


def columns_body(n_p, order, ids, x, *refs):
    outs = refs[-n_p:]
    T = x.shape[1] - 16
    wide = outs[0].shape[2]
    for k in range(x.shape[0]):
        rows = x.at[ids[0] ^ k if order else k]
        for s in range(n_p):
            at = pl.multiple_of((ids[2] ^ s) * wide, 128)
            outs[s][k, :T, :] = rows[:T, pl.ds(at, wide)]
    if len(refs) > n_p:
        for s in range(n_p):
            outs[s][:, T:, :] = refs[0][...]


def gelu_both(u):
    t = jnp.tanh(GELU_A * (u + GELU_B * u * u * u))
    value = 0.5 * u * (1.0 + t)
    slope = 0.5 * (1.0 + t) + 0.5 * u * (1.0 - t * t) * (GELU_A * (1.0 + 3.0 * GELU_B * u * u))
    return value, slope


def experts_body(S, eb, ids, *refs):
    x, c = views(*refs[:2]), views_from(ids, *refs[2:4])
    code, up, down, dx0, dx1, gy0, gy1, gr_o, du_o, ct, gts, dl, ps, xs, cs, gys, dxs = refs[4:]
    step = pl.program_id(0)
    pairs = S // 2
    R = 2 * MOST
    T = x[0].shape[0] - 16
    D = x[0].shape[1]
    ep = ct.shape[1]
    rows = pairs * R
    H = up.shape[2]

    @pl.when(step == 0)
    def _():
        e_id = iota((ep, T), 0).astype(f32)
        start = ids[3].astype(f32)
        dl[...] = jnp.zeros_like(dl)
        for pr in range(pairs):
            ct[pr] = code[pr].astype(f32)
        for k in range(S):
            r = c[k][T:, :T].astype(f32) * 32.0 + c[k][T:, T : 2 * T].astype(f32) - start
            g = x[k][T:, :T].astype(f32) + x[k][T:, T : 2 * T].astype(f32)
            dense = jnp.zeros((ep, T), f32)
            for i in range(r.shape[0]):
                dense += jnp.where(r[i : i + 1] == e_id, g[i : i + 1], 0.0)
            gts[:, k * T : (k + 1) * T] = dense

    slot = iota((R, 2 * T), 0).astype(f32)
    g_slot = [[None] * pairs for _ in range(eb)]
    onehot = [[None] * pairs for _ in range(eb)]
    for pr in range(pairs):
        blocks = []
        for j in range(eb):
            e = step * eb + j
            hot = jnp.where(ct[pr, pl.ds(e, 1), :] == slot, 1.0, 0.0)
            onehot[j][pr] = hot
            g_slot[j][pr] = jnp.sum(
                hot * gts[pl.ds(e, 1), pr * 2 * T : (pr + 1) * 2 * T], axis=-1, keepdims=True
            )
            blocks.append(hot.astype(bf16))
        block = jnp.concatenate(blocks, axis=0)
        ps[pr, pl.ds(pl.multiple_of(step * (eb * R), R), eb * R), :] = block
        for src, dst in ((x, xs), (c, cs)):
            both = jnp.concatenate([src[2 * pr][:T], src[2 * pr + 1][:T]], axis=0)
            got = mm(block, both, 1, 0).astype(bf16)
            for j in range(eb):
                dst[j * rows + pr * R : j * rows + (pr + 1) * R, :] = got[j * R : (j + 1) * R]
    for first in range(0, eb, 2):
        js = list(range(first, min(first + 2, eb)))
        n = len(js)
        span = slice(first * rows, (first + n) * rows)
        g = jnp.concatenate([p for j in js for p in g_slot[j]], axis=0)
        cj = cs[span, :].astype(f32)
        ups = jnp.concatenate([up[j] for j in js], axis=1)
        downs = jnp.concatenate([down[j] for j in js], axis=0)

        def own(v):
            return jnp.concatenate([v[i * rows : (i + 1) * rows, i * H : (i + 1) * H] for i in range(n)], axis=0)

        def spread_out(v):
            if n == 1:
                return v
            zero = jnp.zeros((rows, H), v.dtype)
            return jnp.concatenate(
                [
                    jnp.concatenate([v[i * rows : (i + 1) * rows] if i == b else zero for b in range(n)], axis=1)
                    for i in range(n)
                ],
                axis=0,
            )

        u = own(mm(xs[span, :], ups, 1, 0))
        value, slope = gelu_both(u)
        r = value.astype(bf16)
        y = mm(spread_out(r), downs, 1, 0).astype(bf16).astype(f32)
        dgate = jnp.sum(cj * y, axis=-1, keepdims=True)
        gy = (g * y).astype(bf16)
        dr = own(mm((g * cj).astype(bf16), downs, 1, 1))
        du = (dr * slope).astype(bf16)
        dx = mm(spread_out(du), ups, 1, 1).astype(bf16)
        gr = (g * r.astype(f32)).astype(bf16)
        dlog = dgate * g * (1.0 - g)
        for i, j in enumerate(js):
            e = step * eb + j
            gr_o[j] = gr[i * rows : (i + 1) * rows]
            du_o[j] = du[i * rows : (i + 1) * rows]
            for pr in range(pairs):
                at = pl.ds(pl.multiple_of(step * (eb * R) + j * R, R), R)
                cut = slice(i * rows + pr * R, i * rows + (pr + 1) * R)
                gys[pr, at, :] = gy[cut]
                dxs[pr, at, :] = dx[cut]
                dl[pl.ds(e, 1), pr * 2 * T : (pr + 1) * 2 * T] = jnp.sum(
                    onehot[j][pr] * dlog[cut], axis=0, keepdims=True
                )

    @pl.when(step == pl.num_programs(0) - 1)
    def _():
        for pr in range(pairs):
            for src, d0, d1 in ((dxs, dx0, dx1), (gys, gy0, gy1)):
                got = mm(ps[pr], src[pr], 0, 0).astype(bf16)
                d0[pr, :T] = got[:T]
                d1[pr, :T] = got[T:]
            for x_i, d in ((0, dx0), (1, dx1)):
                k = 2 * pr + x_i
                part = dl[:, k * T : (k + 1) * T].astype(bf16)
                d[pr, T:] = jnp.zeros((16, D), bf16)
                for b in range(ep // 16):
                    d[pr, T:, b * T : (b + 1) * T] = part[16 * b : 16 * b + 16]


def join_body(T, mine, recv, out):
    half = mine.shape[2] // 2
    for s in range(mine.shape[0]):
        out[s, :T] = (mine[s, :T].astype(f32) + recv[s, :T].astype(f32)).astype(bf16)
        if mine.shape[1] > T:
            out[s, T:, :half] = mine[s, T:, :half]
            out[s, T:, half:] = recv[s, T:, :half]


def ffn_back_body(n_p, S, nz, ids, parts, h1, c, fsel, gain, froutes, cnt, dh1_o, db_o, mid_o, dlt, sl):
    T, D = h1.shape
    ep = dlt.shape[0] // S
    half = D // 2
    dxs = parts[0, :T].astype(f32)
    for s in range(1, nz):
        dxs += parts[s, :T].astype(f32)
    for s in range(nz):
        for x in range(2):
            for b in range(ep // 16):
                at = pl.multiple_of(device_of(ids, s, x) * ep + 16 * b, 16)
                dlt[pl.ds(at, 16), :] = parts[s, T:, x * half + b * T : x * half + (b + 1) * T].astype(f32)
    dl = dlt[...].T
    da2 = mm(dl.astype(bf16), fsel[...], 1, 1)
    hat, inv = centre(h1[...])
    dh1 = c[...].astype(f32) + dxs + centre_back(da2, hat, inv, gain[...])
    dh1_o[...] = dh1
    db = dh1.astype(bf16)
    db_o[...] = db
    low = db.astype(f32)
    for e in range(S):
        sl[e] = take_slices(low, n_p, S, e).astype(bf16)
    wide, lane = iota(dl.shape, 1), iota((T, 128), 1)
    few = jnp.zeros((T, 128), f32)
    for i in range(froutes.shape[1]):
        one = jnp.sum(jnp.where(wide == froutes[:, i : i + 1], dl, 0.0), axis=-1, keepdims=True)
        few = jnp.where(lane == i, one, few)
    few = few.T[:16].astype(bf16)
    hi = cnt[...].astype(bf16)
    lo = (cnt[...] - hi.astype(f32)).astype(bf16)
    vectors = []
    for v in (jnp.sum(da2 * hat, axis=0, keepdims=True), jnp.sum(da2, axis=0, keepdims=True)):
        high = v.astype(bf16).astype(f32)
        for part in (high, v - high):
            vectors += [part[:, b * 256 : (b + 1) * 256] for b in range(D // 256)]
    vectors = jnp.concatenate(vectors, axis=0).astype(bf16)
    for s in range(nz):
        m = mid_o.at[s]
        m[:T, :128] = sl[device_of(ids, s, 1)]
        m[:T, 128:] = sl[device_of(ids, s, 0)]
        m[T : T + 16, :T] = few
        m[T : T + 16, T:] = jnp.zeros((16, 256 - T), bf16)
        m[T : T + 16, T : T + ep] = jnp.concatenate([hi, lo], axis=0)
        m[T + 16 :] = vectors


def attention_back_body(db, wo, gt, o, q, k, v, a, p, late_o, dp_o):
    T, D = db.shape
    heads = a.shape[0]
    dh = q.shape[1] // heads
    ea = p.shape[1] // (heads * dh)
    he, hd = heads * ea, heads * dh
    width = ea * dh
    scaling = 1.0 / math.sqrt(dh)
    lane = iota((T, 128), 1)
    dgates = jnp.zeros((T, 128), f32)
    gates = gt[...]
    for h in range(heads):
        hs = slice(h * dh, (h + 1) * dh)
        dz = mm(db[...], wo[h * width : (h + 1) * width, :], 1, 1)
        oh = o[:, hs]
        do = jnp.zeros((T, dh), f32)
        for e in range(ea):
            c = he + h * ea + e
            piece = dz[:, e * dh : (e + 1) * dh]
            do += gates[:, c : c + 1] * piece
            dgates = jnp.where(lane == c, jnp.sum(piece * oh, axis=-1, keepdims=True), dgates)
        do = do.astype(bf16)
        ah = a[h]
        dv = mm(ah.astype(bf16), do, 0, 0).astype(bf16)
        late_o[0, :, hs] = dv
        dvf = dv.astype(f32)
        for e in range(ea):
            c = h * ea + e
            es = slice(c * dh, (c + 1) * dh)
            dp_o[:, es] = (gates[:, c : c + 1] * dvf).astype(bf16)
            dgates = jnp.where(lane == c, jnp.sum(dvf * p[:, es], axis=-1, keepdims=True), dgates)
        da = mm(do, v[:, hs], 1, 1)
        ds = (ah * (da - jnp.sum(ah * da, axis=-1, keepdims=True))).astype(bf16)
        late_o[0, :, hd + h * dh : hd + (h + 1) * dh] = (mm(ds, k[:, hs], 1, 0) * scaling).astype(bf16)
        late_o[0, :, 2 * hd + h * dh : 2 * hd + (h + 1) * dh] = (mm(ds, q[:, hs], 0, 0) * scaling).astype(bf16)
    late_o[0, :, 3 * hd :] = (dgates * gates * (1.0 - gates)).astype(bf16)
    for s in range(1, late_o.shape[0]):
        late_o[s] = late_o[0]


def input_back_body(late, dp, wq, wk, wv, selw, li, gain, dh1, ig_o):
    hd = wq.shape[1]
    da1 = mm(late[0, :, hd : 2 * hd], wq[...], 1, 1)
    da1 += mm(late[0, :, 2 * hd : 3 * hd], wk[...], 1, 1)
    da1 += mm(late[0, :, 3 * hd :], selw[...], 1, 1)
    hat, inv = centre(li[...].astype(f32))
    ig_o[...] = dh1[...] + mm(dp[...], wv[...], 1, 1) + centre_back(da1, hat, inv, gain[...])


def spread(values, gates, lo, heads, ea, dh):
    return jnp.concatenate(
        [
            (gates[:, lo + h * ea + e : lo + h * ea + e + 1] * values[:, h * dh : (h + 1) * dh]).astype(bf16)
            for h in range(heads)
            for e in range(ea)
        ],
        axis=1,
    )


def spread_body(S, heads, ea, ids, e0, e1, c0, c1, z_o, a2_o, lia1_o, gates_o, routes_o):
    early, cpack = views(e0, e1), views_from(ids, c0, c1)
    T = early[0].shape[0]
    hd = early[0].shape[1] - 896
    for k in range(S):
        ts = slice(k * T, (k + 1) * T)
        m = early[k]
        both = m[:, hd : hd + 128].astype(f32)
        gates = both + pltpu.roll(both, 64, 1)
        gates_o[ts, :] = gates
        z_o[ts, :] = spread(m[:, :hd].astype(f32), gates, heads * ea, heads, ea, hd // heads)
        at = hd + 512 if k % 2 == 0 else hd + 128
        lia1_o[ts, :] = m[:, at : at + 256]
        a2_o[ts, :] = m[:, at + 256 : at + 384]
        routes_o[k * 16 : (k + 1) * 16, :] = (
            cpack[k][T:, :T].astype(f32) * 32.0 + cpack[k][T:, T : 2 * T].astype(f32)
        )


def out_rows(acc, outs, ids, w):
    for s, ref in enumerate(outs):
        plane = ids[2] ^ s
        ref[:w] = acc[pl.ds(pl.multiple_of(plane * w, 8), w), :].astype(ref.dtype)


def out_grads_body(S, n_p, w, ids, m0, m1, z, a2, routes, *refs):
    mid, outs = views(m0, m1), refs[:n_p]
    acc, lhs, dlt, cnt = refs[n_p:]
    T = z.shape[0] // S
    EP = dlt.shape[0]
    e_id = iota((EP, T), 0).astype(f32)
    norms = jnp.zeros((16, 256), f32)
    for k in range(S):
        n = mid[k]
        ts = slice(k * T, (k + 1) * T)
        at = 128 if k % 2 == 0 else 0
        lhs[ts, :] = n[:T, at : at + 128]
        few = n[T : T + 16, :T].astype(f32)
        route = routes[k * 16 : (k + 1) * 16, :]
        dense = jnp.zeros((EP, T), f32)
        for i in range(16):
            dense += jnp.where(route[i : i + 1] == e_id, few[i : i + 1], 0.0)
        dlt[:, ts] = dense.astype(bf16)
        tally = n[T : T + 16, T:].astype(f32)
        at = device_of(ids, k // 2, k % 2)
        cnt[pl.ds(at, 1), :] = tally[:1]
        cnt[pl.ds(at + 8, 1), :] = tally[8:9]
        norms += n[T + 16 :].astype(f32)
    wide = z.shape[1]
    acc[:, :wide] = mm(lhs[...], z[...], 0, 0)
    acc[:, wide:] = mm(dlt[...], a2[...], 1, 0).T
    out_rows(acc, outs, ids, w)
    norms = pltpu.roll(norms, lax.rem(256 - (2 * ids[0] + ids[1]) * w, 256), 1)
    norms = jnp.concatenate([norms[0:4] + norms[4:8], norms[8:12] + norms[12:16]], axis=0)
    for ref in outs:
        ref[w:] = jnp.zeros((16, ref.shape[1]), ref.dtype)
        ref[w:, :128] = cnt[...].astype(ref.dtype)
        ref[w:, 128:256] = jnp.concatenate([norms[:, :128], jnp.zeros((8, 128), f32)], axis=0).astype(ref.dtype)


def in_grads_body(S, n_p, heads, ea, w, ids, l0, l1, lia1, gates, wq, wk, selw, *refs):
    late, outs = views(l0, l1), refs[:n_p]
    acc, rhs, qk, wsl = refs[n_p:]
    T = late[0].shape[0]
    hd = wq.shape[1]
    for k in range(S):
        ts = slice(k * T, (k + 1) * T)
        n = late[k]
        rhs[ts, :] = spread(n[:, :hd].astype(f32), gates[ts, :], 0, heads, ea, hd // heads)
        qk[ts, :] = n[:, hd:]
    wide = rhs.shape[1]
    acc[:, :wide] = mm(lia1[:, :128], rhs[...], 0, 0)
    acc[:, wide:] = mm(lia1[:, 128:], qk[...], 0, 0)
    out_rows(acc, outs, ids, w)
    D = wq.shape[0]
    for b in range(n_p):
        at = pl.ds(pl.multiple_of(b * (D // n_p) + (2 * ids[0] + ids[1]) * w, 16), w)
        bs = slice(b * w, (b + 1) * w)
        wsl[bs, :hd] = wq[at, :]
        wsl[bs, hd : 2 * hd] = wk[at, :]
        wsl[bs, 2 * hd :] = selw[at, :]
    da1 = mm(qk[...], wsl[...], 1, 1)
    he2 = 2 * heads * ea
    hat = (lia1[:, :128].astype(f32) - gates[:, he2 : he2 + 1]) * gates[:, he2 + 1 : he2 + 2]
    gain, shift = jnp.sum(da1 * hat, axis=0, keepdims=True), jnp.sum(da1, axis=0, keepdims=True)
    both = jnp.concatenate([gain, shift, jnp.zeros((14, 128), f32)], axis=0)
    for ref in outs:
        ref[w:] = jnp.zeros((16, ref.shape[1]), ref.dtype)
        ref[w:, :128] = both.astype(ref.dtype)


def last_a_body(n_p, S, w, el, ids, *refs):
    parts, (og_o, fg_o, gain_o, shift_o, counts_o, rows) = refs[:n_p], refs[n_p:]
    total = parts[0][...]
    for m in parts[1:]:
        total += m[...].astype(f32)
    wide = og_o.shape[1]
    og_o[...] = total[:w, :wide]
    sel = total[:w, wide:]
    ep = sel.shape[1] // S
    fg_o[...] = jnp.concatenate([sel[:, e * ep : e * ep + el] for e in range(S)], axis=1)[:, : fg_o.shape[1]]
    rows[...] = total[w:, 128:256]
    gain_o[...] = rows[pl.ds(ids[2], 1), :w]
    shift_o[...] = rows[pl.ds(ids[2] + n_p, 1), :w]
    cnt = total[w : w + 8, :128] + total[w + 8 :, :128]
    counts_o[...] = jnp.concatenate([cnt[e : e + 1, :el] for e in range(S)], axis=1)[:, : counts_o.shape[1]]


def last_b_body(n_p, w, hd, he, ids, *refs):
    parts, (vg_o, qg_o, kg_o, vs_o, os_o, gain_o, shift_o) = refs[:n_p], refs[n_p:]
    total = parts[0][...]
    for m in parts[1:]:
        total += m[...].astype(f32)
    wide = vg_o.shape[1]
    vg_o[...] = total[:w, :wide]
    qg_o[...] = total[:w, wide : wide + hd]
    kg_o[...] = total[:w, wide + hd : wide + 2 * hd]
    sel = total[:w, wide + 2 * hd :].T
    vs_o[...] = sel[:he]
    os_o[...] = sel[he : 2 * he]
    norms = pltpu.roll(total[w : w + 8, :128], lax.rem(128 - ids[2] * w, 128), 1)
    gain_o[...] = norms[0:1, :w]
    shift_o[...] = norms[1:2, :w]


def expert_grads_body(n_p, eb, *refs):
    cm, co, xm, xo = refs[:4]
    gr_in, du_in = refs[4 : 4 + n_p], refs[4 + n_p : 4 + 2 * n_p]
    up_o, down_o, ct, got = refs[4 + 2 * n_p :]
    step = pl.program_id(0)
    _, pairs, T, wide = cm.shape
    T2 = 2 * T
    R = 2 * MOST
    rows = pairs * R

    @pl.when(step == 0)
    def _():
        for s in range(n_p):
            for pr in range(pairs):
                ct[s * pairs + pr] = xm[s, pr, T:, :].astype(f32)

    slot = iota((R, T2), 0).astype(f32)
    for s in range(n_p):
        for pr in range(pairs):
            block = jnp.concatenate(
                [
                    jnp.where(ct[s * pairs + pr, pl.ds(step * eb + j, 1), :] == slot, 1.0, 0.0).astype(bf16)
                    for j in range(eb)
                ],
                axis=0,
            )
            both = jnp.concatenate(
                [
                    jnp.concatenate([xm[s, pr, :T], cm[s, pr]], axis=1),
                    jnp.concatenate([xo[s, pr, :T], co[s, pr]], axis=1),
                ],
                axis=0,
            )
            res = mm(block, both, 1, 0).astype(bf16)
            for j in range(eb):
                at = j * n_p * rows + s * rows + pr * R
                got[at : at + R, :] = res[j * R : (j + 1) * R]
    for j in range(eb):
        at = j * n_p * rows
        xj = got[at : at + n_p * rows, :wide]
        cj = got[at : at + n_p * rows, wide:]
        gr = jnp.concatenate([gr_in[s][j] for s in range(n_p)], axis=0)
        du = jnp.concatenate([du_in[s][j] for s in range(n_p)], axis=0)
        up_o[j] = mm(xj, du, 0, 0)
        down_o[j] = mm(gr, cj, 0, 0)


def after(values, *deps):
    return lax.optimization_barrier((values, deps))[0]


class Links:
    def __init__(self):
        self.n_e = lax.axis_size("expert")
        self.nz = self.n_e // 2
        self.n_p = lax.axis_size("dp")
        self.me = lax.axis_index("expert")
        self.z, self.c = self.me // 2, self.me % 2
        self.p = lax.axis_index("dp")

    def core(self, v):
        return lax.ppermute(v, "expert", [(e, e ^ 1) for e in range(self.n_e)])

    def chips(self, v):
        groups = [[2 * s + c for s in range(self.nz)] for c in range(2)]
        return lax.all_to_all(v, "expert", 0, 0, axis_index_groups=groups, tiled=True)

    def chip(self, v, s):
        return lax.ppermute(v, "expert", [(e, (e + 2 * s) % self.n_e) for e in range(self.n_e)])

    def plane(self, v, s):
        return lax.ppermute(v, "dp", [(p, p ^ s) for p in range(self.n_p)])

    def near(self, msgs):
        pairs = [[(e, e ^ (2 * s)) for e in range(self.n_e)] for s in range(self.nz)]
        return [msgs[0]] + [lax.ppermute(msgs[s], "expert", pairs[s]) for s in range(1, self.nz)]

    def relay(self, mine):
        return [mine, self.core(mine)]

    def planes_of(self, msgs):
        return [msgs[0]] + [self.plane(msgs[s], s) for s in range(1, self.n_p)]


def fast_path(
    layer_input, cotangent, lengths, value_routes, output_routes, ffn_routes, att_gain, att_shift,
    query_weight, key_weight, value_weight, output_weight, value_selector, output_selector,
    ffn_gain, ffn_shift, ffn_selector, up_weight, down_weight,
):
    L = Links()
    S, nz, n_p = L.n_e, L.nz, L.n_p
    pairs = S // 2
    T, D = layer_input.shape
    heads = value_routes.shape[1]
    dh = query_weight.shape[1] // heads
    ea = value_selector.shape[1] // heads
    hd, he, wide = heads * dh, heads * ea, heads * ea * dh
    el, _, H = up_weight.shape
    ep = -(-el // 16) * 16
    EP = ep * S
    w = D // (n_p * S)
    Dp = D // n_p
    R = 2 * MOST
    eb = max(d for d in (7, 4, 2, 1) if el % d == 0)

    ids = jnp.stack([L.z, L.c, L.p, L.me * ep]).astype(jnp.int32)
    padded = (ffn_routes // el) * ep + ffn_routes % el
    selw = jnp.pad(jnp.concatenate([value_selector, output_selector], axis=1), ((0, 0), (0, 128 - 2 * he)))
    fsel = jnp.pad(ffn_selector, ((0, 0), (0, S * el - ffn_selector.shape[1])))
    fsel = jnp.pad(fsel.reshape(D, S, el), ((0, 0), (0, 0), (0, ep - el))).reshape(D, EP)
    v_routes, o_routes = value_routes.reshape(T, -1), output_routes.reshape(T, -1)

    live = jnp.arange(T)[:, None] < lengths[0]
    rt = jnp.where(live, padded, EP).T
    tail = jnp.concatenate([rt // 32, rt % 32], axis=1).astype(bf16)
    cpack = jnp.concatenate([cotangent, jnp.pad(tail, ((0, 0), (0, D - 2 * T)))], axis=0)
    c_far = L.near([cpack] * nz)

    h1, xpack, q, k, v, proj, a, o, gt, a1, a2 = call(
        forward_body,
        [
            ((T, D), f32), ((nz, T + 16, D), bf16), ((T, hd), bf16), ((T, hd), bf16), ((T, hd), bf16),
            ((T, wide), f32), ((heads, T, T), f32), ((T, hd), f32), ((T, 128), f32),
            ((T, D), bf16), ((T, D), bf16),
        ],
        [
            layer_input, v_routes, o_routes, padded,
            att_gain[None], att_shift[None], query_weight, key_weight, value_weight, output_weight,
            selw, ffn_gain[None], ffn_shift[None], fsel,
        ],
        scratch=[pltpu.VMEM((T, wide), bf16)],
        smem=[lengths],
        name="forward",
    )
    x_far = L.chips(xpack)
    (early,) = call(
        partial(early_body, n_p, S),
        [((nz, T, hd + 896), bf16)],
        [layer_input, a1, a2, o, gt],
        scratch=[pltpu.VMEM((S, T, 384), bf16)],
        smem=[ids],
        name="early_slices",
    )
    c_msgs = L.relay(jnp.stack(after(c_far, early)))
    ccols = call(
        partial(columns_body, n_p, True), [((nz, T, Dp), bf16)] * n_p, [after(c_msgs[0], c_msgs[1])], smem=[ids],
        name="cotangent_columns",
    )
    cc_all = L.planes_of(ccols)
    code, cnt = call(
        partial(codes_body, S), [((pairs, ep, 2 * T), bf16), ((8, ep), f32)], after(c_msgs, ccols), smem=[ids],
        name="codes",
    )
    x_far = after(x_far, code, cc_all[1:3])
    x_msgs = L.relay(x_far)
    xcols = call(
        partial(columns_body, n_p, False), [((nz, T + ep, Dp), bf16)] * n_p, [x_far, code],
        smem=[ids],
        name="token_columns",
    )
    xc_all = L.planes_of(xcols)
    early_far = L.chips(after(early, x_far))

    n_eb = el // eb
    whole = [pl.BlockSpec(memory_space=pltpu.VMEM)]
    dx0, dx1, gy0, gy1, gr, du = pl.pallas_call(
        partial(experts_body, S, eb),
        grid=(n_eb,),
        out_shape=[
            jax.ShapeDtypeStruct((pairs, T + 16, D), bf16), jax.ShapeDtypeStruct((pairs, T + 16, D), bf16),
            jax.ShapeDtypeStruct((pairs, T, D), bf16), jax.ShapeDtypeStruct((pairs, T, D), bf16),
            jax.ShapeDtypeStruct((el, pairs * R, H), bf16), jax.ShapeDtypeStruct((el, pairs * R, H), bf16),
        ],
        in_specs=[pl.BlockSpec(memory_space=pltpu.SMEM)]
        + whole * 5
        + [
            pl.BlockSpec((eb, D, H), lambda i: (i, 0, 0)),
            pl.BlockSpec((eb, H, D), lambda i: (i, 0, 0)),
        ],
        out_specs=whole * 4 + [pl.BlockSpec((eb, pairs * R, H), lambda i: (i, 0, 0))] * 2,
        scratch_shapes=[
            pltpu.VMEM((pairs, ep, 2 * T), f32), pltpu.VMEM((ep, S * T), f32), pltpu.VMEM((ep, S * T), f32),
            pltpu.VMEM((pairs, el * R, 2 * T), bf16),
            pltpu.VMEM((eb * pairs * R, D), bf16), pltpu.VMEM((eb * pairs * R, D), bf16),
            pltpu.VMEM((pairs, el * R, D), bf16), pltpu.VMEM((pairs, el * R, D), bf16),
        ],
        compiler_params=pltpu.CompilerParams(vmem_limit_bytes=VMEM_LIMIT),
        cost_estimate=SHORT,
        name="experts",
    )(after(ids, xcols), *x_msgs, *c_msgs, code, up_weight, down_weight)

    def join(mine, other, name):
        return call(partial(join_body, T), [(mine.shape, bf16)], [mine, L.core(other)], name=name)[0]

    dx0, dx1, early_far, cc_all, xc_all = lax.optimization_barrier((dx0, dx1, early_far, cc_all, xc_all))
    dx_join = join(dx0, dx1, "join_dx")
    dx_parts = L.chips(dx_join)
    gr, du = after((gr, du), dx_join)
    gr1, du1 = L.plane(gr, 1), L.plane(du, 2)
    early_far, gy0, gy1, cc_all, xc_all = after((early_far, gy0, gy1, cc_all, xc_all), dx_join)
    cc_both, xc_both = L.relay(jnp.stack(cc_all)), L.relay(jnp.stack(xc_all))
    gy_join = join(gy0, gy1, "join_out")
    z_all, a2_s, lia1, gates, routes = call(
        partial(spread_body, S, heads, ea),
        [
            ((S * T, wide), bf16), ((S * T, 128), bf16), ((S * T, 256), bf16), ((S * T, 128), f32),
            ((S * 16, T), f32),
        ],
        [*L.relay(early_far), *c_msgs],
        smem=[ids],
        cost=LONG,
        name="spread_tokens",
    )
    dx_parts, gr1, du1, z_all, gy_join, cc_both, xc_both = lax.optimization_barrier(
        (dx_parts, gr1, du1, z_all, gy_join, cc_both, xc_both)
    )
    gr, du = after((gr, du), dx_parts)
    gr_all = [gr, gr1, L.plane(gr, 2)]
    du_all = [du, L.plane(du, 1), du1]

    dh1, db, mid = call(
        partial(ffn_back_body, n_p, S, nz),
        [((T, D), f32), ((T, D), bf16), ((nz, T + 32, 256), bf16)],
        [dx_parts, h1, cotangent, fsel, ffn_gain[None], padded, cnt],
        scratch=[pltpu.VMEM((EP, T), f32), pltpu.VMEM((S, T, 128), bf16)],
        smem=[ids],
        name="ffn_back",
    )
    mid_far = L.chips(mid)
    late, dp = call(
        attention_back_body,
        [((nz, T, 3 * hd + 128), bf16), ((T, wide), bf16)],
        [db, output_weight, gt, o, q, k, v, a, proj],
        cost=LONG,
        name="attention_back",
    )
    late = after(late, mid_far, gr_all[2], du_all[1])
    gr1, du1 = after((gr1, du1), late)
    gr_all += [L.plane(gr1, 2)]
    du_all += [L.plane(du1, 1)]
    late_far = L.chips(late)
    (input_grad,) = call(
        input_back_body,
        [((T, D), f32)],
        [late, dp, query_weight, key_weight, value_weight, selw, layer_input, att_gain[None], dh1],
        name="input_back",
    )
    mid_far = after(mid_far, input_grad)
    grads_a = call(
        partial(out_grads_body, S, n_p, w),
        [((w + 16, wide + EP), f32)] + [((w + 16, wide + EP), bf16)] * (n_p - 1),
        [*L.relay(mid_far), z_all, a2_s, routes],
        scratch=[
            pltpu.VMEM((128, wide + EP), f32), pltpu.VMEM((S * T, 128), bf16),
            pltpu.VMEM((EP, S * T), bf16), pltpu.VMEM((16, 128), f32),
        ],
        smem=[ids],
        name="out_grads",
    )
    a_parts = L.planes_of(grads_a)
    up_grad, down_grad = pl.pallas_call(
        partial(expert_grads_body, n_p, eb),
        grid=(n_eb,),
        in_specs=whole * 4 + [pl.BlockSpec((eb, pairs * R, H), lambda i: (i, 0, 0))] * (2 * n_p),
        out_specs=[
            pl.BlockSpec((eb, Dp, H), lambda i: (i, 0, 0)),
            pl.BlockSpec((eb, H, Dp), lambda i: (i, 0, 0)),
        ],
        scratch_shapes=[
            pltpu.VMEM((n_p * pairs, ep, 2 * T), f32),
            pltpu.VMEM((eb * n_p * pairs * R, 2 * Dp), bf16),
        ],
        out_shape=[jax.ShapeDtypeStruct((el, Dp, H), f32), jax.ShapeDtypeStruct((el, H, Dp), f32)],
        compiler_params=pltpu.CompilerParams(vmem_limit_bytes=VMEM_LIMIT),
        cost_estimate=SHORT,
        name="expert_grads",
    )(*cc_both, *xc_both, *after(gr_all + du_all, grads_a))

    late_far, a_parts, up_grad = lax.optimization_barrier((late_far, a_parts, up_grad))
    gy_parts = L.chips(after(gy_join, late_far))
    grads_b = call(
        partial(in_grads_body, S, n_p, heads, ea, w),
        [((w + 16, wide + 2 * hd + 128), f32)] + [((w + 16, wide + 2 * hd + 128), bf16)] * (n_p - 1),
        [*L.relay(late_far), lia1, gates, query_weight, key_weight, selw],
        scratch=[
            pltpu.VMEM((128, wide + 2 * hd + 128), f32), pltpu.VMEM((S * T, wide), bf16),
            pltpu.VMEM((S * T, 2 * hd + 128), bf16), pltpu.VMEM((128, 2 * hd + 128), bf16),
        ],
        smem=[ids],
        cost=LONG,
        name="in_grads",
    )
    b_parts = L.planes_of(grads_b)

    output_grad, fgrad, ffn_gain_grad, ffn_shift_grad, counts = call(
        partial(last_a_body, n_p, S, w, el),
        [((w, wide), f32), ((w, EXPERTS), f32), ((1, w), f32), ((1, w), f32), ((1, EXPERTS), f32)],
        after(a_parts, grads_b),
        scratch=[pltpu.VMEM((16, 128), f32)],
        smem=[ids],
        name="last_sum_a",
    )
    gy_parts, b_parts = after((gy_parts, b_parts), fgrad)
    output = (h1 + jnp.sum(gy_parts.astype(f32), axis=0)).astype(bf16)
    value_grad, query_grad, key_grad, vsel, osel, att_gain_grad, att_shift_grad = call(
        partial(last_b_body, n_p, w, hd, he),
        [
            ((w, wide), f32), ((w, hd), f32), ((w, hd), f32), ((he, w), f32), ((he, w), f32),
            ((1, w), f32), ((1, w), f32),
        ],
        after(b_parts, output),
        smem=[ids],
        name="last_sum_b",
    )
    return (
        output, input_grad, att_gain_grad[0], att_shift_grad[0], query_grad, key_grad, value_grad,
        output_grad.T, vsel.T, osel.T, ffn_gain_grad[0], ffn_shift_grad[0], fgrad, up_grad, down_grad, counts[0],
    )


def solution(mesh):
    path = fast_path if mesh.shape["expert"] == 8 and mesh.shape["dp"] == 4 else general_path
    placed = (
        P(("dp", "expert"), None),
        P(("dp", "expert"), None),
        P(("dp", "expert")),
        P(("dp", "expert"), None, None),
        P(("dp", "expert"), None, None),
        P(("dp", "expert"), None),
        P(),
        P(),
        P(),
        P(),
        P(),
        P(),
        P(),
        P(),
        P(),
        P(),
        P(),
        P("expert", None, None),
        P("expert", None, None),
    )
    return jax.shard_map(
        path,
        mesh=mesh,
        in_specs=placed,
        out_specs=(
            P(("dp", "expert"), None),
            P(("dp", "expert"), None),
            P(("dp", "expert")),
            P(("dp", "expert")),
            P(("dp", "expert"), None),
            P(("dp", "expert"), None),
            P(("dp", "expert"), None),
            P(None, ("dp", "expert")),
            P(("dp", "expert"), None),
            P(("dp", "expert"), None),
            P(("dp", "expert")),
            P(("dp", "expert")),
            P(("dp", "expert"), None),
            P("expert", "dp", None),
            P("expert", None, "dp"),
            P(),
        ),
        check_vma=False,
    )
```

```python
import math
from functools import partial

import jax
import jax.numpy as jnp
from jax import lax
from jax.experimental import pallas as pl
from jax.experimental.pallas import tpu as pltpu
from jax.sharding import PartitionSpec as P

EXPERTS = 387
MOST = 8
EPSILON = 1e-05
NEGATIVE = -1e30
f32 = jnp.float32
bf16 = jnp.bfloat16
VMEM_LIMIT = 56 * 1024 * 1024
GELU_A = math.sqrt(2.0 / math.pi)
GELU_B = 0.044715


def layer_norm(values, scaling, offset):
    centred = values - jnp.mean(values, axis=-1, keepdims=True)
    inverse = lax.rsqrt(jnp.mean(centred * centred, axis=-1, keepdims=True) + EPSILON)
    normed = centred * inverse
    return (normed * scaling + offset, normed, inverse)


def norm_backward(upstream, normed, inverse, scaling):
    scaled = upstream * scaling
    centre_term = jnp.mean(scaled, axis=-1, keepdims=True)
    slope_term = jnp.mean(scaled * normed, axis=-1, keepdims=True)
    return inverse * (scaled - centre_term - normed * slope_term)


def gate_table(logits, routes, choices_count):
    chosen = jnp.any(routes[..., None] == jnp.arange(choices_count), axis=-2)
    sigmas = jax.nn.sigmoid(logits)
    return (chosen, sigmas, jnp.where(chosen, sigmas, 0.0))


def general_path(
    layer_input,
    cotangent,
    lengths,
    value_routes,
    output_routes,
    ffn_routes,
    att_gain,
    att_shift,
    query_weight,
    key_weight,
    value_weight,
    output_weight,
    value_selector,
    output_selector,
    ffn_gain,
    ffn_shift,
    ffn_selector,
    up_weight,
    down_weight,
):
    f32 = jnp.float32
    bf16 = jnp.bfloat16
    seq_len, width = layer_input.shape
    heads = value_routes.shape[1]
    head_dim = query_weight.shape[1] // heads
    att_experts = value_selector.shape[1] // heads
    top_ffn = ffn_routes.shape[1]
    exp_local = up_weight.shape[0]
    owners = lax.axis_size("expert")
    padded_experts = exp_local * owners
    capacity = MOST
    scaling = 1.0 / math.sqrt(head_dim)
    positions = jnp.arange(seq_len)
    is_valid = positions < lengths[0]
    validity = is_valid.astype(f32)
    input_float = layer_input.astype(f32)
    norm_att, hat_att, inv_att = layer_norm(input_float, att_gain, att_shift)
    act_att = norm_att.astype(bf16)
    queries = (
        jnp.dot(act_att, query_weight, preferred_element_type=f32)
        .astype(bf16)
        .reshape(seq_len, heads, head_dim)
    )
    key_rows = (
        jnp.dot(act_att, key_weight, preferred_element_type=f32)
        .astype(bf16)
        .reshape(seq_len, heads, head_dim)
    )
    projected = jnp.dot(layer_input, value_weight, preferred_element_type=f32).reshape(
        seq_len, heads, att_experts, head_dim
    )
    value_logits = jnp.dot(act_att, value_selector, preferred_element_type=f32).reshape(
        seq_len, heads, att_experts
    )
    output_logits = jnp.dot(act_att, output_selector, preferred_element_type=f32).reshape(
        seq_len, heads, att_experts
    )
    value_pick, value_sig, value_gates = gate_table(value_logits, value_routes, att_experts)
    out_pick, out_sig, out_gates = gate_table(output_logits, output_routes, att_experts)
    values_low = jnp.sum(value_gates[..., None] * projected, axis=2).astype(bf16)
    causal = (positions[None, :] <= positions[:, None]) & is_valid[None, :]
    raw_scores = jnp.einsum("qhd,khd->hqk", queries, key_rows, preferred_element_type=f32) * scaling
    scores = jnp.where(causal[None], raw_scores, NEGATIVE)
    row_peak = jnp.max(scores, axis=-1, keepdims=True)
    log_total = row_peak + jnp.log(jnp.sum(jnp.exp(scores - row_peak), axis=-1, keepdims=True))
    weights_p = jnp.exp(scores - log_total)
    weights_low = weights_p.astype(bf16)
    attended = jnp.einsum("hqk,khd->qhd", weights_low, values_low, preferred_element_type=f32)
    mixed_rows = (out_gates[..., None] * attended[:, :, None, :]).reshape(seq_len, -1).astype(bf16)
    residual = input_float + jnp.dot(mixed_rows, output_weight, preferred_element_type=f32)
    norm_ffn, hat_ffn, inv_ffn = layer_norm(residual, ffn_gain, ffn_shift)
    act_ffn = norm_ffn.astype(bf16)
    ffn_logits = jnp.dot(act_ffn, ffn_selector, preferred_element_type=f32)
    ffn_sig = jax.nn.sigmoid(jnp.take_along_axis(ffn_logits, ffn_routes, axis=1))
    gate_weights = ffn_sig * validity[:, None]
    entries = ffn_routes.reshape(-1)
    live_entry = jnp.broadcast_to(is_valid[:, None], ffn_routes.shape).reshape(-1)
    onehot_table = (
        (entries[:, None] == jnp.arange(padded_experts)[None, :]) & live_entry[:, None]
    ).astype(jnp.int32)
    before = jnp.cumsum(onehot_table, axis=0) - onehot_table
    slot_rank = jnp.sum(before * onehot_table, axis=1)
    counts_local = jnp.sum(onehot_table, axis=0).astype(f32)
    target = jnp.where(live_entry, entries * capacity + slot_rank, padded_experts * capacity)
    fetch = jnp.minimum(target, padded_experts * capacity - 1)
    total_slots = padded_experts * capacity
    residual_low = residual.astype(bf16)
    copies = jnp.broadcast_to(residual_low[:, None, :], (seq_len, top_ffn, width)).reshape(
        -1, width
    )
    send_rows = jnp.zeros((total_slots, width), bf16).at[target].set(copies, mode="drop")
    received = lax.all_to_all(
        send_rows.reshape(owners, exp_local * capacity, width),
        "expert",
        split_axis=0,
        concat_axis=0,
        tiled=True,
    )
    received = received.reshape(owners, exp_local, capacity, width)
    hidden_pre = jnp.einsum("semd,edh->semh", received, up_weight, preferred_element_type=f32)
    hidden_act = jax.nn.gelu(hidden_pre).astype(bf16)
    expert_out = jnp.einsum(
        "semh,ehd->semd", hidden_act, down_weight, preferred_element_type=f32
    ).astype(bf16)
    returned = lax.all_to_all(
        expert_out.reshape(owners, exp_local * capacity, width),
        "expert",
        split_axis=0,
        concat_axis=0,
        tiled=True,
    )
    gathered = (
        returned.reshape(total_slots, width)[fetch].reshape(seq_len, top_ffn, width).astype(f32)
    )
    final = residual + jnp.einsum("tk,tkd->td", gate_weights, gathered)
    output = final.astype(bf16)
    counts_all = lax.psum(counts_local, ("dp", "expert"))
    grad_final = cotangent.astype(f32)
    grad_rows = (gate_weights[:, :, None] * grad_final[:, None, :]).astype(bf16).reshape(-1, width)
    grad_gate = validity[:, None] * jnp.einsum("tkd,td->tk", gathered, grad_final)
    send_grad = jnp.zeros((total_slots, width), bf16).at[target].set(grad_rows, mode="drop")
    grad_recv = lax.all_to_all(
        send_grad.reshape(owners, exp_local * capacity, width),
        "expert",
        split_axis=0,
        concat_axis=0,
        tiled=True,
    )
    grad_recv = grad_recv.reshape(owners, exp_local, capacity, width)
    down_local = jnp.einsum("semh,semd->ehd", hidden_act, grad_recv, preferred_element_type=f32)
    grad_act = jnp.einsum("semd,ehd->semh", grad_recv, down_weight, preferred_element_type=f32)
    gelu_value, gelu_back = jax.vjp(jax.nn.gelu, hidden_pre)
    grad_pre = gelu_back(grad_act)[0].astype(bf16)
    up_local = jnp.einsum("semd,semh->edh", received, grad_pre, preferred_element_type=f32)
    grad_in = jnp.einsum("semh,edh->semd", grad_pre, up_weight, preferred_element_type=f32).astype(
        bf16
    )
    grad_back = lax.all_to_all(
        grad_in.reshape(owners, exp_local * capacity, width),
        "expert",
        split_axis=0,
        concat_axis=0,
        tiled=True,
    )
    grad_copies = (
        grad_back.reshape(total_slots, width)[fetch].reshape(seq_len, top_ffn, width).astype(f32)
    )
    grad_residual = grad_final + jnp.einsum("t,tkd->td", validity, grad_copies)
    sig_grad = grad_gate * ffn_sig * (1.0 - ffn_sig)
    dense_select = jnp.sum(
        jnp.where(ffn_routes[:, :, None] == jnp.arange(EXPERTS), sig_grad[:, :, None], 0.0), axis=1
    ).astype(bf16)
    ffn_selector_local = jnp.einsum("td,te->de", act_ffn, dense_select, preferred_element_type=f32)
    grad_norm_ffn = jnp.einsum("te,de->td", dense_select, ffn_selector, preferred_element_type=f32)
    ffn_gain_local = jnp.sum(grad_norm_ffn * hat_ffn, axis=0)
    ffn_shift_local = jnp.sum(grad_norm_ffn, axis=0)
    grad_residual = grad_residual + norm_backward(grad_norm_ffn, hat_ffn, inv_ffn, ffn_gain)
    grad_att_low = grad_residual.astype(bf16)
    output_local = jnp.einsum("tc,td->cd", mixed_rows, grad_att_low, preferred_element_type=f32)
    grad_mixed = jnp.einsum("td,cd->tc", grad_att_low, output_weight, preferred_element_type=f32)
    grad_mixed = grad_mixed.reshape(seq_len, heads, att_experts, head_dim)
    grad_attended = jnp.sum(out_gates[..., None] * grad_mixed, axis=2).astype(bf16)
    grad_out_gates = jnp.sum(grad_mixed * attended[:, :, None, :], axis=-1)
    out_select = (
        jnp.where(out_pick, grad_out_gates * out_sig * (1.0 - out_sig), 0.0)
        .reshape(seq_len, -1)
        .astype(bf16)
    )
    grad_weights = jnp.einsum("qhd,khd->hqk", grad_attended, values_low, preferred_element_type=f32)
    row_delta = jnp.sum(weights_p * grad_weights, axis=-1, keepdims=True)
    grad_scores = (weights_p * (grad_weights - row_delta)).astype(bf16)
    grad_queries = (
        (jnp.einsum("hqk,khd->qhd", grad_scores, key_rows, preferred_element_type=f32) * scaling)
        .reshape(seq_len, -1)
        .astype(bf16)
    )
    grad_keys = (
        (jnp.einsum("hqk,qhd->khd", grad_scores, queries, preferred_element_type=f32) * scaling)
        .reshape(seq_len, -1)
        .astype(bf16)
    )
    grad_values = jnp.einsum(
        "hqk,qhd->khd", weights_low, grad_attended, preferred_element_type=f32
    ).astype(bf16)
    grad_values_float = grad_values.astype(f32)
    grad_projected = (
        (value_gates[..., None] * grad_values_float[:, :, None, :])
        .reshape(seq_len, -1)
        .astype(bf16)
    )
    grad_value_gates = jnp.sum(grad_values_float[:, :, None, :] * projected, axis=-1)
    value_select = (
        jnp.where(value_pick, grad_value_gates * value_sig * (1.0 - value_sig), 0.0)
        .reshape(seq_len, -1)
        .astype(bf16)
    )
    value_local = jnp.einsum("td,tc->dc", layer_input, grad_projected, preferred_element_type=f32)
    query_local = jnp.einsum("td,tc->dc", act_att, grad_queries, preferred_element_type=f32)
    key_local = jnp.einsum("td,tc->dc", act_att, grad_keys, preferred_element_type=f32)
    value_selector_local = jnp.einsum(
        "td,tc->dc", act_att, value_select, preferred_element_type=f32
    )
    output_selector_local = jnp.einsum("td,tc->dc", act_att, out_select, preferred_element_type=f32)
    grad_norm_att = jnp.einsum("tc,dc->td", grad_queries, query_weight, preferred_element_type=f32)
    grad_norm_att = grad_norm_att + jnp.einsum(
        "tc,dc->td", grad_keys, key_weight, preferred_element_type=f32
    )
    grad_norm_att = grad_norm_att + jnp.einsum(
        "tc,dc->td", value_select, value_selector, preferred_element_type=f32
    )
    grad_norm_att = grad_norm_att + jnp.einsum(
        "tc,dc->td", out_select, output_selector, preferred_element_type=f32
    )
    att_gain_local = jnp.sum(grad_norm_att * hat_att, axis=0)
    att_shift_local = jnp.sum(grad_norm_att, axis=0)
    input_grad = grad_residual + jnp.einsum(
        "tc,dc->td", grad_projected, value_weight, preferred_element_type=f32
    )
    input_grad = input_grad + norm_backward(grad_norm_att, hat_att, inv_att, att_gain)
    reduced = (
        lax.psum_scatter(att_gain_local, ("dp", "expert"), scatter_dimension=0, tiled=True),
        lax.psum_scatter(att_shift_local, ("dp", "expert"), scatter_dimension=0, tiled=True),
        lax.psum_scatter(query_local, ("dp", "expert"), scatter_dimension=0, tiled=True),
        lax.psum_scatter(key_local, ("dp", "expert"), scatter_dimension=0, tiled=True),
        lax.psum_scatter(value_local, ("dp", "expert"), scatter_dimension=0, tiled=True),
        lax.psum_scatter(output_local, ("dp", "expert"), scatter_dimension=1, tiled=True),
        lax.psum_scatter(value_selector_local, ("dp", "expert"), scatter_dimension=0, tiled=True),
        lax.psum_scatter(output_selector_local, ("dp", "expert"), scatter_dimension=0, tiled=True),
        lax.psum_scatter(ffn_gain_local, ("dp", "expert"), scatter_dimension=0, tiled=True),
        lax.psum_scatter(ffn_shift_local, ("dp", "expert"), scatter_dimension=0, tiled=True),
        lax.psum_scatter(ffn_selector_local, ("dp", "expert"), scatter_dimension=0, tiled=True),
    )
    up_grad, down_grad = (
        lax.psum_scatter(
            up_local.astype(jnp.bfloat16), "dp", scatter_dimension=1, tiled=True
        ).astype(jnp.float32),
        lax.psum_scatter(
            down_local.astype(jnp.bfloat16), "dp", scatter_dimension=2, tiled=True
        ).astype(jnp.float32),
    )
    return (
        output,
        input_grad,
        reduced[0],
        reduced[1],
        reduced[2],
        reduced[3],
        reduced[4],
        reduced[5],
        reduced[6],
        reduced[7],
        reduced[8],
        reduced[9],
        reduced[10],
        up_grad,
        down_grad,
        counts_all[:EXPERTS],
    )


def mm(a, b, ca, cb):
    return lax.dot_general(a, b, (((ca,), (cb,)), ((), ())), preferred_element_type=f32)


def iota(shape, dim):
    return lax.broadcasted_iota(jnp.int32, shape, dim)


def centre(values):
    centred = values - jnp.mean(values, axis=-1, keepdims=True)
    inverse = lax.rsqrt(jnp.mean(centred * centred, axis=-1, keepdims=True) + EPSILON)
    return centred * inverse, inverse


def centre_back(upstream, normed, inverse, gain):
    scaled = upstream * gain
    mean = jnp.mean(scaled, axis=-1, keepdims=True)
    slope = jnp.mean(scaled * normed, axis=-1, keepdims=True)
    return inverse * (scaled - mean - normed * slope)


def device_of(ids, s, x):
    return 2 * s + (ids[1] + x - 2 * ids[1] * x)


SHORT = pl.CostEstimate(flops=1, bytes_accessed=1, transcendentals=0)


LONG = pl.CostEstimate(flops=1, bytes_accessed=1 << 28, transcendentals=0)


def call(body, outs, args, scratch=(), smem=(), name=None, cost=SHORT):
    return pl.pallas_call(
        body,
        out_shape=[jax.ShapeDtypeStruct(s, d) for s, d in outs],
        in_specs=[pl.BlockSpec(memory_space=pltpu.SMEM)] * len(smem)
        + [pl.BlockSpec(memory_space=pltpu.VMEM)] * len(args),
        out_specs=[pl.BlockSpec(memory_space=pltpu.VMEM)] * len(outs),
        scratch_shapes=list(scratch),
        compiler_params=pltpu.CompilerParams(vmem_limit_bytes=VMEM_LIMIT),
        cost_estimate=cost,
        name=name,
    )(*smem, *args)


def forward_body(
    length, li, vroutes, oroutes, froutes, att_gain, att_shift, wq, wk, wv, wo, vsel, osel,
    ffn_gain, ffn_shift, fsel,
    h1_o, xpack_o, q_o, k_o, v_o, p_o, a_o, o_o, gt_o, a1_o, a2_o, mixed,
):
    T, D = li.shape
    heads = vroutes.shape[0]
    dh = wq.shape[1] // heads
    ea = wv.shape[1] // (heads * dh)
    he = heads * ea
    top = froutes.shape[0]
    routes = [vroutes[h] for h in range(heads)] + [oroutes[h] for h in range(heads)] + [froutes[...]]
    routes = jnp.concatenate([r.astype(f32) for r in routes], axis=0)
    routes = jnp.concatenate([routes, jnp.zeros((128 - routes.shape[0], T), f32)], axis=0).T.astype(jnp.int32)
    scaling = 1.0 / math.sqrt(dh)
    x = li[...].astype(f32)
    hat, inv = centre(x)
    mean = jnp.mean(x, axis=-1, keepdims=True)
    a1 = (hat * att_gain[...] + att_shift[...]).astype(bf16)
    a1_o[...] = a1
    logits = jnp.concatenate(
        [mm(a1, vsel[...], 1, 1), mm(a1, osel[...], 1, 1), jnp.zeros((T, 128 - 2 * he), f32)], axis=1
    )
    lane = iota((T, 128), 1)
    chosen = jnp.zeros((T, 128), jnp.bool_)
    for j in range(2 * heads):
        h = j // 2
        chosen |= lane == routes[:, j : j + 1] + h * ea
        chosen |= lane == routes[:, 2 * heads + j : 2 * heads + j + 1] + (he + h * ea)
    gt = jnp.where(chosen, jax.nn.sigmoid(logits), 0.0)
    gt_o[...] = jnp.where(lane == 2 * he, mean, jnp.where(lane == 2 * he + 1, inv, gt))
    q = mm(a1, wq[...], 1, 0).astype(bf16)
    k = mm(a1, wk[...], 1, 0).astype(bf16)
    q_o[...] = q
    k_o[...] = k
    n_live = length[0]
    row, col = iota((T, T), 0), iota((T, T), 1)
    causal = (col <= row) & (col < n_live)
    width = ea * dh
    for h in range(heads):
        proj = mm(li[...], wv[:, h * width : (h + 1) * width], 1, 0)
        p_o[:, h * width : (h + 1) * width] = proj
        v = jnp.zeros((T, dh), f32)
        for e in range(ea):
            v += gt[:, h * ea + e : h * ea + e + 1] * proj[:, e * dh : (e + 1) * dh]
        v = v.astype(bf16)
        v_o[:, h * dh : (h + 1) * dh] = v
        s = mm(q[:, h * dh : (h + 1) * dh], k[:, h * dh : (h + 1) * dh], 1, 1) * scaling
        s = jnp.where(causal, s, NEGATIVE)
        ex = jnp.exp(s - jnp.max(s, axis=-1, keepdims=True))
        a = ex / jnp.sum(ex, axis=-1, keepdims=True)
        a_o[h] = a
        o = mm(a.astype(bf16), v, 1, 0)
        o_o[:, h * dh : (h + 1) * dh] = o
        for e in range(ea):
            c = he + h * ea + e
            mixed[:, (h * ea + e) * dh : (h * ea + e + 1) * dh] = (gt[:, c : c + 1] * o).astype(bf16)
    h1 = x + mm(mixed[...], wo[...], 1, 0)
    h1_o[...] = h1
    hat2, _ = centre(h1)
    a2 = (hat2 * ffn_gain[...] + ffn_shift[...]).astype(bf16)
    a2_o[...] = a2
    sig = jax.nn.sigmoid(mm(a2, fsel[...], 1, 1))
    wide = iota(sig.shape, 1)
    g = jnp.zeros((T, 128), f32)
    for i in range(top):
        c = 4 * heads + i
        one = jnp.sum(jnp.where(wide == routes[:, c : c + 1], sig, 0.0), axis=-1, keepdims=True)
        g = jnp.where(lane == i, one, g)
    g = g.T[:16]
    hi = g.astype(bf16)
    low = h1.astype(bf16)
    for s in range(xpack_o.shape[0]):
        xpack_o[s, :T] = low
        xpack_o[s, T:] = jnp.zeros((16, D), bf16)
        xpack_o[s, T:, :128] = hi
        xpack_o[s, T:, 128:256] = (g - hi.astype(f32)).astype(bf16)


def take_slices(v, n_p, S, e):
    D = v.shape[1]
    w = D // (n_p * S)
    return jnp.concatenate(
        [v[:, (b * S + e) * w : (b * S + e + 1) * w] for b in range(n_p)], axis=1
    )


def views(mine, theirs):
    return [r.at[s] for s in range(mine.shape[0]) for r in (mine, theirs)]


def views_from(ids, mine, theirs):
    return [r.at[ids[0] ^ s] for s in range(mine.shape[0]) for r in (mine, theirs)]


def early_body(n_p, S, ids, li, a1, a2, o, gt, *rest):
    msgs, scratch = rest
    msgs = [msgs.at[s] for s in range(S // 2)]
    hd = o.shape[1]
    for e in range(S):
        for i, v in enumerate((li, a1, a2)):
            scratch[e, :, i * 128 : (i + 1) * 128] = take_slices(v[...].astype(f32), n_p, S, e).astype(bf16)
    hi = gt[...].astype(bf16).astype(f32)
    both = (hi + pltpu.roll(gt[...] - hi, 64, 1)).astype(bf16)
    for s, m in enumerate(msgs):
        m[:, :hd] = o[...].astype(bf16)
        m[:, hd : hd + 128] = both
        m[:, hd + 128 : hd + 512] = scratch[device_of(ids, s, 1)]
        m[:, hd + 512 : hd + 896] = scratch[device_of(ids, s, 0)]


def codes_body(S, ids, *refs):
    c, (code_o, cnt_o) = views_from(ids, *refs[:2]), refs[2:]
    ep = cnt_o.shape[1]
    T = c[0].shape[0] - 16
    strict = (iota((T, T), 0) < iota((T, T), 1)).astype(f32).astype(bf16)
    e_id = iota((ep, T), 0).astype(f32)
    cnt = jnp.zeros((8, ep), f32)
    start = ids[3].astype(f32)
    for k in range(S):
        r = c[k][T:, :T].astype(f32) * 32.0 + c[k][T:, T : 2 * T].astype(f32) - start
        mask = jnp.zeros((ep, T), f32)
        for i in range(r.shape[0]):
            mask = jnp.where(r[i : i + 1] == e_id, 1.0, mask)
        low = mask.astype(bf16)
        rank = mm(low, strict, 1, 0) + (MOST * (k % 2))
        cnt += mm(jnp.ones((8, T), bf16), low, 1, 1)
        code_o[k // 2, :, (k % 2) * T : (k % 2 + 1) * T] = jnp.where(mask > 0.5, rank, -1.0).astype(bf16)
    cnt_o[...] = cnt


def columns_body(n_p, order, ids, x, *refs):
    outs = refs[-n_p:]
    T = x.shape[1] - 16
    wide = outs[0].shape[2]
    for k in range(x.shape[0]):
        rows = x.at[ids[0] ^ k if order else k]
        for s in range(n_p):
            at = pl.multiple_of((ids[2] ^ s) * wide, 128)
            outs[s][k, :T, :] = rows[:T, pl.ds(at, wide)]
    if len(refs) > n_p:
        for s in range(n_p):
            outs[s][:, T:, :] = refs[0][...]


def gelu_both(u):
    t = jnp.tanh(GELU_A * (u + GELU_B * u * u * u))
    value = 0.5 * u * (1.0 + t)
    slope = 0.5 * (1.0 + t) + 0.5 * u * (1.0 - t * t) * (GELU_A * (1.0 + 3.0 * GELU_B * u * u))
    return value, slope


def experts_body(S, eb, ids, *refs):
    x, c = views(*refs[:2]), views_from(ids, *refs[2:4])
    code, up, down, dx0, dx1, gy0, gy1, gr_o, du_o, ct, gts, dl, ps, xs, cs, gys, dxs = refs[4:]
    step = pl.program_id(0)
    pairs = S // 2
    R = 2 * MOST
    T = x[0].shape[0] - 16
    D = x[0].shape[1]
    ep = ct.shape[1]
    rows = pairs * R
    H = up.shape[2]

    @pl.when(step == 0)
    def _():
        e_id = iota((ep, T), 0).astype(f32)
        start = ids[3].astype(f32)
        dl[...] = jnp.zeros_like(dl)
        for pr in range(pairs):
            ct[pr] = code[pr].astype(f32)
        for k in range(S):
            r = c[k][T:, :T].astype(f32) * 32.0 + c[k][T:, T : 2 * T].astype(f32) - start
            g = x[k][T:, :T].astype(f32) + x[k][T:, T : 2 * T].astype(f32)
            dense = jnp.zeros((ep, T), f32)
            for i in range(r.shape[0]):
                dense = jnp.where(r[i : i + 1] == e_id, g[i : i + 1], dense)
            gts[:, k * T : (k + 1) * T] = dense

    slot = iota((R, 2 * T), 0).astype(f32)
    g_slot = [[None] * pairs for _ in range(eb)]
    onehot = [[None] * pairs for _ in range(eb)]
    for pr in range(pairs):
        blocks = []
        for j in range(eb):
            e = step * eb + j
            hot = jnp.where(ct[pr, pl.ds(e, 1), :] == slot, 1.0, 0.0)
            onehot[j][pr] = hot
            g_slot[j][pr] = jnp.sum(
                hot * gts[pl.ds(e, 1), pr * 2 * T : (pr + 1) * 2 * T], axis=-1, keepdims=True
            )
            blocks.append(hot.astype(bf16))
        block = jnp.concatenate(blocks, axis=0)
        ps[pr, pl.ds(pl.multiple_of(step * (eb * R), R), eb * R), :] = block
        for src, dst in ((x, xs), (c, cs)):
            both = jnp.concatenate([src[2 * pr][:T], src[2 * pr + 1][:T]], axis=0)
            got = mm(block, both, 1, 0).astype(bf16)
            for j in range(eb):
                dst[j * rows + pr * R : j * rows + (pr + 1) * R, :] = got[j * R : (j + 1) * R]
    for first in range(0, eb, 2):
        js = list(range(first, min(first + 2, eb)))
        n = len(js)
        span = slice(first * rows, (first + n) * rows)
        g = jnp.concatenate([p for j in js for p in g_slot[j]], axis=0)
        cj = cs[span, :].astype(f32)
        ups = jnp.concatenate([up[j] for j in js], axis=1)
        downs = jnp.concatenate([down[j] for j in js], axis=0)

        def own(v):
            return jnp.concatenate([v[i * rows : (i + 1) * rows, i * H : (i + 1) * H] for i in range(n)], axis=0)

        def spread_out(v):
            if n == 1:
                return v
            zero = jnp.zeros((rows, H), v.dtype)
            return jnp.concatenate(
                [
                    jnp.concatenate([v[i * rows : (i + 1) * rows] if i == b else zero for b in range(n)], axis=1)
                    for i in range(n)
                ],
                axis=0,
            )

        u = own(mm(xs[span, :], ups, 1, 0))
        value, slope = gelu_both(u)
        r = value.astype(bf16)
        y = mm(spread_out(r), downs, 1, 0).astype(bf16).astype(f32)
        dgate = jnp.sum(cj * y, axis=-1, keepdims=True)
        gy = (g * y).astype(bf16)
        dr = own(mm((g * cj).astype(bf16), downs, 1, 1))
        du = (dr * slope).astype(bf16)
        dx = mm(spread_out(du), ups, 1, 1).astype(bf16)
        gr = (g * r.astype(f32)).astype(bf16)
        dlog = dgate * g * (1.0 - g)
        for i, j in enumerate(js):
            e = step * eb + j
            gr_o[j] = gr[i * rows : (i + 1) * rows]
            du_o[j] = du[i * rows : (i + 1) * rows]
            for pr in range(pairs):
                at = pl.ds(pl.multiple_of(step * (eb * R) + j * R, R), R)
                cut = slice(i * rows + pr * R, i * rows + (pr + 1) * R)
                gys[pr, at, :] = gy[cut]
                dxs[pr, at, :] = dx[cut]
                dl[pl.ds(e, 1), pr * 2 * T : (pr + 1) * 2 * T] = jnp.sum(
                    onehot[j][pr] * dlog[cut], axis=0, keepdims=True
                )

    @pl.when(step == pl.num_programs(0) - 1)
    def _():
        for pr in range(pairs):
            for src, d0, d1 in ((dxs, dx0, dx1), (gys, gy0, gy1)):
                got = mm(ps[pr], src[pr], 0, 0).astype(bf16)
                d0[pr, :T] = got[:T]
                d1[pr, :T] = got[T:]
            for x_i, d in ((0, dx0), (1, dx1)):
                k = 2 * pr + x_i
                part = dl[:, k * T : (k + 1) * T].astype(bf16)
                d[pr, T:] = jnp.zeros((16, D), bf16)
                for b in range(ep // 16):
                    d[pr, T:, b * T : (b + 1) * T] = part[16 * b : 16 * b + 16]


def join_body(T, mine, recv, out):
    half = mine.shape[2] // 2
    for s in range(mine.shape[0]):
        out[s, :T] = (mine[s, :T].astype(f32) + recv[s, :T].astype(f32)).astype(bf16)
        if mine.shape[1] > T:
            out[s, T:, :half] = mine[s, T:, :half]
            out[s, T:, half:] = recv[s, T:, :half]


def join_apart_body(nz, ids, mine, recv, *outs):
    for s in range(nz):
        outs[s][...] = (mine[ids[0] ^ s].astype(f32) + recv[ids[0] ^ s].astype(f32)).astype(bf16)


def ffn_back_body(n_p, S, nz, ids, parts, h1, c, fsel, gain, froutes, cnt, dh1_o, db_o, mid_o, dlt, sl):
    T, D = h1.shape
    ep = dlt.shape[0] // S
    half = D // 2
    dxs = parts[0, :T].astype(f32)
    for s in range(1, nz):
        dxs += parts[s, :T].astype(f32)
    for s in range(nz):
        for x in range(2):
            for b in range(ep // 16):
                at = pl.multiple_of(device_of(ids, s, x) * ep + 16 * b, 16)
                dlt[pl.ds(at, 16), :] = parts[s, T:, x * half + b * T : x * half + (b + 1) * T].astype(f32)
    dl = dlt[...].T
    da2 = mm(dl.astype(bf16), fsel[...], 1, 0)
    hat, inv = centre(h1[...])
    dh1 = c[...].astype(f32) + dxs + centre_back(da2, hat, inv, gain[...])
    dh1_o[...] = dh1
    db = dh1.astype(bf16)
    db_o[...] = db
    low = db.astype(f32)
    for e in range(S):
        sl[e] = take_slices(low, n_p, S, e).astype(bf16)
    slot = iota(dlt.shape, 0)
    few = [
        jnp.sum(jnp.where(slot == froutes[i : i + 1, :], dlt[...], 0.0), axis=0, keepdims=True)
        for i in range(froutes.shape[0])
    ]
    few = jnp.concatenate(few, axis=0).astype(bf16)
    hi = cnt[...].astype(bf16)
    lo = (cnt[...] - hi.astype(f32)).astype(bf16)
    vectors = []
    for v in (jnp.sum(da2 * hat, axis=0, keepdims=True), jnp.sum(da2, axis=0, keepdims=True)):
        high = v.astype(bf16).astype(f32)
        for part in (high, v - high):
            vectors += [part[:, b * 256 : (b + 1) * 256] for b in range(D // 256)]
    vectors = jnp.concatenate(vectors, axis=0).astype(bf16)
    for s in range(nz):
        m = mid_o.at[s]
        m[:T, :128] = sl[device_of(ids, s, 1)]
        m[:T, 128:] = sl[device_of(ids, s, 0)]
        m[T : T + 16, :T] = few
        m[T : T + 16, T:] = jnp.zeros((16, 256 - T), bf16)
        m[T : T + 16, T : T + ep] = jnp.concatenate([hi, lo], axis=0)
        m[T + 16 :] = vectors


def attention_back_body(db, wo, gt, o, q, k, v, a, p, late_o, dp_o):
    T, D = db.shape
    heads = a.shape[0]
    dh = q.shape[1] // heads
    ea = p.shape[1] // (heads * dh)
    he, hd = heads * ea, heads * dh
    width = ea * dh
    scaling = 1.0 / math.sqrt(dh)
    lane = iota((T, 128), 1)
    dgates = jnp.zeros((T, 128), f32)
    gates = gt[...]
    for h in range(heads):
        hs = slice(h * dh, (h + 1) * dh)
        dz = mm(db[...], wo[h * width : (h + 1) * width, :], 1, 1)
        oh = o[:, hs]
        do = jnp.zeros((T, dh), f32)
        for e in range(ea):
            c = he + h * ea + e
            piece = dz[:, e * dh : (e + 1) * dh]
            do += gates[:, c : c + 1] * piece
            dgates = jnp.where(lane == c, jnp.sum(piece * oh, axis=-1, keepdims=True), dgates)
        do = do.astype(bf16)
        ah = a[h]
        dv = mm(ah.astype(bf16), do, 0, 0).astype(bf16)
        late_o[0, :, hs] = dv
        dvf = dv.astype(f32)
        for e in range(ea):
            c = h * ea + e
            es = slice(c * dh, (c + 1) * dh)
            dp_o[:, es] = (gates[:, c : c + 1] * dvf).astype(bf16)
            dgates = jnp.where(lane == c, jnp.sum(dvf * p[:, es], axis=-1, keepdims=True), dgates)
        da = mm(do, v[:, hs], 1, 1)
        ds = (ah * (da - jnp.sum(ah * da, axis=-1, keepdims=True))).astype(bf16)
        late_o[0, :, hd + h * dh : hd + (h + 1) * dh] = (mm(ds, k[:, hs], 1, 0) * scaling).astype(bf16)
        late_o[0, :, 2 * hd + h * dh : 2 * hd + (h + 1) * dh] = (mm(ds, q[:, hs], 0, 0) * scaling).astype(bf16)
    late_o[0, :, 3 * hd :] = (dgates * gates * (1.0 - gates)).astype(bf16)
    for s in range(1, late_o.shape[0]):
        late_o[s] = late_o[0]


def input_back_body(late, dp, wq, wk, wv, selw, li, gain, dh1, ig_o):
    hd = wq.shape[1]
    da1 = mm(late[0, :, hd : 2 * hd], wq[...], 1, 1)
    da1 += mm(late[0, :, 2 * hd : 3 * hd], wk[...], 1, 1)
    da1 += mm(late[0, :, 3 * hd :], selw[...], 1, 1)
    hat, inv = centre(li[...].astype(f32))
    ig_o[...] = dh1[...] + mm(dp[...], wv[...], 1, 1) + centre_back(da1, hat, inv, gain[...])


def spread(values, gates, lo, heads, ea, dh):
    return jnp.concatenate(
        [
            (gates[:, lo + h * ea + e : lo + h * ea + e + 1] * values[:, h * dh : (h + 1) * dh]).astype(bf16)
            for h in range(heads)
            for e in range(ea)
        ],
        axis=1,
    )


def spread_body(S, heads, ea, ids, e0, e1, c0, c1, z_o, a2_o, lia1_o, gates_o, routes_o):
    early, cpack = views(e0, e1), views_from(ids, c0, c1)
    T = early[0].shape[0]
    hd = early[0].shape[1] - 896
    for k in range(S):
        ts = slice(k * T, (k + 1) * T)
        m = early[k]
        both = m[:, hd : hd + 128].astype(f32)
        gates = both + pltpu.roll(both, 64, 1)
        gates_o[ts, :] = gates
        z_o[ts, :] = spread(m[:, :hd].astype(f32), gates, heads * ea, heads, ea, hd // heads)
        at = hd + 512 if k % 2 == 0 else hd + 128
        lia1_o[ts, :] = m[:, at : at + 256]
        a2_o[ts, :] = m[:, at + 256 : at + 384]
        routes_o[k * 16 : (k + 1) * 16, :] = (
            cpack[k][T:, :T].astype(f32) * 32.0 + cpack[k][T:, T : 2 * T].astype(f32)
        )


def out_rows(acc, outs, ids, w):
    for s, ref in enumerate(outs):
        plane = ids[2] ^ s
        ref[:, : acc.shape[1]] = acc[pl.ds(pl.multiple_of(plane * w, 8), w), :].astype(ref.dtype)


def out_grads_body(S, n_p, w, ids, m0, m1, z, a2, routes, *refs):
    mid, outs = views(m0, m1), refs[:n_p]
    acc, lhs, dlt, cnt = refs[n_p:]
    T = z.shape[0] // S
    EP = dlt.shape[0]
    e_id = iota((EP, T), 0).astype(f32)
    norms = jnp.zeros((16, 256), f32)
    for k in range(S):
        n = mid[k]
        ts = slice(k * T, (k + 1) * T)
        at = 128 if k % 2 == 0 else 0
        lhs[ts, :] = n[:T, at : at + 128]
        few = n[T : T + 16, :T].astype(f32)
        route = routes[k * 16 : (k + 1) * 16, :]
        dense = jnp.zeros((EP, T), f32)
        for i in range(16):
            dense = jnp.where(route[i : i + 1] == e_id, few[i : i + 1], dense)
        dlt[:, ts] = dense.astype(bf16)
        tally = n[T : T + 16, T:].astype(f32)
        at = device_of(ids, k // 2, k % 2)
        cnt[pl.ds(at, 1), :] = tally[:1]
        cnt[pl.ds(at + 8, 1), :] = tally[8:9]
        norms += n[T + 16 :].astype(f32)
    wide = z.shape[1]
    acc[:, :wide] = mm(lhs[...], z[...], 0, 0)
    acc[:, wide:] = mm(dlt[...], a2[...], 1, 0).T
    out_rows(acc, outs, ids, w)
    norms = pltpu.roll(norms, lax.rem(256 - (2 * ids[0] + ids[1]) * w, 256), 1)
    norms = jnp.concatenate([norms[0:4] + norms[4:8], norms[8:12] + norms[12:16]], axis=0)
    extra = jnp.concatenate([cnt[...], norms[:, :128], jnp.zeros((w - 24, 128), f32)], axis=0)
    for ref in outs:
        ref[:, acc.shape[1] :] = extra.astype(ref.dtype)


def in_grads_body(S, n_p, heads, ea, w, ids, l0, l1, lia1, gates, wq, wk, selw, *refs):
    late, outs = views(l0, l1), refs[:n_p]
    acc, rhs, qk, wsl = refs[n_p:]
    T = late[0].shape[0]
    hd = wq.shape[1]
    for k in range(S):
        ts = slice(k * T, (k + 1) * T)
        n = late[k]
        rhs[ts, :] = spread(n[:, :hd].astype(f32), gates[ts, :], 0, heads, ea, hd // heads)
        qk[ts, :] = n[:, hd:]
    wide = rhs.shape[1]
    acc[:, :wide] = mm(lia1[:, :128], rhs[...], 0, 0)
    acc[:, wide:] = mm(lia1[:, 128:], qk[...], 0, 0)
    D = wq.shape[0]
    for b in range(n_p):
        at = pl.ds(pl.multiple_of(b * (D // n_p) + (2 * ids[0] + ids[1]) * w, 16), w)
        bs = slice(b * w, (b + 1) * w)
        wsl[bs, :hd] = wq[at, :]
        wsl[bs, hd : 2 * hd] = wk[at, :]
        wsl[bs, 2 * hd :] = selw[at, :]
    da1 = mm(qk[...], wsl[...], 1, 1)
    he2 = 2 * heads * ea
    hat = (lia1[:, :128].astype(f32) - gates[:, he2 : he2 + 1]) * gates[:, he2 + 1 : he2 + 2]
    gain, shift = jnp.sum(da1 * hat, axis=0, keepdims=True), jnp.sum(da1, axis=0, keepdims=True)
    for b in range(n_p):
        bs = slice(b * w, (b + 1) * w)
        rows = jnp.concatenate([gain[:, bs], shift[:, bs], jnp.zeros((6, w), f32)], axis=0)
        rows = jnp.concatenate([jnp.zeros((8, 64), f32), rows, jnp.zeros((8, 64 - w), f32)], axis=1)
        acc[b * w : b * w + 8, wide + 2 * hd :] += rows
    out_rows(acc, outs, ids, w)


def last_a_body(n_p, S, w, el, ids, *refs):
    parts, (og_o, fg_o, gain_o, shift_o, counts_o, rows) = refs[:n_p], refs[n_p:]
    total = parts[0][...]
    for m in parts[1:]:
        total += m[...].astype(f32)
    wide = og_o.shape[1]
    og_o[...] = total[:w, :wide]
    ep = (total.shape[1] - 128 - wide) // S
    sel = total[:, wide:]
    fg_o[...] = jnp.concatenate([sel[:, e * ep : e * ep + el] for e in range(S)], axis=1)[:, : fg_o.shape[1]]
    extra = total[:, wide + S * ep :]
    rows[...] = extra[16:24]
    gain_o[...] = rows[pl.ds(ids[2], 1), :w]
    shift_o[...] = rows[pl.ds(ids[2] + n_p, 1), :w]
    cnt = extra[0:8] + extra[8:16]
    counts_o[...] = jnp.concatenate([cnt[e : e + 1, :el] for e in range(S)], axis=1)[:, : counts_o.shape[1]]


def last_b_body(n_p, w, hd, he, *refs):
    parts, (vg_o, qg_o, kg_o, vs_o, os_o, gain_o, shift_o) = refs[:n_p], refs[n_p:]
    total = parts[0][...]
    for m in parts[1:]:
        total += m[...].astype(f32)
    wide = vg_o.shape[1]
    vg_o[...] = total[:w, :wide]
    qg_o[...] = total[:w, wide : wide + hd]
    kg_o[...] = total[:w, wide + hd : wide + 2 * hd]
    sel = total[:w, wide + 2 * hd :].T
    vs_o[...] = sel[:he]
    os_o[...] = sel[he : 2 * he]
    gain_o[...] = total[0:1, wide + 2 * hd + 64 : wide + 2 * hd + 64 + w]
    shift_o[...] = total[1:2, wide + 2 * hd + 64 : wide + 2 * hd + 64 + w]


def expert_grads_body(n_p, eb, first, xm, xo, cm, co, *refs):
    gr_in, du_in = refs[:n_p], refs[n_p : 2 * n_p]
    up_o, down_o, ct, got = refs[-4:]
    start = pl.program_id(0)
    step = start + first
    _, pairs, T, wide = cm.shape
    T2 = 2 * T
    R = 2 * MOST
    rows = pairs * R

    @pl.when(start == 0)
    def _():
        for s in range(n_p):
            for pr in range(pairs):
                ct[s * pairs + pr] = xm[s, pr, T:, :].astype(f32)

    slot = iota((R, T2), 0).astype(f32)
    for s in range(n_p):
        for pr in range(pairs):
            block = jnp.concatenate(
                [
                    jnp.where(ct[s * pairs + pr, pl.ds(step * eb + j, 1), :] == slot, 1.0, 0.0).astype(bf16)
                    for j in range(eb)
                ],
                axis=0,
            )
            both = jnp.concatenate(
                [jnp.concatenate([x[s, pr, :T], c[s, pr]], axis=1) for x, c in ((xm, cm), (xo, co))], axis=0
            )
            res = mm(block, both, 1, 0).astype(bf16)
            for j in range(eb):
                at = j * n_p * rows + s * rows + pr * R
                got[at : at + R, :] = res[j * R : (j + 1) * R]
    for j in range(eb):
        at = j * n_p * rows
        xj = got[at : at + n_p * rows, :wide]
        cj = got[at : at + n_p * rows, wide:]
        gr = jnp.concatenate([gr_in[s][j] for s in range(n_p)], axis=0)
        du = jnp.concatenate([du_in[s][j] for s in range(n_p)], axis=0)
        up_o[j] = mm(xj, du, 0, 0)
        down_o[j] = mm(gr, cj, 0, 0)


def after(values, *deps):
    return lax.optimization_barrier((values, deps))[0]


class Links:
    def __init__(self):
        self.n_e = lax.axis_size("expert")
        self.nz = self.n_e // 2
        self.n_p = lax.axis_size("dp")
        self.me = lax.axis_index("expert")
        self.z, self.c = self.me // 2, self.me % 2
        self.p = lax.axis_index("dp")

    def core(self, v):
        return lax.ppermute(v, "expert", [(e, e ^ 1) for e in range(self.n_e)])

    def chips(self, v):
        groups = [[2 * s + c for s in range(self.nz)] for c in range(2)]
        return lax.all_to_all(v, "expert", 0, 0, axis_index_groups=groups, tiled=True)

    def chip(self, v, s):
        return lax.ppermute(v, "expert", [(e, (e + 2 * s) % self.n_e) for e in range(self.n_e)])

    def plane(self, v, s):
        return lax.ppermute(v, "dp", [(p, p ^ s) for p in range(self.n_p)])

    def near(self, msgs):
        pairs = [[(e, e ^ (2 * s)) for e in range(self.n_e)] for s in range(self.nz)]
        return [msgs[0]] + [lax.ppermute(msgs[s], "expert", pairs[s]) for s in range(1, self.nz)]

    def relay(self, mine):
        return [mine, self.core(mine)]

    def planes_of(self, msgs):
        return [msgs[0]] + [self.plane(msgs[s], s) for s in range(1, self.n_p)]


def fast_path(
    layer_input, cotangent, lengths, value_routes, output_routes, ffn_routes, att_gain, att_shift,
    query_weight, key_weight, value_weight, output_weight, value_selector, output_selector,
    ffn_gain, ffn_shift, ffn_selector, up_weight, down_weight,
):
    L = Links()
    S, nz, n_p = L.n_e, L.nz, L.n_p
    pairs = S // 2
    T, D = layer_input.shape
    heads = value_routes.shape[1]
    dh = query_weight.shape[1] // heads
    ea = value_selector.shape[1] // heads
    hd, he, wide = heads * dh, heads * ea, heads * ea * dh
    el, _, H = up_weight.shape
    ep = -(-el // 16) * 16
    EP = ep * S
    w = D // (n_p * S)
    Dp = D // n_p
    R = 2 * MOST
    eb = max(d for d in (7, 4, 2, 1) if el % d == 0)

    ids = jnp.stack([L.z, L.c, L.p, L.me * ep]).astype(jnp.int32)
    raw = ffn_routes.T
    padded = (raw // el) * ep + raw % el

    rt = jnp.where(jnp.arange(T)[None, :] < lengths[0], padded, EP)
    tail = jnp.concatenate([rt // 32, rt % 32], axis=1).astype(bf16)
    cpack = jnp.concatenate([cotangent, jnp.pad(tail, ((0, 0), (0, D - 2 * T)))], axis=0)
    c_far = L.near([cpack] * nz)

    h1, xpack, q, k, v, proj, a, o, gt, a1, a2 = call(
        forward_body,
        [
            ((T, D), f32), ((nz, T + 16, D), bf16), ((T, hd), bf16), ((T, hd), bf16), ((T, hd), bf16),
            ((T, wide), f32), ((heads, T, T), f32), ((T, hd), f32), ((T, 128), f32),
            ((T, D), bf16), ((T, D), bf16),
        ],
        [
            layer_input, value_routes.transpose(1, 2, 0), output_routes.transpose(1, 2, 0), raw,
            att_gain[None], att_shift[None], query_weight, key_weight, value_weight, output_weight,
            value_selector.T, output_selector.T, ffn_gain[None], ffn_shift[None], ffn_selector.T,
        ],
        scratch=[pltpu.VMEM((T, wide), bf16)],
        smem=[lengths],
        name="forward",
    )
    x_far = L.chips(xpack)
    selectors = after((ffn_selector, value_selector, output_selector), xpack)
    fsel = jnp.pad(selectors[0].T, ((0, S * el - ffn_selector.shape[1]), (0, 0)))
    fsel = jnp.pad(fsel.reshape(S, el, D), ((0, 0), (0, ep - el), (0, 0))).reshape(EP, D)
    selw = jnp.pad(jnp.concatenate(selectors[1:], axis=1), ((0, 0), (0, 128 - 2 * he)))
    (early,) = call(
        partial(early_body, n_p, S),
        [((nz, T, hd + 896), bf16)],
        [layer_input, a1, a2, o, gt],
        scratch=[pltpu.VMEM((S, T, 384), bf16)],
        smem=[ids],
        name="early_slices",
    )
    c_msgs = L.relay(jnp.stack(after(c_far, early, fsel, selw)))
    ccols = call(
        partial(columns_body, n_p, True), [((nz, T, Dp), bf16)] * n_p, [after(c_msgs[0], c_msgs[1])], smem=[ids],
        name="cotangent_columns",
    )
    cc_all = [ccols[0], L.plane(ccols[1], 1), L.plane(ccols[2], 2)]
    code, cnt = call(
        partial(codes_body, S), [((pairs, ep, 2 * T), bf16), ((8, ep), f32)], after(c_msgs, ccols), smem=[ids],
        name="codes",
    )
    x_far = after(x_far, code, cc_all[1:])
    x_msgs = L.relay(x_far)
    xcols = call(
        partial(columns_body, n_p, False), [((nz, T + ep, Dp), bf16)] * n_p, [x_far, code],
        smem=[ids],
        name="token_columns",
    )
    xc_all = L.planes_of(xcols)
    early_far = L.chips(after(early, x_far))

    n_eb = el // eb
    whole = [pl.BlockSpec(memory_space=pltpu.VMEM)]
    dx0, dx1, gy0, gy1, gr, du = pl.pallas_call(
        partial(experts_body, S, eb),
        grid=(n_eb,),
        out_shape=[
            jax.ShapeDtypeStruct((pairs, T + 16, D), bf16), jax.ShapeDtypeStruct((pairs, T + 16, D), bf16),
            jax.ShapeDtypeStruct((pairs, T, D), bf16), jax.ShapeDtypeStruct((pairs, T, D), bf16),
            jax.ShapeDtypeStruct((el, pairs * R, H), bf16), jax.ShapeDtypeStruct((el, pairs * R, H), bf16),
        ],
        in_specs=[pl.BlockSpec(memory_space=pltpu.SMEM)]
        + whole * 5
        + [
            pl.BlockSpec((eb, D, H), lambda i: (i, 0, 0)),
            pl.BlockSpec((eb, H, D), lambda i: (i, 0, 0)),
        ],
        out_specs=whole * 4 + [pl.BlockSpec((eb, pairs * R, H), lambda i: (i, 0, 0))] * 2,
        scratch_shapes=[
            pltpu.VMEM((pairs, ep, 2 * T), f32), pltpu.VMEM((ep, S * T), f32), pltpu.VMEM((ep, S * T), f32),
            pltpu.VMEM((pairs, el * R, 2 * T), bf16),
            pltpu.VMEM((eb * pairs * R, D), bf16), pltpu.VMEM((eb * pairs * R, D), bf16),
            pltpu.VMEM((pairs, el * R, D), bf16), pltpu.VMEM((pairs, el * R, D), bf16),
        ],
        compiler_params=pltpu.CompilerParams(vmem_limit_bytes=VMEM_LIMIT),
        cost_estimate=SHORT,
        name="experts",
    )(after(ids, xcols), *x_msgs, *c_msgs, code, up_weight, down_weight)

    def join(mine, other, name):
        return call(partial(join_body, T), [(mine.shape, bf16)], [mine, L.core(other)], name=name)[0]

    def join_apart(mine, other, name):
        return call(
            partial(join_apart_body, nz), [(mine.shape[1:], bf16)] * nz, [mine, L.core(other)], smem=[ids], name=name
        )

    dx0, dx1, early_far, xc_all = lax.optimization_barrier((dx0, dx1, early_far, xc_all))
    dx_join = join(dx0, dx1, "join_dx")
    dx_parts = L.chips(dx_join)
    gr, du = after((gr, du), dx_join)
    gr1, du1 = L.plane(gr, 1), L.plane(du, 2)
    early_far, gy0, gy1, cc3, xc_all = after((early_far, gy0, gy1, ccols[3], xc_all), dx_join)
    xc_both = L.relay(jnp.stack(xc_all))
    cc_all += [L.plane(cc3, 3)]
    gy_join = join_apart(gy0, gy1, "join_out")
    z_all, a2_s, lia1, gates, routes = call(
        partial(spread_body, S, heads, ea),
        [
            ((S * T, wide), bf16), ((S * T, 128), bf16), ((S * T, 256), bf16), ((S * T, 128), f32),
            ((S * 16, T), f32),
        ],
        [*L.relay(early_far), *c_msgs],
        smem=[ids],
        cost=LONG,
        name="spread_tokens",
    )
    dx_parts, gr1, du1, z_all, gy_join, cc_all, xc_both = lax.optimization_barrier(
        (dx_parts, gr1, du1, z_all, gy_join, cc_all, xc_both)
    )
    cols_both = xc_both + L.relay(jnp.stack(cc_all))
    gr, du = after((gr, du), dx_parts)
    gr_all = [gr, gr1, L.plane(gr, 2)]
    du_all = [du, L.plane(du, 1), du1]

    dh1, db, mid = call(
        partial(ffn_back_body, n_p, S, nz),
        [((T, D), f32), ((T, D), bf16), ((nz, T + 32, 256), bf16)],
        [dx_parts, h1, cotangent, fsel, ffn_gain[None], padded, cnt],
        scratch=[pltpu.VMEM((EP, T), f32), pltpu.VMEM((S, T, 128), bf16)],
        smem=[ids],
        name="ffn_back",
    )
    mid_far = L.chips(mid)
    late, dp = call(
        attention_back_body,
        [((nz, T, 3 * hd + 128), bf16), ((T, wide), bf16)],
        [db, output_weight, gt, o, q, k, v, a, proj],
        cost=LONG,
        name="attention_back",
    )
    late = after(late, mid_far, gr_all[2], du_all[1])
    gr1, du1 = after((gr1, du1), late)
    gr_all += [L.plane(gr1, 2)]
    du_all += [L.plane(du1, 1)]
    late_far = L.chips(late)
    (input_grad,) = call(
        input_back_body,
        [((T, D), f32)],
        [late, dp, query_weight, key_weight, value_weight, selw, layer_input, att_gain[None], dh1],
        name="input_back",
    )
    mid_far = after(mid_far, input_grad)
    grads_a = call(
        partial(out_grads_body, S, n_p, w),
        [((w, wide + EP + 128), f32)] + [((w, wide + EP + 128), bf16)] * (n_p - 1),
        [*L.relay(mid_far), z_all, a2_s, routes],
        scratch=[
            pltpu.VMEM((128, wide + EP), f32), pltpu.VMEM((S * T, 128), bf16),
            pltpu.VMEM((EP, S * T), bf16), pltpu.VMEM((16, 128), f32),
        ],
        smem=[ids],
        name="out_grads",
    )
    a_parts = L.planes_of(grads_a)
    def expert_grads(first, last, args, so_far=()):
        n = len(args)
        return pl.pallas_call(
            partial(expert_grads_body, n_p, eb, first),
            grid=(last - first,),
            in_specs=whole * 4
            + [pl.BlockSpec((eb, pairs * R, H), lambda i: (i + first, 0, 0))] * (2 * n_p)
            + [pl.BlockSpec(memory_space=pl.ANY)] * len(so_far),
            out_specs=[
                pl.BlockSpec((eb, Dp, H), lambda i: (i + first, 0, 0)),
                pl.BlockSpec((eb, H, Dp), lambda i: (i + first, 0, 0)),
            ],
            scratch_shapes=[
                pltpu.VMEM((n_p * pairs, ep, 2 * T), f32),
                pltpu.VMEM((eb * n_p * pairs * R, 2 * Dp), bf16),
            ],
            out_shape=[jax.ShapeDtypeStruct((el, Dp, H), f32), jax.ShapeDtypeStruct((el, H, Dp), f32)],
            input_output_aliases={n + i: i for i in range(len(so_far))},
            compiler_params=pltpu.CompilerParams(vmem_limit_bytes=VMEM_LIMIT),
            cost_estimate=SHORT,
            name="expert_grads",
        )(*args, *so_far)

    cut = n_eb // 2
    grads_in = (*cols_both, *after(gr_all + du_all, grads_a))
    half = expert_grads(0, cut, grads_in)
    late_far, a_parts, half = lax.optimization_barrier((late_far, a_parts, half))
    gy_parts = L.near(after(gy_join, late_far))
    grads_b = call(
        partial(in_grads_body, S, n_p, heads, ea, w),
        [((w, wide + 2 * hd + 128), f32)] + [((w, wide + 2 * hd + 128), bf16)] * (n_p - 1),
        [*L.relay(late_far), lia1, gates, query_weight, key_weight, selw],
        scratch=[
            pltpu.VMEM((128, wide + 2 * hd + 128), f32), pltpu.VMEM((S * T, wide), bf16),
            pltpu.VMEM((S * T, 2 * hd + 128), bf16), pltpu.VMEM((128, 2 * hd + 128), bf16),
        ],
        smem=[ids],
        cost=LONG,
        name="in_grads",
    )
    b_parts = L.planes_of(grads_b)
    up_grad, down_grad = expert_grads(cut, n_eb, after(grads_in, grads_b), half)

    output_grad, fgrad, ffn_gain_grad, ffn_shift_grad, counts = call(
        partial(last_a_body, n_p, S, w, el),
        [((w, wide), f32), ((w, EXPERTS), f32), ((1, w), f32), ((1, w), f32), ((1, EXPERTS), f32)],
        after(a_parts, up_grad),
        scratch=[pltpu.VMEM((8, 128), f32)],
        smem=[ids],
        name="last_sum_a",
    )
    gy_parts, b_parts = after((gy_parts, b_parts), fgrad)
    output = (h1 + sum(m.astype(f32) for m in gy_parts)).astype(bf16)
    value_grad, query_grad, key_grad, vsel, osel, att_gain_grad, att_shift_grad = call(
        partial(last_b_body, n_p, w, hd, he),
        [
            ((w, wide), f32), ((w, hd), f32), ((w, hd), f32), ((he, w), f32), ((he, w), f32),
            ((1, w), f32), ((1, w), f32),
        ],
        after(b_parts, output),
        name="last_sum_b",
    )
    return (
        output, input_grad, att_gain_grad[0], att_shift_grad[0], query_grad, key_grad, value_grad,
        output_grad.T, vsel.T, osel.T, ffn_gain_grad[0], ffn_shift_grad[0], fgrad, up_grad, down_grad, counts[0],
    )


def solution(mesh):
    path = fast_path if mesh.shape["expert"] == 8 and mesh.shape["dp"] == 4 else general_path
    placed = (
        P(("dp", "expert"), None),
        P(("dp", "expert"), None),
        P(("dp", "expert")),
        P(("dp", "expert"), None, None),
        P(("dp", "expert"), None, None),
        P(("dp", "expert"), None),
        P(),
        P(),
        P(),
        P(),
        P(),
        P(),
        P(),
        P(),
        P(),
        P(),
        P(),
        P("expert", None, None),
        P("expert", None, None),
    )
    return jax.shard_map(
        path,
        mesh=mesh,
        in_specs=placed,
        out_specs=(
            P(("dp", "expert"), None),
            P(("dp", "expert"), None),
            P(("dp", "expert")),
            P(("dp", "expert")),
            P(("dp", "expert"), None),
            P(("dp", "expert"), None),
            P(("dp", "expert"), None),
            P(None, ("dp", "expert")),
            P(("dp", "expert"), None),
            P(("dp", "expert"), None),
            P(("dp", "expert")),
            P(("dp", "expert")),
            P(("dp", "expert"), None),
            P("expert", "dp", None),
            P("expert", None, "dp"),
            P(),
        ),
        check_vma=False,
    )
```

```python
import math
from functools import partial

import jax
import jax.numpy as jnp
from jax import lax
from jax.experimental import pallas as pl
from jax.experimental.pallas import tpu as pltpu
from jax.sharding import PartitionSpec as P

EXPERTS = 387
MOST = 8
EPSILON = 1e-05
NEGATIVE = -1e30
f32 = jnp.float32
bf16 = jnp.bfloat16
VMEM_LIMIT = 56 * 1024 * 1024
GELU_A = math.sqrt(2.0 / math.pi)
GELU_B = 0.044715


def layer_norm(values, scaling, offset):
    centred = values - jnp.mean(values, axis=-1, keepdims=True)
    inverse = lax.rsqrt(jnp.mean(centred * centred, axis=-1, keepdims=True) + EPSILON)
    normed = centred * inverse
    return (normed * scaling + offset, normed, inverse)


def norm_backward(upstream, normed, inverse, scaling):
    scaled = upstream * scaling
    centre_term = jnp.mean(scaled, axis=-1, keepdims=True)
    slope_term = jnp.mean(scaled * normed, axis=-1, keepdims=True)
    return inverse * (scaled - centre_term - normed * slope_term)


def gate_table(logits, routes, choices_count):
    chosen = jnp.any(routes[..., None] == jnp.arange(choices_count), axis=-2)
    sigmas = jax.nn.sigmoid(logits)
    return (chosen, sigmas, jnp.where(chosen, sigmas, 0.0))


def general_path(
    layer_input,
    cotangent,
    lengths,
    value_routes,
    output_routes,
    ffn_routes,
    att_gain,
    att_shift,
    query_weight,
    key_weight,
    value_weight,
    output_weight,
    value_selector,
    output_selector,
    ffn_gain,
    ffn_shift,
    ffn_selector,
    up_weight,
    down_weight,
):
    f32 = jnp.float32
    bf16 = jnp.bfloat16
    seq_len, width = layer_input.shape
    heads = value_routes.shape[1]
    head_dim = query_weight.shape[1] // heads
    att_experts = value_selector.shape[1] // heads
    top_ffn = ffn_routes.shape[1]
    exp_local = up_weight.shape[0]
    owners = lax.axis_size("expert")
    padded_experts = exp_local * owners
    capacity = MOST
    scaling = 1.0 / math.sqrt(head_dim)
    positions = jnp.arange(seq_len)
    is_valid = positions < lengths[0]
    validity = is_valid.astype(f32)
    input_float = layer_input.astype(f32)
    norm_att, hat_att, inv_att = layer_norm(input_float, att_gain, att_shift)
    act_att = norm_att.astype(bf16)
    queries = (
        jnp.dot(act_att, query_weight, preferred_element_type=f32)
        .astype(bf16)
        .reshape(seq_len, heads, head_dim)
    )
    key_rows = (
        jnp.dot(act_att, key_weight, preferred_element_type=f32)
        .astype(bf16)
        .reshape(seq_len, heads, head_dim)
    )
    projected = jnp.dot(layer_input, value_weight, preferred_element_type=f32).reshape(
        seq_len, heads, att_experts, head_dim
    )
    value_logits = jnp.dot(act_att, value_selector, preferred_element_type=f32).reshape(
        seq_len, heads, att_experts
    )
    output_logits = jnp.dot(act_att, output_selector, preferred_element_type=f32).reshape(
        seq_len, heads, att_experts
    )
    value_pick, value_sig, value_gates = gate_table(value_logits, value_routes, att_experts)
    out_pick, out_sig, out_gates = gate_table(output_logits, output_routes, att_experts)
    values_low = jnp.sum(value_gates[..., None] * projected, axis=2).astype(bf16)
    causal = (positions[None, :] <= positions[:, None]) & is_valid[None, :]
    raw_scores = jnp.einsum("qhd,khd->hqk", queries, key_rows, preferred_element_type=f32) * scaling
    scores = jnp.where(causal[None], raw_scores, NEGATIVE)
    row_peak = jnp.max(scores, axis=-1, keepdims=True)
    log_total = row_peak + jnp.log(jnp.sum(jnp.exp(scores - row_peak), axis=-1, keepdims=True))
    weights_p = jnp.exp(scores - log_total)
    weights_low = weights_p.astype(bf16)
    attended = jnp.einsum("hqk,khd->qhd", weights_low, values_low, preferred_element_type=f32)
    mixed_rows = (out_gates[..., None] * attended[:, :, None, :]).reshape(seq_len, -1).astype(bf16)
    residual = input_float + jnp.dot(mixed_rows, output_weight, preferred_element_type=f32)
    norm_ffn, hat_ffn, inv_ffn = layer_norm(residual, ffn_gain, ffn_shift)
    act_ffn = norm_ffn.astype(bf16)
    ffn_logits = jnp.dot(act_ffn, ffn_selector, preferred_element_type=f32)
    ffn_sig = jax.nn.sigmoid(jnp.take_along_axis(ffn_logits, ffn_routes, axis=1))
    gate_weights = ffn_sig * validity[:, None]
    entries = ffn_routes.reshape(-1)
    live_entry = jnp.broadcast_to(is_valid[:, None], ffn_routes.shape).reshape(-1)
    onehot_table = (
        (entries[:, None] == jnp.arange(padded_experts)[None, :]) & live_entry[:, None]
    ).astype(jnp.int32)
    before = jnp.cumsum(onehot_table, axis=0) - onehot_table
    slot_rank = jnp.sum(before * onehot_table, axis=1)
    counts_local = jnp.sum(onehot_table, axis=0).astype(f32)
    target = jnp.where(live_entry, entries * capacity + slot_rank, padded_experts * capacity)
    fetch = jnp.minimum(target, padded_experts * capacity - 1)
    total_slots = padded_experts * capacity
    residual_low = residual.astype(bf16)
    copies = jnp.broadcast_to(residual_low[:, None, :], (seq_len, top_ffn, width)).reshape(
        -1, width
    )
    send_rows = jnp.zeros((total_slots, width), bf16).at[target].set(copies, mode="drop")
    received = lax.all_to_all(
        send_rows.reshape(owners, exp_local * capacity, width),
        "expert",
        split_axis=0,
        concat_axis=0,
        tiled=True,
    )
    received = received.reshape(owners, exp_local, capacity, width)
    hidden_pre = jnp.einsum("semd,edh->semh", received, up_weight, preferred_element_type=f32)
    hidden_act = jax.nn.gelu(hidden_pre).astype(bf16)
    expert_out = jnp.einsum(
        "semh,ehd->semd", hidden_act, down_weight, preferred_element_type=f32
    ).astype(bf16)
    returned = lax.all_to_all(
        expert_out.reshape(owners, exp_local * capacity, width),
        "expert",
        split_axis=0,
        concat_axis=0,
        tiled=True,
    )
    gathered = (
        returned.reshape(total_slots, width)[fetch].reshape(seq_len, top_ffn, width).astype(f32)
    )
    final = residual + jnp.einsum("tk,tkd->td", gate_weights, gathered)
    output = final.astype(bf16)
    counts_all = lax.psum(counts_local, ("dp", "expert"))
    grad_final = cotangent.astype(f32)
    grad_rows = (gate_weights[:, :, None] * grad_final[:, None, :]).astype(bf16).reshape(-1, width)
    grad_gate = validity[:, None] * jnp.einsum("tkd,td->tk", gathered, grad_final)
    send_grad = jnp.zeros((total_slots, width), bf16).at[target].set(grad_rows, mode="drop")
    grad_recv = lax.all_to_all(
        send_grad.reshape(owners, exp_local * capacity, width),
        "expert",
        split_axis=0,
        concat_axis=0,
        tiled=True,
    )
    grad_recv = grad_recv.reshape(owners, exp_local, capacity, width)
    down_local = jnp.einsum("semh,semd->ehd", hidden_act, grad_recv, preferred_element_type=f32)
    grad_act = jnp.einsum("semd,ehd->semh", grad_recv, down_weight, preferred_element_type=f32)
    gelu_value, gelu_back = jax.vjp(jax.nn.gelu, hidden_pre)
    grad_pre = gelu_back(grad_act)[0].astype(bf16)
    up_local = jnp.einsum("semd,semh->edh", received, grad_pre, preferred_element_type=f32)
    grad_in = jnp.einsum("semh,edh->semd", grad_pre, up_weight, preferred_element_type=f32).astype(
        bf16
    )
    grad_back = lax.all_to_all(
        grad_in.reshape(owners, exp_local * capacity, width),
        "expert",
        split_axis=0,
        concat_axis=0,
        tiled=True,
    )
    grad_copies = (
        grad_back.reshape(total_slots, width)[fetch].reshape(seq_len, top_ffn, width).astype(f32)
    )
    grad_residual = grad_final + jnp.einsum("t,tkd->td", validity, grad_copies)
    sig_grad = grad_gate * ffn_sig * (1.0 - ffn_sig)
    dense_select = jnp.sum(
        jnp.where(ffn_routes[:, :, None] == jnp.arange(EXPERTS), sig_grad[:, :, None], 0.0), axis=1
    ).astype(bf16)
    ffn_selector_local = jnp.einsum("td,te->de", act_ffn, dense_select, preferred_element_type=f32)
    grad_norm_ffn = jnp.einsum("te,de->td", dense_select, ffn_selector, preferred_element_type=f32)
    ffn_gain_local = jnp.sum(grad_norm_ffn * hat_ffn, axis=0)
    ffn_shift_local = jnp.sum(grad_norm_ffn, axis=0)
    grad_residual = grad_residual + norm_backward(grad_norm_ffn, hat_ffn, inv_ffn, ffn_gain)
    grad_att_low = grad_residual.astype(bf16)
    output_local = jnp.einsum("tc,td->cd", mixed_rows, grad_att_low, preferred_element_type=f32)
    grad_mixed = jnp.einsum("td,cd->tc", grad_att_low, output_weight, preferred_element_type=f32)
    grad_mixed = grad_mixed.reshape(seq_len, heads, att_experts, head_dim)
    grad_attended = jnp.sum(out_gates[..., None] * grad_mixed, axis=2).astype(bf16)
    grad_out_gates = jnp.sum(grad_mixed * attended[:, :, None, :], axis=-1)
    out_select = (
        jnp.where(out_pick, grad_out_gates * out_sig * (1.0 - out_sig), 0.0)
        .reshape(seq_len, -1)
        .astype(bf16)
    )
    grad_weights = jnp.einsum("qhd,khd->hqk", grad_attended, values_low, preferred_element_type=f32)
    row_delta = jnp.sum(weights_p * grad_weights, axis=-1, keepdims=True)
    grad_scores = (weights_p * (grad_weights - row_delta)).astype(bf16)
    grad_queries = (
        (jnp.einsum("hqk,khd->qhd", grad_scores, key_rows, preferred_element_type=f32) * scaling)
        .reshape(seq_len, -1)
        .astype(bf16)
    )
    grad_keys = (
        (jnp.einsum("hqk,qhd->khd", grad_scores, queries, preferred_element_type=f32) * scaling)
        .reshape(seq_len, -1)
        .astype(bf16)
    )
    grad_values = jnp.einsum(
        "hqk,qhd->khd", weights_low, grad_attended, preferred_element_type=f32
    ).astype(bf16)
    grad_values_float = grad_values.astype(f32)
    grad_projected = (
        (value_gates[..., None] * grad_values_float[:, :, None, :])
        .reshape(seq_len, -1)
        .astype(bf16)
    )
    grad_value_gates = jnp.sum(grad_values_float[:, :, None, :] * projected, axis=-1)
    value_select = (
        jnp.where(value_pick, grad_value_gates * value_sig * (1.0 - value_sig), 0.0)
        .reshape(seq_len, -1)
        .astype(bf16)
    )
    value_local = jnp.einsum("td,tc->dc", layer_input, grad_projected, preferred_element_type=f32)
    query_local = jnp.einsum("td,tc->dc", act_att, grad_queries, preferred_element_type=f32)
    key_local = jnp.einsum("td,tc->dc", act_att, grad_keys, preferred_element_type=f32)
    value_selector_local = jnp.einsum(
        "td,tc->dc", act_att, value_select, preferred_element_type=f32
    )
    output_selector_local = jnp.einsum("td,tc->dc", act_att, out_select, preferred_element_type=f32)
    grad_norm_att = jnp.einsum("tc,dc->td", grad_queries, query_weight, preferred_element_type=f32)
    grad_norm_att = grad_norm_att + jnp.einsum(
        "tc,dc->td", grad_keys, key_weight, preferred_element_type=f32
    )
    grad_norm_att = grad_norm_att + jnp.einsum(
        "tc,dc->td", value_select, value_selector, preferred_element_type=f32
    )
    grad_norm_att = grad_norm_att + jnp.einsum(
        "tc,dc->td", out_select, output_selector, preferred_element_type=f32
    )
    att_gain_local = jnp.sum(grad_norm_att * hat_att, axis=0)
    att_shift_local = jnp.sum(grad_norm_att, axis=0)
    input_grad = grad_residual + jnp.einsum(
        "tc,dc->td", grad_projected, value_weight, preferred_element_type=f32
    )
    input_grad = input_grad + norm_backward(grad_norm_att, hat_att, inv_att, att_gain)
    reduced = (
        lax.psum_scatter(att_gain_local, ("dp", "expert"), scatter_dimension=0, tiled=True),
        lax.psum_scatter(att_shift_local, ("dp", "expert"), scatter_dimension=0, tiled=True),
        lax.psum_scatter(query_local, ("dp", "expert"), scatter_dimension=0, tiled=True),
        lax.psum_scatter(key_local, ("dp", "expert"), scatter_dimension=0, tiled=True),
        lax.psum_scatter(value_local, ("dp", "expert"), scatter_dimension=0, tiled=True),
        lax.psum_scatter(output_local, ("dp", "expert"), scatter_dimension=1, tiled=True),
        lax.psum_scatter(value_selector_local, ("dp", "expert"), scatter_dimension=0, tiled=True),
        lax.psum_scatter(output_selector_local, ("dp", "expert"), scatter_dimension=0, tiled=True),
        lax.psum_scatter(ffn_gain_local, ("dp", "expert"), scatter_dimension=0, tiled=True),
        lax.psum_scatter(ffn_shift_local, ("dp", "expert"), scatter_dimension=0, tiled=True),
        lax.psum_scatter(ffn_selector_local, ("dp", "expert"), scatter_dimension=0, tiled=True),
    )
    up_grad, down_grad = (
        lax.psum_scatter(
            up_local.astype(jnp.bfloat16), "dp", scatter_dimension=1, tiled=True
        ).astype(jnp.float32),
        lax.psum_scatter(
            down_local.astype(jnp.bfloat16), "dp", scatter_dimension=2, tiled=True
        ).astype(jnp.float32),
    )
    return (
        output,
        input_grad,
        reduced[0],
        reduced[1],
        reduced[2],
        reduced[3],
        reduced[4],
        reduced[5],
        reduced[6],
        reduced[7],
        reduced[8],
        reduced[9],
        reduced[10],
        up_grad,
        down_grad,
        counts_all[:EXPERTS],
    )


def mm(a, b, ca, cb):
    return lax.dot_general(a, b, (((ca,), (cb,)), ((), ())), preferred_element_type=f32)


def iota(shape, dim):
    return lax.broadcasted_iota(jnp.int32, shape, dim)


def centre(values):
    centred = values - jnp.mean(values, axis=-1, keepdims=True)
    inverse = lax.rsqrt(jnp.mean(centred * centred, axis=-1, keepdims=True) + EPSILON)
    return centred * inverse, inverse


def centre_back(upstream, normed, inverse, gain):
    scaled = upstream * gain
    mean = jnp.mean(scaled, axis=-1, keepdims=True)
    slope = jnp.mean(scaled * normed, axis=-1, keepdims=True)
    return inverse * (scaled - mean - normed * slope)


def device_of(ids, s, x):
    return 2 * s + (ids[1] + x - 2 * ids[1] * x)


SHORT = pl.CostEstimate(flops=1, bytes_accessed=1, transcendentals=0)


LONG = pl.CostEstimate(flops=1, bytes_accessed=1 << 28, transcendentals=0)


def call(body, outs, args, scratch=(), smem=(), name=None, cost=SHORT):
    return pl.pallas_call(
        body,
        out_shape=[jax.ShapeDtypeStruct(s, d) for s, d in outs],
        in_specs=[pl.BlockSpec(memory_space=pltpu.SMEM)] * len(smem)
        + [pl.BlockSpec(memory_space=pltpu.VMEM)] * len(args),
        out_specs=[pl.BlockSpec(memory_space=pltpu.VMEM)] * len(outs),
        scratch_shapes=list(scratch),
        compiler_params=pltpu.CompilerParams(vmem_limit_bytes=VMEM_LIMIT),
        cost_estimate=cost,
        name=name,
    )(*smem, *args)


def forward_body(
    length, li, vroutes, oroutes, froutes, att_gain, att_shift, wq, wk, wv, wo, vsel, osel,
    ffn_gain, ffn_shift, fsel,
    h1_o, xpack_o, q_o, k_o, v_o, p_o, a_o, o_o, gt_o, a1_o, a2_o, mixed,
):
    T, D = li.shape
    heads = vroutes.shape[0]
    dh = wq.shape[1] // heads
    ea = wv.shape[1] // (heads * dh)
    he = heads * ea
    top = froutes.shape[0]
    routes = [vroutes[h] for h in range(heads)] + [oroutes[h] for h in range(heads)] + [froutes[...]]
    routes = jnp.concatenate([r.astype(f32) for r in routes], axis=0)
    routes = jnp.concatenate([routes, jnp.zeros((128 - routes.shape[0], T), f32)], axis=0).T.astype(jnp.int32)
    scaling = 1.0 / math.sqrt(dh)
    x = li[...].astype(f32)
    hat, inv = centre(x)
    mean = jnp.mean(x, axis=-1, keepdims=True)
    a1 = (hat * att_gain[...] + att_shift[...]).astype(bf16)
    a1_o[...] = a1
    logits = jnp.concatenate(
        [mm(a1, vsel[...], 1, 1), mm(a1, osel[...], 1, 1), jnp.zeros((T, 128 - 2 * he), f32)], axis=1
    )
    lane = iota((T, 128), 1)
    chosen = jnp.zeros((T, 128), jnp.bool_)
    for j in range(2 * heads):
        h = j // 2
        chosen |= lane == routes[:, j : j + 1] + h * ea
        chosen |= lane == routes[:, 2 * heads + j : 2 * heads + j + 1] + (he + h * ea)
    gt = jnp.where(chosen, jax.nn.sigmoid(logits), 0.0)
    gt_o[...] = jnp.where(lane == 2 * he, mean, jnp.where(lane == 2 * he + 1, inv, gt))
    q = mm(a1, wq[...], 1, 0).astype(bf16)
    k = mm(a1, wk[...], 1, 0).astype(bf16)
    q_o[...] = q
    k_o[...] = k
    n_live = length[0]
    row, col = iota((T, T), 0), iota((T, T), 1)
    causal = (col <= row) & (col < n_live)
    width = ea * dh
    for h in range(heads):
        proj = mm(li[...], wv[:, h * width : (h + 1) * width], 1, 0)
        p_o[:, h * width : (h + 1) * width] = proj
        v = jnp.zeros((T, dh), f32)
        for e in range(ea):
            v += gt[:, h * ea + e : h * ea + e + 1] * proj[:, e * dh : (e + 1) * dh]
        v = v.astype(bf16)
        v_o[:, h * dh : (h + 1) * dh] = v
        s = mm(q[:, h * dh : (h + 1) * dh], k[:, h * dh : (h + 1) * dh], 1, 1) * scaling
        s = jnp.where(causal, s, NEGATIVE)
        ex = jnp.exp(s - jnp.max(s, axis=-1, keepdims=True))
        a = ex / jnp.sum(ex, axis=-1, keepdims=True)
        a_o[h] = a
        o = mm(a.astype(bf16), v, 1, 0)
        o_o[:, h * dh : (h + 1) * dh] = o
        for e in range(ea):
            c = he + h * ea + e
            mixed[:, (h * ea + e) * dh : (h * ea + e + 1) * dh] = (gt[:, c : c + 1] * o).astype(bf16)
    h1 = x + mm(mixed[...], wo[...], 1, 0)
    h1_o[...] = h1
    hat2, _ = centre(h1)
    a2 = (hat2 * ffn_gain[...] + ffn_shift[...]).astype(bf16)
    a2_o[...] = a2
    sig = jax.nn.sigmoid(mm(a2, fsel[...], 1, 1))
    wide = iota(sig.shape, 1)
    g = jnp.zeros((T, 128), f32)
    for i in range(top):
        c = 4 * heads + i
        one = jnp.sum(jnp.where(wide == routes[:, c : c + 1], sig, 0.0), axis=-1, keepdims=True)
        g = jnp.where(lane == i, one, g)
    g = g.T[:16]
    hi = g.astype(bf16)
    low = h1.astype(bf16)
    for s in range(xpack_o.shape[0]):
        xpack_o[s, :T] = low
        xpack_o[s, T:] = jnp.zeros((16, D), bf16)
        xpack_o[s, T:, :128] = hi
        xpack_o[s, T:, 128:256] = (g - hi.astype(f32)).astype(bf16)


def take_slices(v, n_p, S, e):
    D = v.shape[1]
    w = D // (n_p * S)
    return jnp.concatenate(
        [v[:, (b * S + e) * w : (b * S + e + 1) * w] for b in range(n_p)], axis=1
    )


def views(mine, theirs):
    return [r.at[s] for s in range(mine.shape[0]) for r in (mine, theirs)]


def views_from(ids, mine, theirs):
    return [r.at[ids[0] ^ s] for s in range(mine.shape[0]) for r in (mine, theirs)]


def early_body(n_p, S, ids, li, a1, a2, o, gt, *rest):
    msgs, scratch = rest
    msgs = [msgs.at[s] for s in range(S // 2)]
    hd = o.shape[1]
    for e in range(S):
        for i, v in enumerate((li, a1, a2)):
            scratch[e, :, i * 128 : (i + 1) * 128] = take_slices(v[...].astype(f32), n_p, S, e).astype(bf16)
    hi = gt[...].astype(bf16).astype(f32)
    both = (hi + pltpu.roll(gt[...] - hi, 64, 1)).astype(bf16)
    for s, m in enumerate(msgs):
        m[:, :hd] = o[...].astype(bf16)
        m[:, hd : hd + 128] = both
        m[:, hd + 128 : hd + 512] = scratch[device_of(ids, s, 1)]
        m[:, hd + 512 : hd + 896] = scratch[device_of(ids, s, 0)]


def codes_body(S, ids, *refs):
    c, (code_o, cnt_o, routes_o) = views_from(ids, *refs[:2]), refs[2:]
    ep = cnt_o.shape[1]
    T = code_o.shape[2] // 2
    strict = (iota((T, T), 0) < iota((T, T), 1)).astype(f32).astype(bf16)
    e_id = iota((ep, T), 0).astype(f32)
    cnt = jnp.zeros((8, ep), f32)
    start = ids[3].astype(f32)
    for k in range(S):
        r = c[k][:, :T].astype(f32) * 32.0 + c[k][:, T:].astype(f32)
        routes_o[k * 16 : (k + 1) * 16, :] = r
        r -= start
        mask = jnp.zeros((ep, T), f32)
        for i in range(r.shape[0]):
            mask = jnp.where(r[i : i + 1] == e_id, 1.0, mask)
        low = mask.astype(bf16)
        rank = mm(low, strict, 1, 0) + (MOST * (k % 2))
        cnt += mm(jnp.ones((8, T), bf16), low, 1, 1)
        code_o[k // 2, :, (k % 2) * T : (k % 2 + 1) * T] = jnp.where(mask > 0.5, rank, -1.0).astype(bf16)
    cnt_o[...] = cnt


def columns_body(n_p, order, ids, x, *refs):
    outs = refs[-n_p:]
    T = x.shape[1] - 16
    wide = outs[0].shape[2]
    for k in range(x.shape[0]):
        rows = x.at[ids[0] ^ k if order else k]
        for s in range(n_p):
            at = pl.multiple_of((ids[2] ^ s) * wide, 128)
            outs[s][k, :T, :] = rows[:T, pl.ds(at, wide)]
    if len(refs) > n_p:
        for s in range(n_p):
            outs[s][:, T:, :] = refs[0][...]


def gelu_both(u):
    t = jnp.tanh(GELU_A * (u + GELU_B * u * u * u))
    value = 0.5 * u * (1.0 + t)
    slope = 0.5 * (1.0 + t) + 0.5 * u * (1.0 - t * t) * (GELU_A * (1.0 + 3.0 * GELU_B * u * u))
    return value, slope


def experts_body(S, eb, ids, *refs):
    x, c = views(*refs[:2]), views_from(ids, *refs[2:4])
    code, up, down, dx0, dx1, gy0, gy1, gr_o, du_o, ct, gts, dl, ps, xs, cs, gys, dxs = refs[4:]
    step = pl.program_id(0)
    pairs = S // 2
    R = 2 * MOST
    T = x[0].shape[0] - 16
    D = x[0].shape[1]
    ep = ct.shape[1]
    rows = pairs * R
    H = up.shape[2]

    @pl.when(step == 0)
    def _():
        e_id = iota((ep, T), 0).astype(f32)
        start = ids[3].astype(f32)
        dl[...] = jnp.zeros_like(dl)
        for pr in range(pairs):
            ct[pr] = code[pr].astype(f32)
        for k in range(S):
            r = c[k][T:, :T].astype(f32) * 32.0 + c[k][T:, T : 2 * T].astype(f32) - start
            g = x[k][T:, :T].astype(f32) + x[k][T:, T : 2 * T].astype(f32)
            dense = jnp.zeros((ep, T), f32)
            for i in range(r.shape[0]):
                dense = jnp.where(r[i : i + 1] == e_id, g[i : i + 1], dense)
            gts[:, k * T : (k + 1) * T] = dense

    slot = iota((R, 2 * T), 0).astype(f32)
    g_slot = [[None] * pairs for _ in range(eb)]
    onehot = [[None] * pairs for _ in range(eb)]
    for pr in range(pairs):
        blocks = []
        for j in range(eb):
            e = step * eb + j
            hot = jnp.where(ct[pr, pl.ds(e, 1), :] == slot, 1.0, 0.0)
            onehot[j][pr] = hot
            g_slot[j][pr] = jnp.sum(
                hot * gts[pl.ds(e, 1), pr * 2 * T : (pr + 1) * 2 * T], axis=-1, keepdims=True
            )
            blocks.append(hot.astype(bf16))
        block = jnp.concatenate(blocks, axis=0)
        ps[pr, pl.ds(pl.multiple_of(step * (eb * R), R), eb * R), :] = block
        for src, dst in ((x, xs), (c, cs)):
            both = jnp.concatenate([src[2 * pr][:T], src[2 * pr + 1][:T]], axis=0)
            got = mm(block, both, 1, 0).astype(bf16)
            for j in range(eb):
                dst[j * rows + pr * R : j * rows + (pr + 1) * R, :] = got[j * R : (j + 1) * R]
    for first in range(0, eb, 2):
        js = list(range(first, min(first + 2, eb)))
        n = len(js)
        span = slice(first * rows, (first + n) * rows)
        g = jnp.concatenate([p for j in js for p in g_slot[j]], axis=0)
        cj = cs[span, :].astype(f32)
        ups = jnp.concatenate([up[j] for j in js], axis=1)
        downs = jnp.concatenate([down[j] for j in js], axis=0)

        def own(v):
            return jnp.concatenate([v[i * rows : (i + 1) * rows, i * H : (i + 1) * H] for i in range(n)], axis=0)

        def spread_out(v):
            if n == 1:
                return v
            zero = jnp.zeros((rows, H), v.dtype)
            return jnp.concatenate(
                [
                    jnp.concatenate([v[i * rows : (i + 1) * rows] if i == b else zero for b in range(n)], axis=1)
                    for i in range(n)
                ],
                axis=0,
            )

        u = own(mm(xs[span, :], ups, 1, 0))
        value, slope = gelu_both(u)
        r = value.astype(bf16)
        y = mm(spread_out(r), downs, 1, 0).astype(bf16).astype(f32)
        dgate = jnp.sum(cj * y, axis=-1, keepdims=True)
        gy = (g * y).astype(bf16)
        dr = own(mm((g * cj).astype(bf16), downs, 1, 1))
        du = (dr * slope).astype(bf16)
        dx = mm(spread_out(du), ups, 1, 1).astype(bf16)
        gr = (g * r.astype(f32)).astype(bf16)
        dlog = dgate * g * (1.0 - g)
        for i, j in enumerate(js):
            e = step * eb + j
            gr_o[j] = gr[i * rows : (i + 1) * rows]
            du_o[j] = du[i * rows : (i + 1) * rows]
            for pr in range(pairs):
                at = pl.ds(pl.multiple_of(step * (eb * R) + j * R, R), R)
                cut = slice(i * rows + pr * R, i * rows + (pr + 1) * R)
                gys[pr, at, :] = gy[cut]
                dxs[pr, at, :] = dx[cut]
                dl[pl.ds(e, 1), pr * 2 * T : (pr + 1) * 2 * T] = jnp.sum(
                    onehot[j][pr] * dlog[cut], axis=0, keepdims=True
                )

    @pl.when(step == pl.num_programs(0) - 1)
    def _():
        for pr in range(pairs):
            for src, d0, d1 in ((dxs, dx0, dx1), (gys, gy0, gy1)):
                got = mm(ps[pr], src[pr], 0, 0).astype(bf16)
                d0[pr, :T] = got[:T]
                d1[pr, :T] = got[T:]
            for x_i, d in ((0, dx0), (1, dx1)):
                k = 2 * pr + x_i
                part = dl[:, k * T : (k + 1) * T].astype(bf16)
                d[pr, T:] = jnp.zeros((16, D), bf16)
                for b in range(ep // 16):
                    d[pr, T:, b * T : (b + 1) * T] = part[16 * b : 16 * b + 16]


def join_body(T, mine, recv, out):
    half = mine.shape[2] // 2
    for s in range(mine.shape[0]):
        out[s, :T] = (mine[s, :T].astype(f32) + recv[s, :T].astype(f32)).astype(bf16)
        if mine.shape[1] > T:
            out[s, T:, :half] = mine[s, T:, :half]
            out[s, T:, half:] = recv[s, T:, :half]


def join_apart_body(nz, ids, mine, recv, *outs):
    for s in range(nz):
        outs[s][...] = (mine[ids[0] ^ s].astype(f32) + recv[ids[0] ^ s].astype(f32)).astype(bf16)


def ffn_back_body(n_p, S, nz, ids, parts, h1, c, fsel, gain, froutes, cnt, dh1_o, db_o, mid_o, dlt, sl):
    T, D = h1.shape
    ep = dlt.shape[0] // S
    half = D // 2
    dxs = parts[0, :T].astype(f32)
    for s in range(1, nz):
        dxs += parts[s, :T].astype(f32)
    for s in range(nz):
        for x in range(2):
            for b in range(ep // 16):
                at = pl.multiple_of(device_of(ids, s, x) * ep + 16 * b, 16)
                dlt[pl.ds(at, 16), :] = parts[s, T:, x * half + b * T : x * half + (b + 1) * T].astype(f32)
    dl = dlt[...].T
    da2 = mm(dl.astype(bf16), fsel[...], 1, 0)
    hat, inv = centre(h1[...])
    dh1 = c[...].astype(f32) + dxs + centre_back(da2, hat, inv, gain[...])
    dh1_o[...] = dh1
    db = dh1.astype(bf16)
    db_o[...] = db
    low = db.astype(f32)
    for e in range(S):
        sl[e] = take_slices(low, n_p, S, e).astype(bf16)
    slot = iota(dlt.shape, 0)
    few = [
        jnp.sum(jnp.where(slot == froutes[i : i + 1, :], dlt[...], 0.0), axis=0, keepdims=True)
        for i in range(froutes.shape[0])
    ]
    few = jnp.concatenate(few, axis=0).astype(bf16)
    hi = cnt[...].astype(bf16)
    lo = (cnt[...] - hi.astype(f32)).astype(bf16)
    vectors = []
    for v in (jnp.sum(da2 * hat, axis=0, keepdims=True), jnp.sum(da2, axis=0, keepdims=True)):
        high = v.astype(bf16).astype(f32)
        for part in (high, v - high):
            vectors += [part[:, b * 256 : (b + 1) * 256] for b in range(D // 256)]
    vectors = jnp.concatenate(vectors, axis=0).astype(bf16)
    for s in range(nz):
        m = mid_o.at[s]
        m[:T, :128] = sl[device_of(ids, s, 1)]
        m[:T, 128:] = sl[device_of(ids, s, 0)]
        m[T : T + 16, :T] = few
        m[T : T + 16, T:] = jnp.zeros((16, 256 - T), bf16)
        m[T : T + 16, T : T + ep] = jnp.concatenate([hi, lo], axis=0)
        m[T + 16 :] = vectors


def attention_back_body(db, wo, gt, o, q, k, v, a, p, late_o, dp_o):
    T, D = db.shape
    heads = a.shape[0]
    dh = q.shape[1] // heads
    ea = p.shape[1] // (heads * dh)
    he, hd = heads * ea, heads * dh
    width = ea * dh
    scaling = 1.0 / math.sqrt(dh)
    gates = gt[...]
    lane = iota((T, 128), 1)
    every = range(heads)
    hs = [slice(h * dh, (h + 1) * dh) for h in every]
    dz = [mm(db[...], wo[h * width : (h + 1) * width, :], 1, 1) for h in every]
    do = []
    for h in every:
        total = jnp.zeros((T, dh), f32)
        for e in range(ea):
            c = he + h * ea + e
            total += gates[:, c : c + 1] * dz[h][:, e * dh : (e + 1) * dh]
        do.append(total.astype(bf16))
    da = [mm(do[h], v[:, hs[h]], 1, 1) for h in every]
    dv = [mm(a[h].astype(bf16), do[h], 0, 0).astype(bf16) for h in every]
    ds = [(a[h] * (da[h] - jnp.sum(a[h] * da[h], axis=-1, keepdims=True))).astype(bf16) for h in every]
    dq = [(mm(ds[h], k[:, hs[h]], 1, 0) * scaling).astype(bf16) for h in every]
    dk = [(mm(ds[h], q[:, hs[h]], 0, 0) * scaling).astype(bf16) for h in every]
    dgates = jnp.zeros((T, 128), f32)
    for h in every:
        oh, dvf = o[:, hs[h]], dv[h].astype(f32)
        for e in range(ea):
            c = h * ea + e
            es = slice(c * dh, (c + 1) * dh)
            dp_o[:, es] = (gates[:, c : c + 1] * dvf).astype(bf16)
            out_sum = jnp.sum(dz[h][:, e * dh : (e + 1) * dh] * oh, axis=-1, keepdims=True)
            in_sum = jnp.sum(dvf * p[:, es], axis=-1, keepdims=True)
            dgates = jnp.where(lane == he + c, out_sum, jnp.where(lane == c, in_sum, dgates))
    sel = (dgates * gates * (1.0 - gates)).astype(bf16)
    for s in range(late_o.shape[0]):
        for h in every:
            late_o[s, :, hs[h]] = dv[h]
            late_o[s, :, hd + h * dh : hd + (h + 1) * dh] = dq[h]
            late_o[s, :, 2 * hd + h * dh : 2 * hd + (h + 1) * dh] = dk[h]
        late_o[s, :, 3 * hd :] = sel


def input_back_body(late, dp, wq, wk, wv, selw, li, gain, dh1, ig_o):
    hd = wq.shape[1]
    da1 = mm(late[0, :, hd : 2 * hd], wq[...], 1, 1)
    da1 += mm(late[0, :, 2 * hd : 3 * hd], wk[...], 1, 1)
    da1 += mm(late[0, :, 3 * hd :], selw[...], 1, 1)
    hat, inv = centre(li[...].astype(f32))
    ig_o[...] = dh1[...] + mm(dp[...], wv[...], 1, 1) + centre_back(da1, hat, inv, gain[...])


def spread(values, gates, lo, heads, ea, dh):
    return jnp.concatenate(
        [
            (gates[:, lo + h * ea + e : lo + h * ea + e + 1] * values[:, h * dh : (h + 1) * dh]).astype(bf16)
            for h in range(heads)
            for e in range(ea)
        ],
        axis=1,
    )


def spread_body(S, n_p, w, heads, ea, ids, e0, e1, wq, wk, selw, z_o, a2_o, lia1_o, hat_o, gates_o, wsl_o):
    early = views(e0, e1)
    T = early[0].shape[0]
    D, hd = wq.shape
    for b in range(n_p):
        at = pl.ds(pl.multiple_of(b * (D // n_p) + (2 * ids[0] + ids[1]) * w, 16), w)
        bs = slice(b * w, (b + 1) * w)
        wsl_o[bs, :hd] = wq[at, :]
        wsl_o[bs, hd : 2 * hd] = wk[at, :]
        wsl_o[bs, 2 * hd :] = selw[at, :]
    for k in range(S):
        ts = slice(k * T, (k + 1) * T)
        m = early[k]
        both = m[:, hd : hd + 128].astype(f32)
        gates = both + pltpu.roll(both, 64, 1)
        gates_o[ts, :] = gates
        z_o[ts, :] = spread(m[:, :hd].astype(f32), gates, heads * ea, heads, ea, hd // heads)
        at = hd + 512 if k % 2 == 0 else hd + 128
        li = m[:, at : at + 128].astype(f32)
        he2 = 2 * heads * ea
        lia1_o[:128, ts] = li.T.astype(bf16)
        lia1_o[128:, ts] = m[:, at + 128 : at + 256].astype(f32).T.astype(bf16)
        hat_o[:, ts] = ((li - gates[:, he2 : he2 + 1]) * gates[:, he2 + 1 : he2 + 2]).T
        a2_o[ts, :] = m[:, at + 256 : at + 384]


def out_rows(acc, outs, ids, w):
    for s, ref in enumerate(outs):
        plane = ids[2] ^ s
        ref[:, : acc.shape[1]] = acc[pl.ds(pl.multiple_of(plane * w, 8), w), :].astype(ref.dtype)


def out_grads_body(S, n_p, w, ids, m0, m1, z, a2, routes, *refs):
    mid, outs = views(m0, m1), refs[:n_p]
    acc, lhs, dlt, cnt = refs[n_p:]
    T = z.shape[0] // S
    EP = dlt.shape[0]
    e_id = iota((EP, T), 0).astype(f32)
    norms = jnp.zeros((16, 256), f32)
    for k in range(S):
        n = mid[k]
        ts = slice(k * T, (k + 1) * T)
        at = 128 if k % 2 == 0 else 0
        lhs[ts, :] = n[:T, at : at + 128]
        few = n[T : T + 16, :T].astype(f32)
        route = routes[k * 16 : (k + 1) * 16, :]
        dense = jnp.zeros((EP, T), f32)
        for i in range(16):
            dense = jnp.where(route[i : i + 1] == e_id, few[i : i + 1], dense)
        dlt[:, ts] = dense.astype(bf16)
        tally = n[T : T + 16, T:].astype(f32)
        at = device_of(ids, k // 2, k % 2)
        cnt[pl.ds(at, 1), :] = tally[:1]
        cnt[pl.ds(at + 8, 1), :] = tally[8:9]
        norms += n[T + 16 :].astype(f32)
    wide = z.shape[1]
    acc[:, :wide] = mm(lhs[...], z[...], 0, 0)
    acc[:, wide:] = mm(dlt[...], a2[...], 1, 0).T
    out_rows(acc, outs, ids, w)
    norms = pltpu.roll(norms, lax.rem(256 - (2 * ids[0] + ids[1]) * w, 256), 1)
    norms = jnp.concatenate([norms[0:4] + norms[4:8], norms[8:12] + norms[12:16]], axis=0)
    extra = jnp.concatenate([cnt[...], norms[:, :128], jnp.zeros((w - 24, 128), f32)], axis=0)
    for ref in outs:
        ref[:, acc.shape[1] :] = extra.astype(ref.dtype)


def in_grads_body(n_p, heads, ea, w, hd, ids, l0, l1, lia1, hat, gates, wsl, *refs):
    outs, (acc, rhs, qk, sums) = refs[:n_p], refs[n_p:]
    step = pl.program_id(0)
    T = l0.shape[1]
    wide = rhs.shape[1]

    @pl.when(step == 0)
    def _():
        acc[...] = jnp.zeros_like(acc)
        sums[...] = jnp.zeros_like(sums)

    for x, n in enumerate((l0, l1)):
        ts = slice(x * T, (x + 1) * T)
        rhs[ts, :] = spread(n[0, :, :hd].astype(f32), gates[ts, :], 0, heads, ea, hd // heads)
        qk[ts, :] = n[0, :, hd:]
    acc[:, :wide] += mm(lia1[:128, :], rhs[...], 1, 0)
    acc[:, wide:] += mm(lia1[128:, :], qk[...], 1, 0)
    da1 = mm(wsl[...], qk[...], 1, 1)
    gain = jnp.sum(da1 * hat[...], axis=1, keepdims=True)
    shift = jnp.sum(da1, axis=1, keepdims=True)
    lane = iota((128, 128), 1)
    sums[...] += jnp.where(lane == 64, gain, jnp.where(lane == 65, shift, 0.0))

    @pl.when(step == pl.num_programs(0) - 1)
    def _():
        acc[:, wide + 2 * hd :] += sums[...]
        out_rows(acc, outs, ids, w)


def last_a_body(n_p, S, w, el, ids, *refs):
    parts, (og_o, fg_o, gain_o, shift_o, counts_o, rows) = refs[:n_p], refs[n_p:]
    total = parts[0][...]
    for m in parts[1:]:
        total += m[...].astype(f32)
    wide = og_o.shape[1]
    og_o[...] = total[:w, :wide]
    ep = (total.shape[1] - 128 - wide) // S
    sel = total[:, wide:]
    fg_o[...] = jnp.concatenate([sel[:, e * ep : e * ep + el] for e in range(S)], axis=1)[:, : fg_o.shape[1]]
    extra = total[:, wide + S * ep :]
    rows[...] = extra[16:24]
    gain_o[...] = rows[pl.ds(ids[2], 1), :w]
    shift_o[...] = rows[pl.ds(ids[2] + n_p, 1), :w]
    cnt = extra[0:8] + extra[8:16]
    counts_o[...] = jnp.concatenate([cnt[e : e + 1, :el] for e in range(S)], axis=1)[:, : counts_o.shape[1]]


def last_b_body(n_p, w, hd, he, *refs):
    parts, (vg_o, qg_o, kg_o, vs_o, os_o, gain_o, shift_o) = refs[:n_p], refs[n_p:]
    total = parts[0][...]
    for m in parts[1:]:
        total += m[...].astype(f32)
    wide = vg_o.shape[1]
    vg_o[...] = total[:w, :wide]
    qg_o[...] = total[:w, wide : wide + hd]
    kg_o[...] = total[:w, wide + hd : wide + 2 * hd]
    sel = total[:w, wide + 2 * hd :].T
    vs_o[...] = sel[:he]
    os_o[...] = sel[he : 2 * he]
    gain_o[...] = sel[64:65]
    shift_o[...] = sel[65:66]


def expert_grads_body(n_p, eb, first, xm, xo, cm, co, *refs):
    gr_in, du_in = refs[:n_p], refs[n_p : 2 * n_p]
    up_o, down_o, ct, got = refs[-4:]
    start = pl.program_id(0)
    step = start + first
    _, pairs, T, wide = cm.shape
    T2 = 2 * T
    R = 2 * MOST
    rows = pairs * R

    @pl.when(start == 0)
    def _():
        for s in range(n_p):
            for pr in range(pairs):
                ct[s * pairs + pr] = xm[s, pr, T:, :].astype(f32)

    slot = iota((R, T2), 0).astype(f32)
    for s in range(n_p):
        for pr in range(pairs):
            block = jnp.concatenate(
                [
                    jnp.where(ct[s * pairs + pr, pl.ds(step * eb + j, 1), :] == slot, 1.0, 0.0).astype(bf16)
                    for j in range(eb)
                ],
                axis=0,
            )
            both = jnp.concatenate(
                [jnp.concatenate([x[s, pr, :T], c[s, pr]], axis=1) for x, c in ((xm, cm), (xo, co))], axis=0
            )
            res = mm(block, both, 1, 0).astype(bf16)
            for j in range(eb):
                at = j * n_p * rows + s * rows + pr * R
                got[at : at + R, :] = res[j * R : (j + 1) * R]
    for j in range(eb):
        at = j * n_p * rows
        xj = got[at : at + n_p * rows, :wide]
        cj = got[at : at + n_p * rows, wide:]
        gr = jnp.concatenate([gr_in[s][j] for s in range(n_p)], axis=0)
        du = jnp.concatenate([du_in[s][j] for s in range(n_p)], axis=0)
        up_o[j] = mm(xj, du, 0, 0)
        down_o[j] = mm(gr, cj, 0, 0)


def after(values, *deps):
    return lax.optimization_barrier((values, deps))[0]


class Links:
    def __init__(self):
        self.n_e = lax.axis_size("expert")
        self.nz = self.n_e // 2
        self.n_p = lax.axis_size("dp")
        self.me = lax.axis_index("expert")
        self.z, self.c = self.me // 2, self.me % 2
        self.p = lax.axis_index("dp")

    def core(self, v):
        return lax.ppermute(v, "expert", [(e, e ^ 1) for e in range(self.n_e)])

    def chips(self, v):
        groups = [[2 * s + c for s in range(self.nz)] for c in range(2)]
        return lax.all_to_all(v, "expert", 0, 0, axis_index_groups=groups, tiled=True)

    def chip(self, v, s):
        return lax.ppermute(v, "expert", [(e, (e + 2 * s) % self.n_e) for e in range(self.n_e)])

    def plane(self, v, s):
        return lax.ppermute(v, "dp", [(p, p ^ s) for p in range(self.n_p)])

    def near(self, msgs):
        pairs = [[(e, e ^ (2 * s)) for e in range(self.n_e)] for s in range(self.nz)]
        return [msgs[0]] + [lax.ppermute(msgs[s], "expert", pairs[s]) for s in range(1, self.nz)]

    def relay(self, mine):
        return [mine, self.core(mine)]

    def planes_of(self, msgs):
        return [msgs[0]] + [self.plane(msgs[s], s) for s in range(1, self.n_p)]


def fast_path(
    layer_input, cotangent, lengths, value_routes, output_routes, ffn_routes, att_gain, att_shift,
    query_weight, key_weight, value_weight, output_weight, value_selector, output_selector,
    ffn_gain, ffn_shift, ffn_selector, up_weight, down_weight,
):
    L = Links()
    S, nz, n_p = L.n_e, L.nz, L.n_p
    pairs = S // 2
    T, D = layer_input.shape
    heads = value_routes.shape[1]
    dh = query_weight.shape[1] // heads
    ea = value_selector.shape[1] // heads
    hd, he, wide = heads * dh, heads * ea, heads * ea * dh
    el, _, H = up_weight.shape
    ep = -(-el // 16) * 16
    EP = ep * S
    w = D // (n_p * S)
    Dp = D // n_p
    R = 2 * MOST
    eb = max(d for d in (7, 4, 2, 1) if el % d == 0)

    ids = jnp.stack([L.z, L.c, L.p, L.me * ep]).astype(jnp.int32)
    raw = ffn_routes.T
    padded = (raw // el) * ep + raw % el

    rt = jnp.where(jnp.arange(T)[None, :] < lengths[0], padded, EP)
    tail = jnp.concatenate([rt // 32, rt % 32], axis=1).astype(bf16)
    cpack = jnp.concatenate([cotangent, jnp.pad(tail, ((0, 0), (0, D - 2 * T)))], axis=0)
    c_far = L.near([cpack] * nz)

    h1, xpack, q, k, v, proj, a, o, gt, a1, a2 = call(
        forward_body,
        [
            ((T, D), f32), ((nz, T + 16, D), bf16), ((T, hd), bf16), ((T, hd), bf16), ((T, hd), bf16),
            ((T, wide), f32), ((heads, T, T), f32), ((T, hd), f32), ((T, 128), f32),
            ((T, D), bf16), ((T, D), bf16),
        ],
        [
            layer_input, value_routes.transpose(1, 2, 0), output_routes.transpose(1, 2, 0), raw,
            att_gain[None], att_shift[None], query_weight, key_weight, value_weight, output_weight,
            value_selector.T, output_selector.T, ffn_gain[None], ffn_shift[None], ffn_selector.T,
        ],
        scratch=[pltpu.VMEM((T, wide), bf16)],
        smem=[lengths],
        name="forward",
    )
    x_far = L.chips(xpack)
    selectors = after((ffn_selector, value_selector, output_selector), xpack)
    fsel = jnp.pad(selectors[0].T, ((0, S * el - ffn_selector.shape[1]), (0, 0)))
    fsel = jnp.pad(fsel.reshape(S, el, D), ((0, 0), (0, ep - el), (0, 0))).reshape(EP, D)
    selw = jnp.pad(jnp.concatenate(selectors[1:], axis=1), ((0, 0), (0, 128 - 2 * he)))
    (early,) = call(
        partial(early_body, n_p, S),
        [((nz, T, hd + 896), bf16)],
        [layer_input, a1, a2, o, gt],
        scratch=[pltpu.VMEM((S, T, 384), bf16)],
        smem=[ids],
        name="early_slices",
    )
    c_msgs = L.relay(jnp.stack(after(c_far, early, fsel, selw)))
    ccols = call(
        partial(columns_body, n_p, True), [((nz, T, Dp), bf16)] * n_p, [after(c_msgs[0], c_msgs[1])], smem=[ids],
        name="cotangent_columns",
    )
    cc_all = [ccols[0], L.plane(ccols[1], 1), L.plane(ccols[2], 2)]
    tail_rows = pl.BlockSpec((nz, 16, 2 * T), lambda i: (0, T // 16, 0))
    code, cnt, routes = pl.pallas_call(
        partial(codes_body, S),
        grid=(1,),
        in_specs=[pl.BlockSpec(memory_space=pltpu.SMEM), tail_rows, tail_rows],
        out_specs=[pl.BlockSpec(memory_space=pltpu.VMEM)] * 3,
        out_shape=[
            jax.ShapeDtypeStruct((pairs, ep, 2 * T), bf16), jax.ShapeDtypeStruct((8, ep), f32),
            jax.ShapeDtypeStruct((S * 16, T), f32),
        ],
        compiler_params=pltpu.CompilerParams(vmem_limit_bytes=VMEM_LIMIT),
        cost_estimate=SHORT,
        name="codes",
    )(ids, *after(c_msgs, ccols))
    x_far = after(x_far, code, cc_all[1:])
    x_msgs = L.relay(x_far)
    xcols = call(
        partial(columns_body, n_p, False), [((nz, T + ep, Dp), bf16)] * n_p, [x_far, code],
        smem=[ids],
        name="token_columns",
    )
    xc_all = L.planes_of(xcols)
    early_far = L.chips(after(early, x_far))

    n_eb = el // eb
    whole = [pl.BlockSpec(memory_space=pltpu.VMEM)]
    dx0, dx1, gy0, gy1, gr, du = pl.pallas_call(
        partial(experts_body, S, eb),
        grid=(n_eb,),
        out_shape=[
            jax.ShapeDtypeStruct((pairs, T + 16, D), bf16), jax.ShapeDtypeStruct((pairs, T + 16, D), bf16),
            jax.ShapeDtypeStruct((pairs, T, D), bf16), jax.ShapeDtypeStruct((pairs, T, D), bf16),
            jax.ShapeDtypeStruct((el, pairs * R, H), bf16), jax.ShapeDtypeStruct((el, pairs * R, H), bf16),
        ],
        in_specs=[pl.BlockSpec(memory_space=pltpu.SMEM)]
        + whole * 5
        + [
            pl.BlockSpec((eb, D, H), lambda i: (i, 0, 0)),
            pl.BlockSpec((eb, H, D), lambda i: (i, 0, 0)),
        ],
        out_specs=whole * 4 + [pl.BlockSpec((eb, pairs * R, H), lambda i: (i, 0, 0))] * 2,
        scratch_shapes=[
            pltpu.VMEM((pairs, ep, 2 * T), f32), pltpu.VMEM((ep, S * T), f32), pltpu.VMEM((ep, S * T), f32),
            pltpu.VMEM((pairs, el * R, 2 * T), bf16),
            pltpu.VMEM((eb * pairs * R, D), bf16), pltpu.VMEM((eb * pairs * R, D), bf16),
            pltpu.VMEM((pairs, el * R, D), bf16), pltpu.VMEM((pairs, el * R, D), bf16),
        ],
        compiler_params=pltpu.CompilerParams(vmem_limit_bytes=VMEM_LIMIT),
        cost_estimate=SHORT,
        name="experts",
    )(after(ids, xcols), *x_msgs, *c_msgs, code, up_weight, down_weight)

    def join(mine, other, name):
        return call(partial(join_body, T), [(mine.shape, bf16)], [mine, L.core(other)], name=name)[0]

    def join_apart(mine, other, name):
        return call(
            partial(join_apart_body, nz), [(mine.shape[1:], bf16)] * nz, [mine, L.core(other)], smem=[ids], name=name
        )

    dx0, dx1, early_far, xc_all = lax.optimization_barrier((dx0, dx1, early_far, xc_all))
    dx_join = join(dx0, dx1, "join_dx")
    dx_parts = L.chips(dx_join)
    gr, du = after((gr, du), dx_join)
    gr1, du1 = L.plane(gr, 1), L.plane(du, 2)
    early_far, gy0, gy1, cc3, xc_all = after((early_far, gy0, gy1, ccols[3], xc_all), dx_join)
    xc_both = L.relay(jnp.stack(xc_all))
    cc_all += [L.plane(cc3, 3)]
    gy_join = join_apart(gy0, gy1, "join_out")
    z_all, a2_s, lia1, hat_s, gates, wsl = call(
        partial(spread_body, S, n_p, w, heads, ea),
        [
            ((S * T, wide), bf16), ((S * T, 128), bf16), ((256, S * T), bf16), ((128, S * T), f32),
            ((S * T, 128), f32), ((128, 2 * hd + 128), bf16),
        ],
        [*L.relay(early_far), query_weight, key_weight, selw],
        smem=[ids],
        cost=LONG,
        name="spread_tokens",
    )
    dx_parts, gr1, du1, z_all, gy_join, cc_all, xc_both = lax.optimization_barrier(
        (dx_parts, gr1, du1, z_all, gy_join, cc_all, xc_both)
    )
    cols_both = xc_both + L.relay(jnp.stack(cc_all))
    gr, du = after((gr, du), dx_parts)
    gr_all = [gr, gr1, L.plane(gr, 2)]
    du_all = [du, L.plane(du, 1), du1]

    dh1, db, mid = call(
        partial(ffn_back_body, n_p, S, nz),
        [((T, D), f32), ((T, D), bf16), ((nz, T + 32, 256), bf16)],
        [dx_parts, h1, cotangent, fsel, ffn_gain[None], padded, cnt],
        scratch=[pltpu.VMEM((EP, T), f32), pltpu.VMEM((S, T, 128), bf16)],
        smem=[ids],
        name="ffn_back",
    )
    mid_far = L.chips(mid)
    late, dp = call(
        attention_back_body,
        [((nz, T, 3 * hd + 128), bf16), ((T, wide), bf16)],
        [db, output_weight, gt, o, q, k, v, a, proj],
        cost=LONG,
        name="attention_back",
    )
    late = after(late, mid_far, gr_all[2], du_all[1])
    gr1, du1 = after((gr1, du1), late)
    gr_all += [L.plane(gr1, 2)]
    du_all += [L.plane(du1, 1)]
    late_far = L.chips(late)
    (input_grad,) = call(
        input_back_body,
        [((T, D), f32)],
        [late, dp, query_weight, key_weight, value_weight, selw, layer_input, att_gain[None], dh1],
        name="input_back",
    )
    mid_far = after(mid_far, input_grad)
    grads_a = call(
        partial(out_grads_body, S, n_p, w),
        [((w, wide + EP + 128), f32)] + [((w, wide + EP + 128), bf16)] * (n_p - 1),
        [*L.relay(mid_far), z_all, a2_s, routes],
        scratch=[
            pltpu.VMEM((128, wide + EP), f32), pltpu.VMEM((S * T, 128), bf16),
            pltpu.VMEM((EP, S * T), bf16), pltpu.VMEM((16, 128), f32),
        ],
        smem=[ids],
        name="out_grads",
    )
    a_parts = L.planes_of(grads_a)
    def expert_grads(first, last, args, so_far=()):
        n = len(args)
        return pl.pallas_call(
            partial(expert_grads_body, n_p, eb, first),
            grid=(last - first,),
            in_specs=whole * 4
            + [pl.BlockSpec((eb, pairs * R, H), lambda i: (i + first, 0, 0))] * (2 * n_p)
            + [pl.BlockSpec(memory_space=pl.ANY)] * len(so_far),
            out_specs=[
                pl.BlockSpec((eb, Dp, H), lambda i: (i + first, 0, 0)),
                pl.BlockSpec((eb, H, Dp), lambda i: (i + first, 0, 0)),
            ],
            scratch_shapes=[
                pltpu.VMEM((n_p * pairs, ep, 2 * T), f32),
                pltpu.VMEM((eb * n_p * pairs * R, 2 * Dp), bf16),
            ],
            out_shape=[jax.ShapeDtypeStruct((el, Dp, H), f32), jax.ShapeDtypeStruct((el, H, Dp), f32)],
            input_output_aliases={n + i: i for i in range(len(so_far))},
            compiler_params=pltpu.CompilerParams(vmem_limit_bytes=VMEM_LIMIT),
            cost_estimate=SHORT,
            name="expert_grads",
        )(*args, *so_far)

    cut = (n_eb + 1) // 2
    grads_in = (*cols_both, *after(gr_all + du_all, grads_a))
    half = expert_grads(0, cut, grads_in)
    late_far, a_parts, half = lax.optimization_barrier((late_far, a_parts, half))
    gy_parts = L.near(after(gy_join, late_far))
    late_block = pl.BlockSpec((1, T, 3 * hd + 128), lambda i: (i, 0, 0))
    grads_b = pl.pallas_call(
        partial(in_grads_body, n_p, heads, ea, w, hd),
        grid=(nz,),
        in_specs=[
            pl.BlockSpec(memory_space=pltpu.SMEM), late_block, late_block,
            pl.BlockSpec((256, 2 * T), lambda i: (0, i)), pl.BlockSpec((128, 2 * T), lambda i: (0, i)),
            pl.BlockSpec((2 * T, 128), lambda i: (i, 0)), whole[0],
        ],
        out_specs=whole * n_p,
        out_shape=[
            jax.ShapeDtypeStruct((w, wide + 2 * hd + 128), f32 if s == 0 else bf16) for s in range(n_p)
        ],
        scratch_shapes=[
            pltpu.VMEM((128, wide + 2 * hd + 128), f32), pltpu.VMEM((2 * T, wide), bf16),
            pltpu.VMEM((2 * T, 2 * hd + 128), bf16), pltpu.VMEM((128, 128), f32),
        ],
        compiler_params=pltpu.CompilerParams(vmem_limit_bytes=VMEM_LIMIT),
        cost_estimate=LONG,
        name="in_grads",
    )(ids, *L.relay(late_far), lia1, hat_s, gates, wsl)
    b_parts = L.planes_of(grads_b)
    up_grad, down_grad = expert_grads(cut, n_eb, after(grads_in, grads_b), half)

    output_grad, fgrad, ffn_gain_grad, ffn_shift_grad, counts = call(
        partial(last_a_body, n_p, S, w, el),
        [((w, wide), f32), ((w, EXPERTS), f32), ((1, w), f32), ((1, w), f32), ((1, EXPERTS), f32)],
        after(a_parts, up_grad),
        scratch=[pltpu.VMEM((8, 128), f32)],
        smem=[ids],
        name="last_sum_a",
    )
    gy_parts, b_parts = after((gy_parts, b_parts), fgrad)
    output = (h1 + sum(m.astype(f32) for m in gy_parts)).astype(bf16)
    value_grad, query_grad, key_grad, vsel, osel, att_gain_grad, att_shift_grad = call(
        partial(last_b_body, n_p, w, hd, he),
        [
            ((w, wide), f32), ((w, hd), f32), ((w, hd), f32), ((he, w), f32), ((he, w), f32),
            ((1, w), f32), ((1, w), f32),
        ],
        after(b_parts, output),
        name="last_sum_b",
    )
    return (
        output, input_grad, att_gain_grad[0], att_shift_grad[0], query_grad, key_grad, value_grad,
        output_grad.T, vsel.T, osel.T, ffn_gain_grad[0], ffn_shift_grad[0], fgrad, up_grad, down_grad, counts[0],
    )


def solution(mesh):
    path = fast_path if mesh.shape["expert"] == 8 and mesh.shape["dp"] == 4 else general_path
    placed = (
        P(("dp", "expert"), None),
        P(("dp", "expert"), None),
        P(("dp", "expert")),
        P(("dp", "expert"), None, None),
        P(("dp", "expert"), None, None),
        P(("dp", "expert"), None),
        P(),
        P(),
        P(),
        P(),
        P(),
        P(),
        P(),
        P(),
        P(),
        P(),
        P(),
        P("expert", None, None),
        P("expert", None, None),
    )
    return jax.shard_map(
        path,
        mesh=mesh,
        in_specs=placed,
        out_specs=(
            P(("dp", "expert"), None),
            P(("dp", "expert"), None),
            P(("dp", "expert")),
            P(("dp", "expert")),
            P(("dp", "expert"), None),
            P(("dp", "expert"), None),
            P(("dp", "expert"), None),
            P(None, ("dp", "expert")),
            P(("dp", "expert"), None),
            P(("dp", "expert"), None),
            P(("dp", "expert")),
            P(("dp", "expert")),
            P(("dp", "expert"), None),
            P("expert", "dp", None),
            P("expert", None, "dp"),
            P(),
        ),
        check_vma=False,
    )
```

```python
import math
from functools import partial

import jax
import jax.numpy as jnp
from jax import lax
from jax.experimental import pallas as pl
from jax.experimental.pallas import tpu as pltpu
from jax.sharding import PartitionSpec as P

EXPERTS = 387
MOST = 8
EPSILON = 1e-05
NEGATIVE = -1e30
f32 = jnp.float32
bf16 = jnp.bfloat16
VMEM_LIMIT = 56 * 1024 * 1024
GELU_A = math.sqrt(2.0 / math.pi)
GELU_B = 0.044715


def layer_norm(values, scaling, offset):
    centred = values - jnp.mean(values, axis=-1, keepdims=True)
    inverse = lax.rsqrt(jnp.mean(centred * centred, axis=-1, keepdims=True) + EPSILON)
    normed = centred * inverse
    return (normed * scaling + offset, normed, inverse)


def norm_backward(upstream, normed, inverse, scaling):
    scaled = upstream * scaling
    centre_term = jnp.mean(scaled, axis=-1, keepdims=True)
    slope_term = jnp.mean(scaled * normed, axis=-1, keepdims=True)
    return inverse * (scaled - centre_term - normed * slope_term)


def gate_table(logits, routes, choices_count):
    chosen = jnp.any(routes[..., None] == jnp.arange(choices_count), axis=-2)
    sigmas = jax.nn.sigmoid(logits)
    return (chosen, sigmas, jnp.where(chosen, sigmas, 0.0))


def general_path(
    layer_input,
    cotangent,
    lengths,
    value_routes,
    output_routes,
    ffn_routes,
    att_gain,
    att_shift,
    query_weight,
    key_weight,
    value_weight,
    output_weight,
    value_selector,
    output_selector,
    ffn_gain,
    ffn_shift,
    ffn_selector,
    up_weight,
    down_weight,
):
    f32 = jnp.float32
    bf16 = jnp.bfloat16
    seq_len, width = layer_input.shape
    heads = value_routes.shape[1]
    head_dim = query_weight.shape[1] // heads
    att_experts = value_selector.shape[1] // heads
    top_ffn = ffn_routes.shape[1]
    exp_local = up_weight.shape[0]
    owners = lax.axis_size("expert")
    padded_experts = exp_local * owners
    capacity = MOST
    scaling = 1.0 / math.sqrt(head_dim)
    positions = jnp.arange(seq_len)
    is_valid = positions < lengths[0]
    validity = is_valid.astype(f32)
    input_float = layer_input.astype(f32)
    norm_att, hat_att, inv_att = layer_norm(input_float, att_gain, att_shift)
    act_att = norm_att.astype(bf16)
    queries = (
        jnp.dot(act_att, query_weight, preferred_element_type=f32)
        .astype(bf16)
        .reshape(seq_len, heads, head_dim)
    )
    key_rows = (
        jnp.dot(act_att, key_weight, preferred_element_type=f32)
        .astype(bf16)
        .reshape(seq_len, heads, head_dim)
    )
    projected = jnp.dot(layer_input, value_weight, preferred_element_type=f32).reshape(
        seq_len, heads, att_experts, head_dim
    )
    value_logits = jnp.dot(act_att, value_selector, preferred_element_type=f32).reshape(
        seq_len, heads, att_experts
    )
    output_logits = jnp.dot(act_att, output_selector, preferred_element_type=f32).reshape(
        seq_len, heads, att_experts
    )
    value_pick, value_sig, value_gates = gate_table(value_logits, value_routes, att_experts)
    out_pick, out_sig, out_gates = gate_table(output_logits, output_routes, att_experts)
    values_low = jnp.sum(value_gates[..., None] * projected, axis=2).astype(bf16)
    causal = (positions[None, :] <= positions[:, None]) & is_valid[None, :]
    raw_scores = jnp.einsum("qhd,khd->hqk", queries, key_rows, preferred_element_type=f32) * scaling
    scores = jnp.where(causal[None], raw_scores, NEGATIVE)
    row_peak = jnp.max(scores, axis=-1, keepdims=True)
    log_total = row_peak + jnp.log(jnp.sum(jnp.exp(scores - row_peak), axis=-1, keepdims=True))
    weights_p = jnp.exp(scores - log_total)
    weights_low = weights_p.astype(bf16)
    attended = jnp.einsum("hqk,khd->qhd", weights_low, values_low, preferred_element_type=f32)
    mixed_rows = (out_gates[..., None] * attended[:, :, None, :]).reshape(seq_len, -1).astype(bf16)
    residual = input_float + jnp.dot(mixed_rows, output_weight, preferred_element_type=f32)
    norm_ffn, hat_ffn, inv_ffn = layer_norm(residual, ffn_gain, ffn_shift)
    act_ffn = norm_ffn.astype(bf16)
    ffn_logits = jnp.dot(act_ffn, ffn_selector, preferred_element_type=f32)
    ffn_sig = jax.nn.sigmoid(jnp.take_along_axis(ffn_logits, ffn_routes, axis=1))
    gate_weights = ffn_sig * validity[:, None]
    entries = ffn_routes.reshape(-1)
    live_entry = jnp.broadcast_to(is_valid[:, None], ffn_routes.shape).reshape(-1)
    onehot_table = (
        (entries[:, None] == jnp.arange(padded_experts)[None, :]) & live_entry[:, None]
    ).astype(jnp.int32)
    before = jnp.cumsum(onehot_table, axis=0) - onehot_table
    slot_rank = jnp.sum(before * onehot_table, axis=1)
    counts_local = jnp.sum(onehot_table, axis=0).astype(f32)
    target = jnp.where(live_entry, entries * capacity + slot_rank, padded_experts * capacity)
    fetch = jnp.minimum(target, padded_experts * capacity - 1)
    total_slots = padded_experts * capacity
    residual_low = residual.astype(bf16)
    copies = jnp.broadcast_to(residual_low[:, None, :], (seq_len, top_ffn, width)).reshape(
        -1, width
    )
    send_rows = jnp.zeros((total_slots, width), bf16).at[target].set(copies, mode="drop")
    received = lax.all_to_all(
        send_rows.reshape(owners, exp_local * capacity, width),
        "expert",
        split_axis=0,
        concat_axis=0,
        tiled=True,
    )
    received = received.reshape(owners, exp_local, capacity, width)
    hidden_pre = jnp.einsum("semd,edh->semh", received, up_weight, preferred_element_type=f32)
    hidden_act = jax.nn.gelu(hidden_pre).astype(bf16)
    expert_out = jnp.einsum(
        "semh,ehd->semd", hidden_act, down_weight, preferred_element_type=f32
    ).astype(bf16)
    returned = lax.all_to_all(
        expert_out.reshape(owners, exp_local * capacity, width),
        "expert",
        split_axis=0,
        concat_axis=0,
        tiled=True,
    )
    gathered = (
        returned.reshape(total_slots, width)[fetch].reshape(seq_len, top_ffn, width).astype(f32)
    )
    final = residual + jnp.einsum("tk,tkd->td", gate_weights, gathered)
    output = final.astype(bf16)
    counts_all = lax.psum(counts_local, ("dp", "expert"))
    grad_final = cotangent.astype(f32)
    grad_rows = (gate_weights[:, :, None] * grad_final[:, None, :]).astype(bf16).reshape(-1, width)
    grad_gate = validity[:, None] * jnp.einsum("tkd,td->tk", gathered, grad_final)
    send_grad = jnp.zeros((total_slots, width), bf16).at[target].set(grad_rows, mode="drop")
    grad_recv = lax.all_to_all(
        send_grad.reshape(owners, exp_local * capacity, width),
        "expert",
        split_axis=0,
        concat_axis=0,
        tiled=True,
    )
    grad_recv = grad_recv.reshape(owners, exp_local, capacity, width)
    down_local = jnp.einsum("semh,semd->ehd", hidden_act, grad_recv, preferred_element_type=f32)
    grad_act = jnp.einsum("semd,ehd->semh", grad_recv, down_weight, preferred_element_type=f32)
    gelu_value, gelu_back = jax.vjp(jax.nn.gelu, hidden_pre)
    grad_pre = gelu_back(grad_act)[0].astype(bf16)
    up_local = jnp.einsum("semd,semh->edh", received, grad_pre, preferred_element_type=f32)
    grad_in = jnp.einsum("semh,edh->semd", grad_pre, up_weight, preferred_element_type=f32).astype(
        bf16
    )
    grad_back = lax.all_to_all(
        grad_in.reshape(owners, exp_local * capacity, width),
        "expert",
        split_axis=0,
        concat_axis=0,
        tiled=True,
    )
    grad_copies = (
        grad_back.reshape(total_slots, width)[fetch].reshape(seq_len, top_ffn, width).astype(f32)
    )
    grad_residual = grad_final + jnp.einsum("t,tkd->td", validity, grad_copies)
    sig_grad = grad_gate * ffn_sig * (1.0 - ffn_sig)
    dense_select = jnp.sum(
        jnp.where(ffn_routes[:, :, None] == jnp.arange(EXPERTS), sig_grad[:, :, None], 0.0), axis=1
    ).astype(bf16)
    ffn_selector_local = jnp.einsum("td,te->de", act_ffn, dense_select, preferred_element_type=f32)
    grad_norm_ffn = jnp.einsum("te,de->td", dense_select, ffn_selector, preferred_element_type=f32)
    ffn_gain_local = jnp.sum(grad_norm_ffn * hat_ffn, axis=0)
    ffn_shift_local = jnp.sum(grad_norm_ffn, axis=0)
    grad_residual = grad_residual + norm_backward(grad_norm_ffn, hat_ffn, inv_ffn, ffn_gain)
    grad_att_low = grad_residual.astype(bf16)
    output_local = jnp.einsum("tc,td->cd", mixed_rows, grad_att_low, preferred_element_type=f32)
    grad_mixed = jnp.einsum("td,cd->tc", grad_att_low, output_weight, preferred_element_type=f32)
    grad_mixed = grad_mixed.reshape(seq_len, heads, att_experts, head_dim)
    grad_attended = jnp.sum(out_gates[..., None] * grad_mixed, axis=2).astype(bf16)
    grad_out_gates = jnp.sum(grad_mixed * attended[:, :, None, :], axis=-1)
    out_select = (
        jnp.where(out_pick, grad_out_gates * out_sig * (1.0 - out_sig), 0.0)
        .reshape(seq_len, -1)
        .astype(bf16)
    )
    grad_weights = jnp.einsum("qhd,khd->hqk", grad_attended, values_low, preferred_element_type=f32)
    row_delta = jnp.sum(weights_p * grad_weights, axis=-1, keepdims=True)
    grad_scores = (weights_p * (grad_weights - row_delta)).astype(bf16)
    grad_queries = (
        (jnp.einsum("hqk,khd->qhd", grad_scores, key_rows, preferred_element_type=f32) * scaling)
        .reshape(seq_len, -1)
        .astype(bf16)
    )
    grad_keys = (
        (jnp.einsum("hqk,qhd->khd", grad_scores, queries, preferred_element_type=f32) * scaling)
        .reshape(seq_len, -1)
        .astype(bf16)
    )
    grad_values = jnp.einsum(
        "hqk,qhd->khd", weights_low, grad_attended, preferred_element_type=f32
    ).astype(bf16)
    grad_values_float = grad_values.astype(f32)
    grad_projected = (
        (value_gates[..., None] * grad_values_float[:, :, None, :])
        .reshape(seq_len, -1)
        .astype(bf16)
    )
    grad_value_gates = jnp.sum(grad_values_float[:, :, None, :] * projected, axis=-1)
    value_select = (
        jnp.where(value_pick, grad_value_gates * value_sig * (1.0 - value_sig), 0.0)
        .reshape(seq_len, -1)
        .astype(bf16)
    )
    value_local = jnp.einsum("td,tc->dc", layer_input, grad_projected, preferred_element_type=f32)
    query_local = jnp.einsum("td,tc->dc", act_att, grad_queries, preferred_element_type=f32)
    key_local = jnp.einsum("td,tc->dc", act_att, grad_keys, preferred_element_type=f32)
    value_selector_local = jnp.einsum(
        "td,tc->dc", act_att, value_select, preferred_element_type=f32
    )
    output_selector_local = jnp.einsum("td,tc->dc", act_att, out_select, preferred_element_type=f32)
    grad_norm_att = jnp.einsum("tc,dc->td", grad_queries, query_weight, preferred_element_type=f32)
    grad_norm_att = grad_norm_att + jnp.einsum(
        "tc,dc->td", grad_keys, key_weight, preferred_element_type=f32
    )
    grad_norm_att = grad_norm_att + jnp.einsum(
        "tc,dc->td", value_select, value_selector, preferred_element_type=f32
    )
    grad_norm_att = grad_norm_att + jnp.einsum(
        "tc,dc->td", out_select, output_selector, preferred_element_type=f32
    )
    att_gain_local = jnp.sum(grad_norm_att * hat_att, axis=0)
    att_shift_local = jnp.sum(grad_norm_att, axis=0)
    input_grad = grad_residual + jnp.einsum(
        "tc,dc->td", grad_projected, value_weight, preferred_element_type=f32
    )
    input_grad = input_grad + norm_backward(grad_norm_att, hat_att, inv_att, att_gain)
    reduced = (
        lax.psum_scatter(att_gain_local, ("dp", "expert"), scatter_dimension=0, tiled=True),
        lax.psum_scatter(att_shift_local, ("dp", "expert"), scatter_dimension=0, tiled=True),
        lax.psum_scatter(query_local, ("dp", "expert"), scatter_dimension=0, tiled=True),
        lax.psum_scatter(key_local, ("dp", "expert"), scatter_dimension=0, tiled=True),
        lax.psum_scatter(value_local, ("dp", "expert"), scatter_dimension=0, tiled=True),
        lax.psum_scatter(output_local, ("dp", "expert"), scatter_dimension=1, tiled=True),
        lax.psum_scatter(value_selector_local, ("dp", "expert"), scatter_dimension=0, tiled=True),
        lax.psum_scatter(output_selector_local, ("dp", "expert"), scatter_dimension=0, tiled=True),
        lax.psum_scatter(ffn_gain_local, ("dp", "expert"), scatter_dimension=0, tiled=True),
        lax.psum_scatter(ffn_shift_local, ("dp", "expert"), scatter_dimension=0, tiled=True),
        lax.psum_scatter(ffn_selector_local, ("dp", "expert"), scatter_dimension=0, tiled=True),
    )
    up_grad, down_grad = (
        lax.psum_scatter(
            up_local.astype(jnp.bfloat16), "dp", scatter_dimension=1, tiled=True
        ).astype(jnp.float32),
        lax.psum_scatter(
            down_local.astype(jnp.bfloat16), "dp", scatter_dimension=2, tiled=True
        ).astype(jnp.float32),
    )
    return (
        output,
        input_grad,
        reduced[0],
        reduced[1],
        reduced[2],
        reduced[3],
        reduced[4],
        reduced[5],
        reduced[6],
        reduced[7],
        reduced[8],
        reduced[9],
        reduced[10],
        up_grad,
        down_grad,
        counts_all[:EXPERTS],
    )


def mm(a, b, ca, cb):
    return lax.dot_general(a, b, (((ca,), (cb,)), ((), ())), preferred_element_type=f32)


def iota(shape, dim):
    return lax.broadcasted_iota(jnp.int32, shape, dim)


def centre(values):
    centred = values - jnp.mean(values, axis=-1, keepdims=True)
    inverse = lax.rsqrt(jnp.mean(centred * centred, axis=-1, keepdims=True) + EPSILON)
    return centred * inverse, inverse


def centre_back(upstream, normed, inverse, gain):
    scaled = upstream * gain
    mean = jnp.mean(scaled, axis=-1, keepdims=True)
    slope = jnp.mean(scaled * normed, axis=-1, keepdims=True)
    return inverse * (scaled - mean - normed * slope)


def device_of(ids, s, x):
    return 2 * s + (ids[1] + x - 2 * ids[1] * x)


SHORT = pl.CostEstimate(flops=1, bytes_accessed=1, transcendentals=0)


LONG = pl.CostEstimate(flops=1, bytes_accessed=1 << 28, transcendentals=0)


def call(body, outs, args, scratch=(), smem=(), name=None, cost=SHORT):
    return pl.pallas_call(
        body,
        out_shape=[jax.ShapeDtypeStruct(s, d) for s, d in outs],
        in_specs=[pl.BlockSpec(memory_space=pltpu.SMEM)] * len(smem)
        + [pl.BlockSpec(memory_space=pltpu.VMEM)] * len(args),
        out_specs=[pl.BlockSpec(memory_space=pltpu.VMEM)] * len(outs),
        scratch_shapes=list(scratch),
        compiler_params=pltpu.CompilerParams(vmem_limit_bytes=VMEM_LIMIT),
        cost_estimate=cost,
        name=name,
    )(*smem, *args)


def forward_body(
    length, li, vroutes, oroutes, froutes, att_gain, att_shift, wq, wk, wv, wo, vsel, osel,
    ffn_gain, ffn_shift, fsel,
    h1_o, xpack_o, q_o, k_o, v_o, p_o, a_o, o_o, gt_o, a1_o, a2_o, mixed,
):
    T, D = li.shape
    heads = vroutes.shape[0]
    dh = wq.shape[1] // heads
    ea = wv.shape[1] // (heads * dh)
    he = heads * ea
    top = froutes.shape[0]
    routes = [vroutes[h] for h in range(heads)] + [oroutes[h] for h in range(heads)] + [froutes[...]]
    routes = jnp.concatenate([r.astype(f32) for r in routes], axis=0)
    routes = jnp.concatenate([routes, jnp.zeros((128 - routes.shape[0], T), f32)], axis=0).T.astype(jnp.int32)
    scaling = 1.0 / math.sqrt(dh)
    x = li[...].astype(f32)
    hat, inv = centre(x)
    mean = jnp.mean(x, axis=-1, keepdims=True)
    a1 = (hat * att_gain[...] + att_shift[...]).astype(bf16)
    a1_o[...] = a1
    logits = jnp.concatenate(
        [mm(a1, vsel[...], 1, 1), mm(a1, osel[...], 1, 1), jnp.zeros((T, 128 - 2 * he), f32)], axis=1
    )
    lane = iota((T, 128), 1)
    chosen = jnp.zeros((T, 128), jnp.bool_)
    for j in range(2 * heads):
        h = j // 2
        chosen |= lane == routes[:, j : j + 1] + h * ea
        chosen |= lane == routes[:, 2 * heads + j : 2 * heads + j + 1] + (he + h * ea)
    gt = jnp.where(chosen, jax.nn.sigmoid(logits), 0.0)
    gt_o[...] = jnp.where(lane == 2 * he, mean, jnp.where(lane == 2 * he + 1, inv, gt))
    q = mm(a1, wq[...], 1, 0).astype(bf16)
    k = mm(a1, wk[...], 1, 0).astype(bf16)
    q_o[...] = q
    k_o[...] = k
    n_live = length[0]
    row, col = iota((T, T), 0), iota((T, T), 1)
    causal = (col <= row) & (col < n_live)
    width = ea * dh
    for h in range(heads):
        proj = mm(li[...], wv[:, h * width : (h + 1) * width], 1, 0)
        p_o[:, h * width : (h + 1) * width] = proj
        v = jnp.zeros((T, dh), f32)
        for e in range(ea):
            v += gt[:, h * ea + e : h * ea + e + 1] * proj[:, e * dh : (e + 1) * dh]
        v = v.astype(bf16)
        v_o[:, h * dh : (h + 1) * dh] = v
        s = mm(q[:, h * dh : (h + 1) * dh], k[:, h * dh : (h + 1) * dh], 1, 1) * scaling
        s = jnp.where(causal, s, NEGATIVE)
        ex = jnp.exp(s - jnp.max(s, axis=-1, keepdims=True))
        a = ex / jnp.sum(ex, axis=-1, keepdims=True)
        a_o[h] = a
        o = mm(a.astype(bf16), v, 1, 0)
        o_o[:, h * dh : (h + 1) * dh] = o
        for e in range(ea):
            c = he + h * ea + e
            mixed[:, (h * ea + e) * dh : (h * ea + e + 1) * dh] = (gt[:, c : c + 1] * o).astype(bf16)
    h1 = x + mm(mixed[...], wo[...], 1, 0)
    h1_o[...] = h1
    hat2, _ = centre(h1)
    a2 = (hat2 * ffn_gain[...] + ffn_shift[...]).astype(bf16)
    a2_o[...] = a2
    sig = jax.nn.sigmoid(mm(a2, fsel[...], 1, 1))
    wide = iota(sig.shape, 1)
    g = jnp.zeros((T, 128), f32)
    for i in range(top):
        c = 4 * heads + i
        one = jnp.sum(jnp.where(wide == routes[:, c : c + 1], sig, 0.0), axis=-1, keepdims=True)
        g = jnp.where(lane == i, one, g)
    g = g.T[:16]
    hi = g.astype(bf16)
    low = h1.astype(bf16)
    for s in range(xpack_o.shape[0]):
        xpack_o[s, :T] = low
        xpack_o[s, T:] = jnp.zeros((16, D), bf16)
        xpack_o[s, T:, :128] = hi
        xpack_o[s, T:, 128:256] = (g - hi.astype(f32)).astype(bf16)


def take_slices(v, n_p, S, e):
    D = v.shape[1]
    w = D // (n_p * S)
    return jnp.concatenate(
        [v[:, (b * S + e) * w : (b * S + e + 1) * w] for b in range(n_p)], axis=1
    )


def views(mine, theirs):
    return [r.at[s] for s in range(mine.shape[0]) for r in (mine, theirs)]


def views_from(ids, mine, theirs):
    return [r.at[ids[0] ^ s] for s in range(mine.shape[0]) for r in (mine, theirs)]


def early_body(n_p, S, ids, li, a1, a2, o, gt, *rest):
    msgs, scratch = rest
    msgs = [msgs.at[s] for s in range(S // 2)]
    hd = o.shape[1]
    for e in range(S):
        for i, v in enumerate((li, a1, a2)):
            scratch[e, :, i * 128 : (i + 1) * 128] = take_slices(v[...].astype(f32), n_p, S, e).astype(bf16)
    hi = gt[...].astype(bf16).astype(f32)
    both = (hi + pltpu.roll(gt[...] - hi, 64, 1)).astype(bf16)
    for s, m in enumerate(msgs):
        m[:, :hd] = o[...].astype(bf16)
        m[:, hd : hd + 128] = both
        m[:, hd + 128 : hd + 512] = scratch[device_of(ids, s, 1)]
        m[:, hd + 512 : hd + 896] = scratch[device_of(ids, s, 0)]


def codes_body(S, ids, *refs):
    c, (code_o, cnt_o, routes_o) = views_from(ids, *refs[:2]), refs[2:]
    ep = cnt_o.shape[1]
    T = code_o.shape[2] // 2
    strict = (iota((T, T), 0) < iota((T, T), 1)).astype(f32).astype(bf16)
    e_id = iota((ep, T), 0).astype(f32)
    cnt = jnp.zeros((8, ep), f32)
    start = ids[3].astype(f32)
    for k in range(S):
        r = c[k][:, :T].astype(f32) * 32.0 + c[k][:, T:].astype(f32)
        routes_o[k * 16 : (k + 1) * 16, :] = r
        r -= start
        mask = jnp.zeros((ep, T), f32)
        for i in range(r.shape[0]):
            mask = jnp.where(r[i : i + 1] == e_id, 1.0, mask)
        low = mask.astype(bf16)
        rank = mm(low, strict, 1, 0) + (MOST * (k % 2))
        cnt += mm(jnp.ones((8, T), bf16), low, 1, 1)
        code_o[k // 2, :, (k % 2) * T : (k % 2 + 1) * T] = jnp.where(mask > 0.5, rank, -1.0).astype(bf16)
    cnt_o[...] = cnt


def columns_body(n_p, order, ids, x, *refs):
    outs = refs[-n_p:]
    T = x.shape[1] - 16
    wide = outs[0].shape[2]
    for k in range(x.shape[0]):
        rows = x.at[ids[0] ^ k if order else k]
        for s in range(n_p):
            at = pl.multiple_of((ids[2] ^ s) * wide, 128)
            outs[s][k, :T, :] = rows[:T, pl.ds(at, wide)]
    if len(refs) > n_p:
        for s in range(n_p):
            outs[s][:, T:, :] = refs[0][...]


def gelu_both(u):
    t = jnp.tanh(GELU_A * (u + GELU_B * u * u * u))
    value = 0.5 * u * (1.0 + t)
    slope = 0.5 * (1.0 + t) + 0.5 * u * (1.0 - t * t) * (GELU_A * (1.0 + 3.0 * GELU_B * u * u))
    return value, slope


def experts_body(S, eb, ids, *refs):
    x, c = views(*refs[:2]), views_from(ids, *refs[2:4])
    code, up, down, dx0, dx1, gy0, gy1, gr_o, du_o, ct, gts, dl, ps, xs, cs, gys, dxs = refs[4:]
    step = pl.program_id(0)
    pairs = S // 2
    R = 2 * MOST
    T = x[0].shape[0] - 16
    D = x[0].shape[1]
    ep = ct.shape[1]
    rows = pairs * R
    H = up.shape[2]

    @pl.when(step == 0)
    def _():
        e_id = iota((ep, T), 0).astype(f32)
        start = ids[3].astype(f32)
        dl[...] = jnp.zeros_like(dl)
        for pr in range(pairs):
            ct[pr] = code[pr].astype(f32)
        for k in range(S):
            r = c[k][T:, :T].astype(f32) * 32.0 + c[k][T:, T : 2 * T].astype(f32) - start
            g = x[k][T:, :T].astype(f32) + x[k][T:, T : 2 * T].astype(f32)
            dense = jnp.zeros((ep, T), f32)
            for i in range(r.shape[0]):
                dense = jnp.where(r[i : i + 1] == e_id, g[i : i + 1], dense)
            gts[:, k * T : (k + 1) * T] = dense

    slot = iota((R, 2 * T), 0).astype(f32)
    g_slot = [[None] * pairs for _ in range(eb)]
    onehot = [[None] * pairs for _ in range(eb)]
    for pr in range(pairs):
        blocks = []
        for j in range(eb):
            e = step * eb + j
            hot = jnp.where(ct[pr, pl.ds(e, 1), :] == slot, 1.0, 0.0)
            onehot[j][pr] = hot
            g_slot[j][pr] = jnp.sum(
                hot * gts[pl.ds(e, 1), pr * 2 * T : (pr + 1) * 2 * T], axis=-1, keepdims=True
            )
            blocks.append(hot.astype(bf16))
        block = jnp.concatenate(blocks, axis=0)
        ps[pr, pl.ds(pl.multiple_of(step * (eb * R), R), eb * R), :] = block
        for src, dst in ((x, xs), (c, cs)):
            both = jnp.concatenate([src[2 * pr][:T], src[2 * pr + 1][:T]], axis=0)
            got = mm(block, both, 1, 0).astype(bf16)
            for j in range(eb):
                dst[j * rows + pr * R : j * rows + (pr + 1) * R, :] = got[j * R : (j + 1) * R]
    units = [list(range(first, min(first + 2, eb))) for first in range(0, eb, 2)]
    every = range(len(units))
    spans = [slice(js[0] * rows, (js[-1] + 1) * rows) for js in units]

    def own(v, n):
        return jnp.concatenate([v[i * rows : (i + 1) * rows, i * H : (i + 1) * H] for i in range(n)], axis=0)

    def spread_out(v, n):
        if n == 1:
            return v
        zero = jnp.zeros((rows, H), v.dtype)
        return jnp.concatenate(
            [
                jnp.concatenate([v[i * rows : (i + 1) * rows] if i == b else zero for b in range(n)], axis=1)
                for i in range(n)
            ],
            axis=0,
        )

    gs = [jnp.concatenate([p for j in js for p in g_slot[j]], axis=0) for js in units]
    ups = [jnp.concatenate([up[j] for j in js], axis=1) for js in units]
    downs = [jnp.concatenate([down[j] for j in js], axis=0) for js in units]
    us = [own(mm(xs[spans[m], :], ups[m], 1, 0), len(units[m])) for m in every]
    drs = [
        own(mm((gs[m] * cs[spans[m], :].astype(f32)).astype(bf16), downs[m], 1, 1), len(units[m])) for m in every
    ]
    dus, rs = [], []
    for m in every:
        value, slope = gelu_both(us[m])
        rs.append(value.astype(bf16))
        dus.append((drs[m] * slope).astype(bf16))
    ys = [mm(spread_out(rs[m], len(units[m])), downs[m], 1, 0).astype(bf16) for m in every]
    dxu = [mm(spread_out(dus[m], len(units[m])), ups[m], 1, 1).astype(bf16) for m in every]
    for m in every:
        js = units[m]
        g = gs[m]
        r, du = rs[m], dus[m]
        y, dx = ys[m].astype(f32), dxu[m]
        dgate = jnp.sum(cs[spans[m], :].astype(f32) * y, axis=-1, keepdims=True)
        gy = (g * y).astype(bf16)
        gr = (g * r.astype(f32)).astype(bf16)
        dlog = dgate * g * (1.0 - g)
        for i, j in enumerate(js):
            e = step * eb + j
            gr_o[j] = gr[i * rows : (i + 1) * rows]
            du_o[j] = du[i * rows : (i + 1) * rows]
            for pr in range(pairs):
                at = pl.ds(pl.multiple_of(step * (eb * R) + j * R, R), R)
                cut = slice(i * rows + pr * R, i * rows + (pr + 1) * R)
                gys[pr, at, :] = gy[cut]
                dxs[pr, at, :] = dx[cut]
                dl[pl.ds(e, 1), pr * 2 * T : (pr + 1) * 2 * T] = jnp.sum(
                    onehot[j][pr] * dlog[cut], axis=0, keepdims=True
                )

    @pl.when(step == pl.num_programs(0) - 1)
    def _():
        for pr in range(pairs):
            for src, d0, d1 in ((dxs, dx0, dx1), (gys, gy0, gy1)):
                got = mm(ps[pr], src[pr], 0, 0).astype(bf16)
                d0[pr, :T] = got[:T]
                d1[pr, :T] = got[T:]
            for x_i, d in ((0, dx0), (1, dx1)):
                k = 2 * pr + x_i
                part = dl[:, k * T : (k + 1) * T].astype(bf16)
                d[pr, T:] = jnp.zeros((16, D), bf16)
                for b in range(ep // 16):
                    d[pr, T:, b * T : (b + 1) * T] = part[16 * b : 16 * b + 16]


def join_body(T, mine, recv, out):
    half = mine.shape[2] // 2
    for s in range(mine.shape[0]):
        out[s, :T] = (mine[s, :T].astype(f32) + recv[s, :T].astype(f32)).astype(bf16)
        if mine.shape[1] > T:
            out[s, T:, :half] = mine[s, T:, :half]
            out[s, T:, half:] = recv[s, T:, :half]


def join_apart_body(nz, ids, mine, recv, *outs):
    for s in range(nz):
        outs[s][...] = (mine[ids[0] ^ s].astype(f32) + recv[ids[0] ^ s].astype(f32)).astype(bf16)


def ffn_back_body(n_p, S, nz, ids, parts, h1, c, fsel, gain, froutes, cnt, dh1_o, db_o, mid_o, dlt, sl):
    T, D = h1.shape
    ep = dlt.shape[0] // S
    half = D // 2
    dxs = parts[0, :T].astype(f32)
    for s in range(1, nz):
        dxs += parts[s, :T].astype(f32)
    for s in range(nz):
        for x in range(2):
            for b in range(ep // 16):
                at = pl.multiple_of(device_of(ids, s, x) * ep + 16 * b, 16)
                dlt[pl.ds(at, 16), :] = parts[s, T:, x * half + b * T : x * half + (b + 1) * T].astype(f32)
    dl = dlt[...].T
    da2 = mm(dl.astype(bf16), fsel[...], 1, 0)
    hat, inv = centre(h1[...])
    dh1 = c[...].astype(f32) + dxs + centre_back(da2, hat, inv, gain[...])
    dh1_o[...] = dh1
    db = dh1.astype(bf16)
    db_o[...] = db
    low = db.astype(f32)
    for e in range(S):
        sl[e] = take_slices(low, n_p, S, e).astype(bf16)
    slot = iota(dlt.shape, 0)
    few = [
        jnp.sum(jnp.where(slot == froutes[i : i + 1, :], dlt[...], 0.0), axis=0, keepdims=True)
        for i in range(froutes.shape[0])
    ]
    few = jnp.concatenate(few, axis=0).astype(bf16)
    hi = cnt[...].astype(bf16)
    lo = (cnt[...] - hi.astype(f32)).astype(bf16)
    vectors = []
    for v in (jnp.sum(da2 * hat, axis=0, keepdims=True), jnp.sum(da2, axis=0, keepdims=True)):
        high = v.astype(bf16).astype(f32)
        for part in (high, v - high):
            vectors += [part[:, b * 256 : (b + 1) * 256] for b in range(D // 256)]
    vectors = jnp.concatenate(vectors, axis=0).astype(bf16)
    for s in range(nz):
        m = mid_o.at[s]
        m[:T, :128] = sl[device_of(ids, s, 1)]
        m[:T, 128:] = sl[device_of(ids, s, 0)]
        m[T : T + 16, :T] = few
        m[T : T + 16, T:] = jnp.zeros((16, 256 - T), bf16)
        m[T : T + 16, T : T + ep] = jnp.concatenate([hi, lo], axis=0)
        m[T + 16 :] = vectors


def attention_back_body(db, wo, gt, o, q, k, v, a, p, late_o, dp_o):
    T, D = db.shape
    heads = a.shape[0]
    dh = q.shape[1] // heads
    ea = p.shape[1] // (heads * dh)
    he, hd = heads * ea, heads * dh
    width = ea * dh
    scaling = 1.0 / math.sqrt(dh)
    gates = gt[...]
    lane = iota((T, 128), 1)
    every = range(heads)
    hs = [slice(h * dh, (h + 1) * dh) for h in every]
    dz = [mm(db[...], wo[h * width : (h + 1) * width, :], 1, 1) for h in every]
    do = []
    for h in every:
        total = jnp.zeros((T, dh), f32)
        for e in range(ea):
            c = he + h * ea + e
            total += gates[:, c : c + 1] * dz[h][:, e * dh : (e + 1) * dh]
        do.append(total.astype(bf16))
    da = [mm(do[h], v[:, hs[h]], 1, 1) for h in every]
    dv = [mm(a[h].astype(bf16), do[h], 0, 0).astype(bf16) for h in every]
    ds = [(a[h] * (da[h] - jnp.sum(a[h] * da[h], axis=-1, keepdims=True))).astype(bf16) for h in every]
    dq = [(mm(ds[h], k[:, hs[h]], 1, 0) * scaling).astype(bf16) for h in every]
    dk = [(mm(ds[h], q[:, hs[h]], 0, 0) * scaling).astype(bf16) for h in every]
    dgates = jnp.zeros((T, 128), f32)
    for h in every:
        oh, dvf = o[:, hs[h]], dv[h].astype(f32)
        for e in range(ea):
            c = h * ea + e
            es = slice(c * dh, (c + 1) * dh)
            dp_o[:, es] = (gates[:, c : c + 1] * dvf).astype(bf16)
            out_sum = jnp.sum(dz[h][:, e * dh : (e + 1) * dh] * oh, axis=-1, keepdims=True)
            in_sum = jnp.sum(dvf * p[:, es], axis=-1, keepdims=True)
            dgates = jnp.where(lane == he + c, out_sum, jnp.where(lane == c, in_sum, dgates))
    sel = (dgates * gates * (1.0 - gates)).astype(bf16)
    for s in range(late_o.shape[0]):
        for h in every:
            late_o[s, :, hs[h]] = dv[h]
            late_o[s, :, hd + h * dh : hd + (h + 1) * dh] = dq[h]
            late_o[s, :, 2 * hd + h * dh : 2 * hd + (h + 1) * dh] = dk[h]
        late_o[s, :, 3 * hd :] = sel


def input_back_body(late, dp, wq, wk, wv, selw, li, gain, dh1, ig_o):
    hd = wq.shape[1]
    da1 = mm(late[0, :, hd : 2 * hd], wq[...], 1, 1)
    da1 += mm(late[0, :, 2 * hd : 3 * hd], wk[...], 1, 1)
    da1 += mm(late[0, :, 3 * hd :], selw[...], 1, 1)
    hat, inv = centre(li[...].astype(f32))
    ig_o[...] = dh1[...] + mm(dp[...], wv[...], 1, 1) + centre_back(da1, hat, inv, gain[...])


def spread(values, gates, lo, heads, ea, dh):
    return jnp.concatenate(
        [
            (gates[:, lo + h * ea + e : lo + h * ea + e + 1] * values[:, h * dh : (h + 1) * dh]).astype(bf16)
            for h in range(heads)
            for e in range(ea)
        ],
        axis=1,
    )


def spread_body(S, n_p, w, heads, ea, ids, e0, e1, wq, wk, selw, z_o, a2_o, lia1_o, hat_o, gates_o, wsl_o):
    early = views(e0, e1)
    T = early[0].shape[0]
    D, hd = wq.shape
    for b in range(n_p):
        at = pl.ds(pl.multiple_of(b * (D // n_p) + (2 * ids[0] + ids[1]) * w, 16), w)
        bs = slice(b * w, (b + 1) * w)
        wsl_o[bs, :hd] = wq[at, :]
        wsl_o[bs, hd : 2 * hd] = wk[at, :]
        wsl_o[bs, 2 * hd :] = selw[at, :]
    for k in range(S):
        ts = slice(k * T, (k + 1) * T)
        m = early[k]
        both = m[:, hd : hd + 128].astype(f32)
        gates = both + pltpu.roll(both, 64, 1)
        gates_o[ts, :] = gates
        z_o[ts, :] = spread(m[:, :hd].astype(f32), gates, heads * ea, heads, ea, hd // heads)
        at = hd + 512 if k % 2 == 0 else hd + 128
        li = m[:, at : at + 128].astype(f32)
        he2 = 2 * heads * ea
        lia1_o[:128, ts] = li.T.astype(bf16)
        lia1_o[128:, ts] = m[:, at + 128 : at + 256].astype(f32).T.astype(bf16)
        hat_o[:, ts] = ((li - gates[:, he2 : he2 + 1]) * gates[:, he2 + 1 : he2 + 2]).T
        a2_o[ts, :] = m[:, at + 256 : at + 384]


def out_rows(acc, outs, ids, w):
    for s, ref in enumerate(outs):
        plane = ids[2] ^ s
        ref[:, : acc.shape[1]] = acc[pl.ds(pl.multiple_of(plane * w, 8), w), :].astype(ref.dtype)


def out_grads_body(S, n_p, w, ids, m0, m1, z, a2, routes, *refs):
    mid, outs = views(m0, m1), refs[:n_p]
    acc, lhs, dlt, cnt = refs[n_p:]
    T = z.shape[0] // S
    EP = dlt.shape[0]
    e_id = iota((EP, T), 0).astype(f32)
    norms = jnp.zeros((16, 256), f32)
    for k in range(S):
        n = mid[k]
        ts = slice(k * T, (k + 1) * T)
        at = 128 if k % 2 == 0 else 0
        lhs[ts, :] = n[:T, at : at + 128]
        few = n[T : T + 16, :T].astype(f32)
        route = routes[k * 16 : (k + 1) * 16, :]
        dense = jnp.zeros((EP, T), f32)
        for i in range(16):
            dense = jnp.where(route[i : i + 1] == e_id, few[i : i + 1], dense)
        dlt[:, ts] = dense.astype(bf16)
        tally = n[T : T + 16, T:].astype(f32)
        at = device_of(ids, k // 2, k % 2)
        cnt[pl.ds(at, 1), :] = tally[:1]
        cnt[pl.ds(at + 8, 1), :] = tally[8:9]
        norms += n[T + 16 :].astype(f32)
    wide = z.shape[1]
    acc[:, :wide] = mm(lhs[...], z[...], 0, 0)
    acc[:, wide:] = mm(dlt[...], a2[...], 1, 0).T
    out_rows(acc, outs, ids, w)
    norms = pltpu.roll(norms, lax.rem(256 - (2 * ids[0] + ids[1]) * w, 256), 1)
    norms = jnp.concatenate([norms[0:4] + norms[4:8], norms[8:12] + norms[12:16]], axis=0)
    extra = jnp.concatenate([cnt[...], norms[:, :128], jnp.zeros((w - 24, 128), f32)], axis=0)
    for ref in outs:
        ref[:, acc.shape[1] :] = extra.astype(ref.dtype)


def in_grads_body(n_p, heads, ea, w, hd, ids, l0, l1, lia1, hat, gates, wsl, *refs):
    outs, (acc, rhs, qk, sums) = refs[:n_p], refs[n_p:]
    step = pl.program_id(0)
    T = l0.shape[1]
    wide = rhs.shape[1]

    @pl.when(step == 0)
    def _():
        acc[...] = jnp.zeros_like(acc)
        sums[...] = jnp.zeros_like(sums)

    for x, n in enumerate((l0, l1)):
        ts = slice(x * T, (x + 1) * T)
        rhs[ts, :] = spread(n[0, :, :hd].astype(f32), gates[ts, :], 0, heads, ea, hd // heads)
        qk[ts, :] = n[0, :, hd:]
    acc[:, :wide] += mm(lia1[:128, :], rhs[...], 1, 0)
    acc[:, wide:] += mm(lia1[128:, :], qk[...], 1, 0)
    da1 = mm(wsl[...], qk[...], 1, 1)
    gain = jnp.sum(da1 * hat[...], axis=1, keepdims=True)
    shift = jnp.sum(da1, axis=1, keepdims=True)
    lane = iota((128, 128), 1)
    sums[...] += jnp.where(lane == 64, gain, jnp.where(lane == 65, shift, 0.0))

    @pl.when(step == pl.num_programs(0) - 1)
    def _():
        acc[:, wide + 2 * hd :] += sums[...]
        out_rows(acc, outs, ids, w)


def last_a_body(n_p, S, w, el, ids, *refs):
    parts, (og_o, fg_o, gain_o, shift_o, counts_o, rows) = refs[:n_p], refs[n_p:]
    total = parts[0][...]
    for m in parts[1:]:
        total += m[...].astype(f32)
    wide = og_o.shape[1]
    og_o[...] = total[:w, :wide]
    ep = (total.shape[1] - 128 - wide) // S
    sel = total[:, wide:]
    fg_o[...] = jnp.concatenate([sel[:, e * ep : e * ep + el] for e in range(S)], axis=1)[:, : fg_o.shape[1]]
    extra = total[:, wide + S * ep :]
    rows[...] = extra[16:24]
    gain_o[...] = rows[pl.ds(ids[2], 1), :w]
    shift_o[...] = rows[pl.ds(ids[2] + n_p, 1), :w]
    cnt = extra[0:8] + extra[8:16]
    counts_o[...] = jnp.concatenate([cnt[e : e + 1, :el] for e in range(S)], axis=1)[:, : counts_o.shape[1]]


def last_b_body(n_p, w, hd, he, *refs):
    parts, (vg_o, qg_o, kg_o, vs_o, os_o, gain_o, shift_o) = refs[:n_p], refs[n_p:]
    total = parts[0][...]
    for m in parts[1:]:
        total += m[...].astype(f32)
    wide = vg_o.shape[1]
    vg_o[...] = total[:w, :wide]
    qg_o[...] = total[:w, wide : wide + hd]
    kg_o[...] = total[:w, wide + hd : wide + 2 * hd]
    sel = total[:w, wide + 2 * hd :].T
    vs_o[...] = sel[:he]
    os_o[...] = sel[he : 2 * he]
    gain_o[...] = sel[64:65]
    shift_o[...] = sel[65:66]


def expert_grads_body(n_p, eb, first, xm, xo, cm, co, *refs):
    gr_in, du_in = refs[:n_p], refs[n_p : 2 * n_p]
    up_o, down_o, ct, got = refs[-4:]
    start = pl.program_id(0)
    step = start + first
    _, pairs, T, wide = cm.shape
    T2 = 2 * T
    R = 2 * MOST
    rows = pairs * R

    @pl.when(start == 0)
    def _():
        for s in range(n_p):
            for pr in range(pairs):
                ct[s * pairs + pr] = xm[s, pr, T:, :].astype(f32)

    slot = iota((R, T2), 0).astype(f32)
    for s in range(n_p):
        for pr in range(pairs):
            block = jnp.concatenate(
                [
                    jnp.where(ct[s * pairs + pr, pl.ds(step * eb + j, 1), :] == slot, 1.0, 0.0).astype(bf16)
                    for j in range(eb)
                ],
                axis=0,
            )
            both = jnp.concatenate(
                [jnp.concatenate([x[s, pr, :T], c[s, pr]], axis=1) for x, c in ((xm, cm), (xo, co))], axis=0
            )
            res = mm(block, both, 1, 0).astype(bf16)
            for j in range(eb):
                at = j * n_p * rows + s * rows + pr * R
                got[at : at + R, :] = res[j * R : (j + 1) * R]
    for j in range(eb):
        at = j * n_p * rows
        xj = got[at : at + n_p * rows, :wide]
        cj = got[at : at + n_p * rows, wide:]
        gr = jnp.concatenate([gr_in[s][j] for s in range(n_p)], axis=0)
        du = jnp.concatenate([du_in[s][j] for s in range(n_p)], axis=0)
        up_o[j] = mm(xj, du, 0, 0)
        down_o[j] = mm(gr, cj, 0, 0)


def after(values, *deps):
    return lax.optimization_barrier((values, deps))[0]


class Links:
    def __init__(self):
        self.n_e = lax.axis_size("expert")
        self.nz = self.n_e // 2
        self.n_p = lax.axis_size("dp")
        self.me = lax.axis_index("expert")
        self.z, self.c = self.me // 2, self.me % 2
        self.p = lax.axis_index("dp")

    def core(self, v):
        return lax.ppermute(v, "expert", [(e, e ^ 1) for e in range(self.n_e)])

    def chips(self, v):
        groups = [[2 * s + c for s in range(self.nz)] for c in range(2)]
        return lax.all_to_all(v, "expert", 0, 0, axis_index_groups=groups, tiled=True)

    def chip(self, v, s):
        return lax.ppermute(v, "expert", [(e, (e + 2 * s) % self.n_e) for e in range(self.n_e)])

    def plane(self, v, s):
        return lax.ppermute(v, "dp", [(p, p ^ s) for p in range(self.n_p)])

    def near(self, msgs):
        pairs = [[(e, e ^ (2 * s)) for e in range(self.n_e)] for s in range(self.nz)]
        return [msgs[0]] + [lax.ppermute(msgs[s], "expert", pairs[s]) for s in range(1, self.nz)]

    def relay(self, mine):
        return [mine, self.core(mine)]

    def planes_of(self, msgs):
        return [msgs[0]] + [self.plane(msgs[s], s) for s in range(1, self.n_p)]


def fast_path(
    layer_input, cotangent, lengths, value_routes, output_routes, ffn_routes, att_gain, att_shift,
    query_weight, key_weight, value_weight, output_weight, value_selector, output_selector,
    ffn_gain, ffn_shift, ffn_selector, up_weight, down_weight,
):
    L = Links()
    S, nz, n_p = L.n_e, L.nz, L.n_p
    pairs = S // 2
    T, D = layer_input.shape
    heads = value_routes.shape[1]
    dh = query_weight.shape[1] // heads
    ea = value_selector.shape[1] // heads
    hd, he, wide = heads * dh, heads * ea, heads * ea * dh
    el, _, H = up_weight.shape
    ep = -(-el // 16) * 16
    EP = ep * S
    w = D // (n_p * S)
    Dp = D // n_p
    R = 2 * MOST
    eb = max(d for d in (7, 4, 2, 1) if el % d == 0)

    ids = jnp.stack([L.z, L.c, L.p, L.me * ep]).astype(jnp.int32)
    raw = ffn_routes.T
    padded = (raw // el) * ep + raw % el

    rt = jnp.where(jnp.arange(T)[None, :] < lengths[0], padded, EP)
    tail = jnp.concatenate([rt // 32, rt % 32], axis=1).astype(bf16)
    cpack = jnp.concatenate([cotangent, jnp.pad(tail, ((0, 0), (0, D - 2 * T)))], axis=0)
    c_far = L.near([cpack] * nz)

    h1, xpack, q, k, v, proj, a, o, gt, a1, a2 = call(
        forward_body,
        [
            ((T, D), f32), ((nz, T + 16, D), bf16), ((T, hd), bf16), ((T, hd), bf16), ((T, hd), bf16),
            ((T, wide), f32), ((heads, T, T), f32), ((T, hd), f32), ((T, 128), f32),
            ((T, D), bf16), ((T, D), bf16),
        ],
        [
            layer_input, value_routes.transpose(1, 2, 0), output_routes.transpose(1, 2, 0), raw,
            att_gain[None], att_shift[None], query_weight, key_weight, value_weight, output_weight,
            value_selector.T, output_selector.T, ffn_gain[None], ffn_shift[None], ffn_selector.T,
        ],
        scratch=[pltpu.VMEM((T, wide), bf16)],
        smem=[lengths],
        name="forward",
    )
    x_far = L.chips(xpack)
    selectors = after((ffn_selector, value_selector, output_selector), xpack)
    fsel = jnp.pad(selectors[0].T, ((0, S * el - ffn_selector.shape[1]), (0, 0)))
    fsel = jnp.pad(fsel.reshape(S, el, D), ((0, 0), (0, ep - el), (0, 0))).reshape(EP, D)
    selw = jnp.pad(jnp.concatenate(selectors[1:], axis=1), ((0, 0), (0, 128 - 2 * he)))
    (early,) = call(
        partial(early_body, n_p, S),
        [((nz, T, hd + 896), bf16)],
        [layer_input, a1, a2, o, gt],
        scratch=[pltpu.VMEM((S, T, 384), bf16)],
        smem=[ids],
        name="early_slices",
    )
    c_msgs = L.relay(jnp.stack(after(c_far, early, fsel, selw)))
    ccols = call(
        partial(columns_body, n_p, True), [((nz, T, Dp), bf16)] * n_p, [after(c_msgs[0], c_msgs[1])], smem=[ids],
        name="cotangent_columns",
    )
    cc_all = [ccols[0], L.plane(ccols[1], 1), L.plane(ccols[2], 2)]
    tail_rows = pl.BlockSpec((nz, 16, 2 * T), lambda i: (0, T // 16, 0))
    code, cnt, routes = pl.pallas_call(
        partial(codes_body, S),
        grid=(1,),
        in_specs=[pl.BlockSpec(memory_space=pltpu.SMEM), tail_rows, tail_rows],
        out_specs=[pl.BlockSpec(memory_space=pltpu.VMEM)] * 3,
        out_shape=[
            jax.ShapeDtypeStruct((pairs, ep, 2 * T), bf16), jax.ShapeDtypeStruct((8, ep), f32),
            jax.ShapeDtypeStruct((S * 16, T), f32),
        ],
        compiler_params=pltpu.CompilerParams(vmem_limit_bytes=VMEM_LIMIT),
        cost_estimate=SHORT,
        name="codes",
    )(ids, *after(c_msgs, ccols))
    x_far = after(x_far, code, cc_all[1:])
    x_msgs = L.relay(x_far)
    xcols = call(
        partial(columns_body, n_p, False), [((nz, T + ep, Dp), bf16)] * n_p, [x_far, code],
        smem=[ids],
        name="token_columns",
    )
    xc_all = L.planes_of(xcols)
    early_far = L.chips(after(early, x_far))

    n_eb = el // eb
    whole = [pl.BlockSpec(memory_space=pltpu.VMEM)]
    dx0, dx1, gy0, gy1, gr, du = pl.pallas_call(
        partial(experts_body, S, eb),
        grid=(n_eb,),
        out_shape=[
            jax.ShapeDtypeStruct((pairs, T + 16, D), bf16), jax.ShapeDtypeStruct((pairs, T + 16, D), bf16),
            jax.ShapeDtypeStruct((pairs, T, D), bf16), jax.ShapeDtypeStruct((pairs, T, D), bf16),
            jax.ShapeDtypeStruct((el, pairs * R, H), bf16), jax.ShapeDtypeStruct((el, pairs * R, H), bf16),
        ],
        in_specs=[pl.BlockSpec(memory_space=pltpu.SMEM)]
        + whole * 5
        + [
            pl.BlockSpec((eb, D, H), lambda i: (i, 0, 0)),
            pl.BlockSpec((eb, H, D), lambda i: (i, 0, 0)),
        ],
        out_specs=whole * 4 + [pl.BlockSpec((eb, pairs * R, H), lambda i: (i, 0, 0))] * 2,
        scratch_shapes=[
            pltpu.VMEM((pairs, ep, 2 * T), f32), pltpu.VMEM((ep, S * T), f32), pltpu.VMEM((ep, S * T), f32),
            pltpu.VMEM((pairs, el * R, 2 * T), bf16),
            pltpu.VMEM((eb * pairs * R, D), bf16), pltpu.VMEM((eb * pairs * R, D), bf16),
            pltpu.VMEM((pairs, el * R, D), bf16), pltpu.VMEM((pairs, el * R, D), bf16),
        ],
        compiler_params=pltpu.CompilerParams(vmem_limit_bytes=VMEM_LIMIT),
        cost_estimate=SHORT,
        name="experts",
    )(after(ids, xcols), *x_msgs, *c_msgs, code, up_weight, down_weight)

    def join(mine, other, name):
        return call(partial(join_body, T), [(mine.shape, bf16)], [mine, L.core(other)], name=name)[0]

    def join_apart(mine, other, name):
        return call(
            partial(join_apart_body, nz), [(mine.shape[1:], bf16)] * nz, [mine, L.core(other)], smem=[ids], name=name
        )

    dx0, dx1, early_far, xc_all = lax.optimization_barrier((dx0, dx1, early_far, xc_all))
    dx_join = join(dx0, dx1, "join_dx")
    dx_parts = L.chips(dx_join)
    gr, du = after((gr, du), dx_join)
    gr1, du1 = L.plane(gr, 1), L.plane(du, 2)
    early_far, gy0, gy1, cc3, xc_all = after((early_far, gy0, gy1, ccols[3], xc_all), dx_join)
    xc_both = L.relay(jnp.stack(xc_all))
    cc_all += [L.plane(cc3, 3)]
    gy_join = join_apart(gy0, gy1, "join_out")
    z_all, a2_s, lia1, hat_s, gates, wsl = call(
        partial(spread_body, S, n_p, w, heads, ea),
        [
            ((S * T, wide), bf16), ((S * T, 128), bf16), ((256, S * T), bf16), ((128, S * T), f32),
            ((S * T, 128), f32), ((128, 2 * hd + 128), bf16),
        ],
        [*L.relay(early_far), query_weight, key_weight, selw],
        smem=[ids],
        cost=LONG,
        name="spread_tokens",
    )
    dx_parts, gr1, du1, z_all, gy_join, cc_all, xc_both = lax.optimization_barrier(
        (dx_parts, gr1, du1, z_all, gy_join, cc_all, xc_both)
    )
    cols_both = xc_both + L.relay(jnp.stack(cc_all))
    gr, du = after((gr, du), dx_parts)
    gr_all = [gr, gr1, L.plane(gr, 2)]
    du_all = [du, L.plane(du, 1), du1]

    dh1, db, mid = call(
        partial(ffn_back_body, n_p, S, nz),
        [((T, D), f32), ((T, D), bf16), ((nz, T + 32, 256), bf16)],
        [dx_parts, h1, cotangent, fsel, ffn_gain[None], padded, cnt],
        scratch=[pltpu.VMEM((EP, T), f32), pltpu.VMEM((S, T, 128), bf16)],
        smem=[ids],
        name="ffn_back",
    )
    mid_far = L.chips(mid)
    late, dp = call(
        attention_back_body,
        [((nz, T, 3 * hd + 128), bf16), ((T, wide), bf16)],
        [db, output_weight, gt, o, q, k, v, a, proj],
        cost=LONG,
        name="attention_back",
    )
    late = after(late, mid_far, gr_all[2], du_all[1])
    gr1, du1 = after((gr1, du1), late)
    gr_all += [L.plane(gr1, 2)]
    du_all += [L.plane(du1, 1)]
    late_far = L.chips(late)
    (input_grad,) = call(
        input_back_body,
        [((T, D), f32)],
        [late, dp, query_weight, key_weight, value_weight, selw, layer_input, att_gain[None], dh1],
        name="input_back",
    )
    mid_far = after(mid_far, input_grad)
    grads_a = call(
        partial(out_grads_body, S, n_p, w),
        [((w, wide + EP + 128), f32)] + [((w, wide + EP + 128), bf16)] * (n_p - 1),
        [*L.relay(mid_far), z_all, a2_s, routes],
        scratch=[
            pltpu.VMEM((128, wide + EP), f32), pltpu.VMEM((S * T, 128), bf16),
            pltpu.VMEM((EP, S * T), bf16), pltpu.VMEM((16, 128), f32),
        ],
        smem=[ids],
        name="out_grads",
    )
    a_parts = L.planes_of(grads_a)
    def expert_grads(first, last, args, so_far=()):
        n = len(args)
        return pl.pallas_call(
            partial(expert_grads_body, n_p, eb, first),
            grid=(last - first,),
            in_specs=whole * 4
            + [pl.BlockSpec((eb, pairs * R, H), lambda i: (i + first, 0, 0))] * (2 * n_p)
            + [pl.BlockSpec(memory_space=pl.ANY)] * len(so_far),
            out_specs=[
                pl.BlockSpec((eb, Dp, H), lambda i: (i + first, 0, 0)),
                pl.BlockSpec((eb, H, Dp), lambda i: (i + first, 0, 0)),
            ],
            scratch_shapes=[
                pltpu.VMEM((n_p * pairs, ep, 2 * T), f32),
                pltpu.VMEM((eb * n_p * pairs * R, 2 * Dp), bf16),
            ],
            out_shape=[jax.ShapeDtypeStruct((el, Dp, H), f32), jax.ShapeDtypeStruct((el, H, Dp), f32)],
            input_output_aliases={n + i: i for i in range(len(so_far))},
            compiler_params=pltpu.CompilerParams(vmem_limit_bytes=VMEM_LIMIT),
            cost_estimate=SHORT,
            name="expert_grads",
        )(*args, *so_far)

    cut = (n_eb + 1) // 2
    grads_in = (*cols_both, *after(gr_all + du_all, grads_a))
    half = expert_grads(0, cut, grads_in)
    late_far, a_parts, half = lax.optimization_barrier((late_far, a_parts, half))
    gy_parts = L.near(after(gy_join, late_far))
    late_block = pl.BlockSpec((1, T, 3 * hd + 128), lambda i: (i, 0, 0))
    grads_b = pl.pallas_call(
        partial(in_grads_body, n_p, heads, ea, w, hd),
        grid=(nz,),
        in_specs=[
            pl.BlockSpec(memory_space=pltpu.SMEM), late_block, late_block,
            pl.BlockSpec((256, 2 * T), lambda i: (0, i)), pl.BlockSpec((128, 2 * T), lambda i: (0, i)),
            pl.BlockSpec((2 * T, 128), lambda i: (i, 0)), whole[0],
        ],
        out_specs=whole * n_p,
        out_shape=[
            jax.ShapeDtypeStruct((w, wide + 2 * hd + 128), f32 if s == 0 else bf16) for s in range(n_p)
        ],
        scratch_shapes=[
            pltpu.VMEM((128, wide + 2 * hd + 128), f32), pltpu.VMEM((2 * T, wide), bf16),
            pltpu.VMEM((2 * T, 2 * hd + 128), bf16), pltpu.VMEM((128, 128), f32),
        ],
        compiler_params=pltpu.CompilerParams(vmem_limit_bytes=VMEM_LIMIT),
        cost_estimate=LONG,
        name="in_grads",
    )(ids, *L.relay(late_far), lia1, hat_s, gates, wsl)
    b_parts = L.planes_of(grads_b)
    up_grad, down_grad = expert_grads(cut, n_eb, after(grads_in, grads_b), half)

    output_grad, fgrad, ffn_gain_grad, ffn_shift_grad, counts = call(
        partial(last_a_body, n_p, S, w, el),
        [((w, wide), f32), ((w, EXPERTS), f32), ((1, w), f32), ((1, w), f32), ((1, EXPERTS), f32)],
        after(a_parts, up_grad),
        scratch=[pltpu.VMEM((8, 128), f32)],
        smem=[ids],
        name="last_sum_a",
    )
    gy_parts, b_parts = after((gy_parts, b_parts), fgrad)
    output = (h1 + sum(m.astype(f32) for m in gy_parts)).astype(bf16)
    value_grad, query_grad, key_grad, vsel, osel, att_gain_grad, att_shift_grad = call(
        partial(last_b_body, n_p, w, hd, he),
        [
            ((w, wide), f32), ((w, hd), f32), ((w, hd), f32), ((he, w), f32), ((he, w), f32),
            ((1, w), f32), ((1, w), f32),
        ],
        after(b_parts, output),
        name="last_sum_b",
    )
    return (
        output, input_grad, att_gain_grad[0], att_shift_grad[0], query_grad, key_grad, value_grad,
        output_grad.T, vsel.T, osel.T, ffn_gain_grad[0], ffn_shift_grad[0], fgrad, up_grad, down_grad, counts[0],
    )


def solution(mesh):
    path = fast_path if mesh.shape["expert"] == 8 and mesh.shape["dp"] == 4 else general_path
    placed = (
        P(("dp", "expert"), None),
        P(("dp", "expert"), None),
        P(("dp", "expert")),
        P(("dp", "expert"), None, None),
        P(("dp", "expert"), None, None),
        P(("dp", "expert"), None),
        P(),
        P(),
        P(),
        P(),
        P(),
        P(),
        P(),
        P(),
        P(),
        P(),
        P(),
        P("expert", None, None),
        P("expert", None, None),
    )
    return jax.shard_map(
        path,
        mesh=mesh,
        in_specs=placed,
        out_specs=(
            P(("dp", "expert"), None),
            P(("dp", "expert"), None),
            P(("dp", "expert")),
            P(("dp", "expert")),
            P(("dp", "expert"), None),
            P(("dp", "expert"), None),
            P(("dp", "expert"), None),
            P(None, ("dp", "expert")),
            P(("dp", "expert"), None),
            P(("dp", "expert"), None),
            P(("dp", "expert")),
            P(("dp", "expert")),
            P(("dp", "expert"), None),
            P("expert", "dp", None),
            P("expert", None, "dp"),
            P(),
        ),
        check_vma=False,
    )
```

```python
import math
from functools import partial

import jax
import jax.numpy as jnp
from jax import lax
from jax.experimental import pallas as pl
from jax.experimental.pallas import tpu as pltpu
from jax.sharding import PartitionSpec as P

EXPERTS = 387
MOST = 8
EPSILON = 1e-05
NEGATIVE = -1e30
f32 = jnp.float32
bf16 = jnp.bfloat16
VMEM_LIMIT = 56 * 1024 * 1024
GELU_A = math.sqrt(2.0 / math.pi)
GELU_B = 0.044715


def layer_norm(values, scaling, offset):
    centred = values - jnp.mean(values, axis=-1, keepdims=True)
    inverse = lax.rsqrt(jnp.mean(centred * centred, axis=-1, keepdims=True) + EPSILON)
    normed = centred * inverse
    return (normed * scaling + offset, normed, inverse)


def norm_backward(upstream, normed, inverse, scaling):
    scaled = upstream * scaling
    centre_term = jnp.mean(scaled, axis=-1, keepdims=True)
    slope_term = jnp.mean(scaled * normed, axis=-1, keepdims=True)
    return inverse * (scaled - centre_term - normed * slope_term)


def gate_table(logits, routes, choices_count):
    chosen = jnp.any(routes[..., None] == jnp.arange(choices_count), axis=-2)
    sigmas = jax.nn.sigmoid(logits)
    return (chosen, sigmas, jnp.where(chosen, sigmas, 0.0))


def general_path(
    layer_input,
    cotangent,
    lengths,
    value_routes,
    output_routes,
    ffn_routes,
    att_gain,
    att_shift,
    query_weight,
    key_weight,
    value_weight,
    output_weight,
    value_selector,
    output_selector,
    ffn_gain,
    ffn_shift,
    ffn_selector,
    up_weight,
    down_weight,
):
    f32 = jnp.float32
    bf16 = jnp.bfloat16
    seq_len, width = layer_input.shape
    heads = value_routes.shape[1]
    head_dim = query_weight.shape[1] // heads
    att_experts = value_selector.shape[1] // heads
    top_ffn = ffn_routes.shape[1]
    exp_local = up_weight.shape[0]
    owners = lax.axis_size("expert")
    padded_experts = exp_local * owners
    capacity = MOST
    scaling = 1.0 / math.sqrt(head_dim)
    positions = jnp.arange(seq_len)
    is_valid = positions < lengths[0]
    validity = is_valid.astype(f32)
    input_float = layer_input.astype(f32)
    norm_att, hat_att, inv_att = layer_norm(input_float, att_gain, att_shift)
    act_att = norm_att.astype(bf16)
    queries = (
        jnp.dot(act_att, query_weight, preferred_element_type=f32)
        .astype(bf16)
        .reshape(seq_len, heads, head_dim)
    )
    key_rows = (
        jnp.dot(act_att, key_weight, preferred_element_type=f32)
        .astype(bf16)
        .reshape(seq_len, heads, head_dim)
    )
    projected = jnp.dot(layer_input, value_weight, preferred_element_type=f32).reshape(
        seq_len, heads, att_experts, head_dim
    )
    value_logits = jnp.dot(act_att, value_selector, preferred_element_type=f32).reshape(
        seq_len, heads, att_experts
    )
    output_logits = jnp.dot(act_att, output_selector, preferred_element_type=f32).reshape(
        seq_len, heads, att_experts
    )
    value_pick, value_sig, value_gates = gate_table(value_logits, value_routes, att_experts)
    out_pick, out_sig, out_gates = gate_table(output_logits, output_routes, att_experts)
    values_low = jnp.sum(value_gates[..., None] * projected, axis=2).astype(bf16)
    causal = (positions[None, :] <= positions[:, None]) & is_valid[None, :]
    raw_scores = jnp.einsum("qhd,khd->hqk", queries, key_rows, preferred_element_type=f32) * scaling
    scores = jnp.where(causal[None], raw_scores, NEGATIVE)
    row_peak = jnp.max(scores, axis=-1, keepdims=True)
    log_total = row_peak + jnp.log(jnp.sum(jnp.exp(scores - row_peak), axis=-1, keepdims=True))
    weights_p = jnp.exp(scores - log_total)
    weights_low = weights_p.astype(bf16)
    attended = jnp.einsum("hqk,khd->qhd", weights_low, values_low, preferred_element_type=f32)
    mixed_rows = (out_gates[..., None] * attended[:, :, None, :]).reshape(seq_len, -1).astype(bf16)
    residual = input_float + jnp.dot(mixed_rows, output_weight, preferred_element_type=f32)
    norm_ffn, hat_ffn, inv_ffn = layer_norm(residual, ffn_gain, ffn_shift)
    act_ffn = norm_ffn.astype(bf16)
    ffn_logits = jnp.dot(act_ffn, ffn_selector, preferred_element_type=f32)
    ffn_sig = jax.nn.sigmoid(jnp.take_along_axis(ffn_logits, ffn_routes, axis=1))
    gate_weights = ffn_sig * validity[:, None]
    entries = ffn_routes.reshape(-1)
    live_entry = jnp.broadcast_to(is_valid[:, None], ffn_routes.shape).reshape(-1)
    onehot_table = (
        (entries[:, None] == jnp.arange(padded_experts)[None, :]) & live_entry[:, None]
    ).astype(jnp.int32)
    before = jnp.cumsum(onehot_table, axis=0) - onehot_table
    slot_rank = jnp.sum(before * onehot_table, axis=1)
    counts_local = jnp.sum(onehot_table, axis=0).astype(f32)
    target = jnp.where(live_entry, entries * capacity + slot_rank, padded_experts * capacity)
    fetch = jnp.minimum(target, padded_experts * capacity - 1)
    total_slots = padded_experts * capacity
    residual_low = residual.astype(bf16)
    copies = jnp.broadcast_to(residual_low[:, None, :], (seq_len, top_ffn, width)).reshape(
        -1, width
    )
    send_rows = jnp.zeros((total_slots, width), bf16).at[target].set(copies, mode="drop")
    received = lax.all_to_all(
        send_rows.reshape(owners, exp_local * capacity, width),
        "expert",
        split_axis=0,
        concat_axis=0,
        tiled=True,
    )
    received = received.reshape(owners, exp_local, capacity, width)
    hidden_pre = jnp.einsum("semd,edh->semh", received, up_weight, preferred_element_type=f32)
    hidden_act = jax.nn.gelu(hidden_pre).astype(bf16)
    expert_out = jnp.einsum(
        "semh,ehd->semd", hidden_act, down_weight, preferred_element_type=f32
    ).astype(bf16)
    returned = lax.all_to_all(
        expert_out.reshape(owners, exp_local * capacity, width),
        "expert",
        split_axis=0,
        concat_axis=0,
        tiled=True,
    )
    gathered = (
        returned.reshape(total_slots, width)[fetch].reshape(seq_len, top_ffn, width).astype(f32)
    )
    final = residual + jnp.einsum("tk,tkd->td", gate_weights, gathered)
    output = final.astype(bf16)
    counts_all = lax.psum(counts_local, ("dp", "expert"))
    grad_final = cotangent.astype(f32)
    grad_rows = (gate_weights[:, :, None] * grad_final[:, None, :]).astype(bf16).reshape(-1, width)
    grad_gate = validity[:, None] * jnp.einsum("tkd,td->tk", gathered, grad_final)
    send_grad = jnp.zeros((total_slots, width), bf16).at[target].set(grad_rows, mode="drop")
    grad_recv = lax.all_to_all(
        send_grad.reshape(owners, exp_local * capacity, width),
        "expert",
        split_axis=0,
        concat_axis=0,
        tiled=True,
    )
    grad_recv = grad_recv.reshape(owners, exp_local, capacity, width)
    down_local = jnp.einsum("semh,semd->ehd", hidden_act, grad_recv, preferred_element_type=f32)
    grad_act = jnp.einsum("semd,ehd->semh", grad_recv, down_weight, preferred_element_type=f32)
    gelu_value, gelu_back = jax.vjp(jax.nn.gelu, hidden_pre)
    grad_pre = gelu_back(grad_act)[0].astype(bf16)
    up_local = jnp.einsum("semd,semh->edh", received, grad_pre, preferred_element_type=f32)
    grad_in = jnp.einsum("semh,edh->semd", grad_pre, up_weight, preferred_element_type=f32).astype(
        bf16
    )
    grad_back = lax.all_to_all(
        grad_in.reshape(owners, exp_local * capacity, width),
        "expert",
        split_axis=0,
        concat_axis=0,
        tiled=True,
    )
    grad_copies = (
        grad_back.reshape(total_slots, width)[fetch].reshape(seq_len, top_ffn, width).astype(f32)
    )
    grad_residual = grad_final + jnp.einsum("t,tkd->td", validity, grad_copies)
    sig_grad = grad_gate * ffn_sig * (1.0 - ffn_sig)
    dense_select = jnp.sum(
        jnp.where(ffn_routes[:, :, None] == jnp.arange(EXPERTS), sig_grad[:, :, None], 0.0), axis=1
    ).astype(bf16)
    ffn_selector_local = jnp.einsum("td,te->de", act_ffn, dense_select, preferred_element_type=f32)
    grad_norm_ffn = jnp.einsum("te,de->td", dense_select, ffn_selector, preferred_element_type=f32)
    ffn_gain_local = jnp.sum(grad_norm_ffn * hat_ffn, axis=0)
    ffn_shift_local = jnp.sum(grad_norm_ffn, axis=0)
    grad_residual = grad_residual + norm_backward(grad_norm_ffn, hat_ffn, inv_ffn, ffn_gain)
    grad_att_low = grad_residual.astype(bf16)
    output_local = jnp.einsum("tc,td->cd", mixed_rows, grad_att_low, preferred_element_type=f32)
    grad_mixed = jnp.einsum("td,cd->tc", grad_att_low, output_weight, preferred_element_type=f32)
    grad_mixed = grad_mixed.reshape(seq_len, heads, att_experts, head_dim)
    grad_attended = jnp.sum(out_gates[..., None] * grad_mixed, axis=2).astype(bf16)
    grad_out_gates = jnp.sum(grad_mixed * attended[:, :, None, :], axis=-1)
    out_select = (
        jnp.where(out_pick, grad_out_gates * out_sig * (1.0 - out_sig), 0.0)
        .reshape(seq_len, -1)
        .astype(bf16)
    )
    grad_weights = jnp.einsum("qhd,khd->hqk", grad_attended, values_low, preferred_element_type=f32)
    row_delta = jnp.sum(weights_p * grad_weights, axis=-1, keepdims=True)
    grad_scores = (weights_p * (grad_weights - row_delta)).astype(bf16)
    grad_queries = (
        (jnp.einsum("hqk,khd->qhd", grad_scores, key_rows, preferred_element_type=f32) * scaling)
        .reshape(seq_len, -1)
        .astype(bf16)
    )
    grad_keys = (
        (jnp.einsum("hqk,qhd->khd", grad_scores, queries, preferred_element_type=f32) * scaling)
        .reshape(seq_len, -1)
        .astype(bf16)
    )
    grad_values = jnp.einsum(
        "hqk,qhd->khd", weights_low, grad_attended, preferred_element_type=f32
    ).astype(bf16)
    grad_values_float = grad_values.astype(f32)
    grad_projected = (
        (value_gates[..., None] * grad_values_float[:, :, None, :])
        .reshape(seq_len, -1)
        .astype(bf16)
    )
    grad_value_gates = jnp.sum(grad_values_float[:, :, None, :] * projected, axis=-1)
    value_select = (
        jnp.where(value_pick, grad_value_gates * value_sig * (1.0 - value_sig), 0.0)
        .reshape(seq_len, -1)
        .astype(bf16)
    )
    value_local = jnp.einsum("td,tc->dc", layer_input, grad_projected, preferred_element_type=f32)
    query_local = jnp.einsum("td,tc->dc", act_att, grad_queries, preferred_element_type=f32)
    key_local = jnp.einsum("td,tc->dc", act_att, grad_keys, preferred_element_type=f32)
    value_selector_local = jnp.einsum(
        "td,tc->dc", act_att, value_select, preferred_element_type=f32
    )
    output_selector_local = jnp.einsum("td,tc->dc", act_att, out_select, preferred_element_type=f32)
    grad_norm_att = jnp.einsum("tc,dc->td", grad_queries, query_weight, preferred_element_type=f32)
    grad_norm_att = grad_norm_att + jnp.einsum(
        "tc,dc->td", grad_keys, key_weight, preferred_element_type=f32
    )
    grad_norm_att = grad_norm_att + jnp.einsum(
        "tc,dc->td", value_select, value_selector, preferred_element_type=f32
    )
    grad_norm_att = grad_norm_att + jnp.einsum(
        "tc,dc->td", out_select, output_selector, preferred_element_type=f32
    )
    att_gain_local = jnp.sum(grad_norm_att * hat_att, axis=0)
    att_shift_local = jnp.sum(grad_norm_att, axis=0)
    input_grad = grad_residual + jnp.einsum(
        "tc,dc->td", grad_projected, value_weight, preferred_element_type=f32
    )
    input_grad = input_grad + norm_backward(grad_norm_att, hat_att, inv_att, att_gain)
    reduced = (
        lax.psum_scatter(att_gain_local, ("dp", "expert"), scatter_dimension=0, tiled=True),
        lax.psum_scatter(att_shift_local, ("dp", "expert"), scatter_dimension=0, tiled=True),
        lax.psum_scatter(query_local, ("dp", "expert"), scatter_dimension=0, tiled=True),
        lax.psum_scatter(key_local, ("dp", "expert"), scatter_dimension=0, tiled=True),
        lax.psum_scatter(value_local, ("dp", "expert"), scatter_dimension=0, tiled=True),
        lax.psum_scatter(output_local, ("dp", "expert"), scatter_dimension=1, tiled=True),
        lax.psum_scatter(value_selector_local, ("dp", "expert"), scatter_dimension=0, tiled=True),
        lax.psum_scatter(output_selector_local, ("dp", "expert"), scatter_dimension=0, tiled=True),
        lax.psum_scatter(ffn_gain_local, ("dp", "expert"), scatter_dimension=0, tiled=True),
        lax.psum_scatter(ffn_shift_local, ("dp", "expert"), scatter_dimension=0, tiled=True),
        lax.psum_scatter(ffn_selector_local, ("dp", "expert"), scatter_dimension=0, tiled=True),
    )
    up_grad, down_grad = (
        lax.psum_scatter(
            up_local.astype(jnp.bfloat16), "dp", scatter_dimension=1, tiled=True
        ).astype(jnp.float32),
        lax.psum_scatter(
            down_local.astype(jnp.bfloat16), "dp", scatter_dimension=2, tiled=True
        ).astype(jnp.float32),
    )
    return (
        output,
        input_grad,
        reduced[0],
        reduced[1],
        reduced[2],
        reduced[3],
        reduced[4],
        reduced[5],
        reduced[6],
        reduced[7],
        reduced[8],
        reduced[9],
        reduced[10],
        up_grad,
        down_grad,
        counts_all[:EXPERTS],
    )


def mm(a, b, ca, cb):
    return lax.dot_general(a, b, (((ca,), (cb,)), ((), ())), preferred_element_type=f32)


def iota(shape, dim):
    return lax.broadcasted_iota(jnp.int32, shape, dim)


def centre(values):
    centred = values - jnp.mean(values, axis=-1, keepdims=True)
    inverse = lax.rsqrt(jnp.mean(centred * centred, axis=-1, keepdims=True) + EPSILON)
    return centred * inverse, inverse


def centre_back(upstream, normed, inverse, gain):
    scaled = upstream * gain
    mean = jnp.mean(scaled, axis=-1, keepdims=True)
    slope = jnp.mean(scaled * normed, axis=-1, keepdims=True)
    return inverse * (scaled - mean - normed * slope)


def device_of(ids, s, x):
    return 2 * s + (ids[1] + x - 2 * ids[1] * x)


SHORT = pl.CostEstimate(flops=1, bytes_accessed=1, transcendentals=0)


LONG = pl.CostEstimate(flops=1, bytes_accessed=1 << 28, transcendentals=0)


def call(body, outs, args, scratch=(), smem=(), name=None, cost=SHORT):
    return pl.pallas_call(
        body,
        out_shape=[jax.ShapeDtypeStruct(s, d) for s, d in outs],
        in_specs=[pl.BlockSpec(memory_space=pltpu.SMEM)] * len(smem)
        + [pl.BlockSpec(memory_space=pltpu.VMEM)] * len(args),
        out_specs=[pl.BlockSpec(memory_space=pltpu.VMEM)] * len(outs),
        scratch_shapes=list(scratch),
        compiler_params=pltpu.CompilerParams(vmem_limit_bytes=VMEM_LIMIT),
        cost_estimate=cost,
        name=name,
    )(*smem, *args)


def forward_body(
    length, li, vroutes, oroutes, froutes, att_gain, att_shift, wq, wk, wv, wo, vsel, osel,
    ffn_gain, ffn_shift, fsel,
    h1_o, xpack_o, q_o, k_o, v_o, p_o, a_o, o_o, gt_o, a1_o, a2_o, mixed,
):
    T, D = li.shape
    heads = vroutes.shape[0]
    dh = wq.shape[1] // heads
    ea = wv.shape[1] // (heads * dh)
    he = heads * ea
    top = froutes.shape[0]
    routes = [vroutes[h] for h in range(heads)] + [oroutes[h] for h in range(heads)] + [froutes[...]]
    routes = jnp.concatenate([r.astype(f32) for r in routes], axis=0)
    routes = jnp.concatenate([routes, jnp.zeros((128 - routes.shape[0], T), f32)], axis=0).T.astype(jnp.int32)
    scaling = 1.0 / math.sqrt(dh)
    x = li[...].astype(f32)
    hat, inv = centre(x)
    mean = jnp.mean(x, axis=-1, keepdims=True)
    a1 = (hat * att_gain[...] + att_shift[...]).astype(bf16)
    a1_o[...] = a1
    logits = jnp.concatenate(
        [mm(a1, vsel[...], 1, 1), mm(a1, osel[...], 1, 1), jnp.zeros((T, 128 - 2 * he), f32)], axis=1
    )
    lane = iota((T, 128), 1)
    chosen = jnp.zeros((T, 128), jnp.bool_)
    for j in range(2 * heads):
        h = j // 2
        chosen |= lane == routes[:, j : j + 1] + h * ea
        chosen |= lane == routes[:, 2 * heads + j : 2 * heads + j + 1] + (he + h * ea)
    gt = jnp.where(chosen, jax.nn.sigmoid(logits), 0.0)
    gt_o[...] = jnp.where(lane == 2 * he, mean, jnp.where(lane == 2 * he + 1, inv, gt))
    q = mm(a1, wq[...], 1, 0).astype(bf16)
    k = mm(a1, wk[...], 1, 0).astype(bf16)
    q_o[...] = q
    k_o[...] = k
    n_live = length[0]
    row, col = iota((T, T), 0), iota((T, T), 1)
    causal = (col <= row) & (col < n_live)
    width = ea * dh
    every = range(heads)
    hs = [slice(h * dh, (h + 1) * dh) for h in every]
    scores = [jnp.where(causal, mm(q[:, hs[h]], k[:, hs[h]], 1, 1) * scaling, NEGATIVE) for h in every]
    proj = [mm(li[...], wv[:, h * width : (h + 1) * width], 1, 0) for h in every]
    vs, weights = [], []
    for h in every:
        p_o[:, h * width : (h + 1) * width] = proj[h]
        v = jnp.zeros((T, dh), f32)
        for e in range(ea):
            v += gt[:, h * ea + e : h * ea + e + 1] * proj[h][:, e * dh : (e + 1) * dh]
        vs.append(v.astype(bf16))
        v_o[:, hs[h]] = vs[h]
        ex = jnp.exp(scores[h] - jnp.max(scores[h], axis=-1, keepdims=True))
        a = ex / jnp.sum(ex, axis=-1, keepdims=True)
        a_o[h] = a
        weights.append(a.astype(bf16))
    attended = [mm(weights[h], vs[h], 1, 0) for h in every]
    for h in every:
        o_o[:, hs[h]] = attended[h]
        for e in range(ea):
            c = he + h * ea + e
            mixed[:, (h * ea + e) * dh : (h * ea + e + 1) * dh] = (gt[:, c : c + 1] * attended[h]).astype(bf16)
    h1 = x + mm(mixed[...], wo[...], 1, 0)
    h1_o[...] = h1
    hat2, _ = centre(h1)
    a2 = (hat2 * ffn_gain[...] + ffn_shift[...]).astype(bf16)
    a2_o[...] = a2
    sig = jax.nn.sigmoid(mm(a2, fsel[...], 1, 1))
    wide = iota(sig.shape, 1)
    g = jnp.zeros((T, 128), f32)
    for i in range(top):
        c = 4 * heads + i
        one = jnp.sum(jnp.where(wide == routes[:, c : c + 1], sig, 0.0), axis=-1, keepdims=True)
        g = jnp.where(lane == i, one, g)
    g = g.T[:16]
    hi = g.astype(bf16)
    low = h1.astype(bf16)
    for s in range(xpack_o.shape[0]):
        xpack_o[s, :T] = low
        xpack_o[s, T:] = jnp.zeros((16, D), bf16)
        xpack_o[s, T:, :128] = hi
        xpack_o[s, T:, 128:256] = (g - hi.astype(f32)).astype(bf16)


def take_slices(v, n_p, S, e):
    D = v.shape[1]
    w = D // (n_p * S)
    return jnp.concatenate(
        [v[:, (b * S + e) * w : (b * S + e + 1) * w] for b in range(n_p)], axis=1
    )


def views(mine, theirs):
    return [r.at[s] for s in range(mine.shape[0]) for r in (mine, theirs)]


def views_from(ids, mine, theirs):
    return [r.at[ids[0] ^ s] for s in range(mine.shape[0]) for r in (mine, theirs)]


def early_body(n_p, S, ids, li, a1, a2, o, gt, *rest):
    msgs, scratch = rest
    msgs = [msgs.at[s] for s in range(S // 2)]
    hd = o.shape[1]
    for e in range(S):
        for i, v in enumerate((li, a1, a2)):
            scratch[e, :, i * 128 : (i + 1) * 128] = take_slices(v[...].astype(f32), n_p, S, e).astype(bf16)
    hi = gt[...].astype(bf16).astype(f32)
    both = (hi + pltpu.roll(gt[...] - hi, 64, 1)).astype(bf16)
    for s, m in enumerate(msgs):
        m[:, :hd] = o[...].astype(bf16)
        m[:, hd : hd + 128] = both
        m[:, hd + 128 : hd + 512] = scratch[device_of(ids, s, 1)]
        m[:, hd + 512 : hd + 896] = scratch[device_of(ids, s, 0)]


def codes_body(S, ids, *refs):
    c, (code_o, cnt_o, routes_o) = views_from(ids, *refs[:2]), refs[2:]
    ep = cnt_o.shape[1]
    T = code_o.shape[2] // 2
    strict = (iota((T, T), 0) < iota((T, T), 1)).astype(f32).astype(bf16)
    e_id = iota((ep, T), 0).astype(f32)
    cnt = jnp.zeros((8, ep), f32)
    start = ids[3].astype(f32)
    for k in range(S):
        r = c[k][:, :T].astype(f32) * 32.0 + c[k][:, T:].astype(f32)
        routes_o[k * 16 : (k + 1) * 16, :] = r
        r -= start
        mask = jnp.zeros((ep, T), f32)
        for i in range(r.shape[0]):
            mask = jnp.where(r[i : i + 1] == e_id, 1.0, mask)
        low = mask.astype(bf16)
        rank = mm(low, strict, 1, 0) + (MOST * (k % 2))
        cnt += mm(jnp.ones((8, T), bf16), low, 1, 1)
        code_o[k // 2, :, (k % 2) * T : (k % 2 + 1) * T] = jnp.where(mask > 0.5, rank, -1.0).astype(bf16)
    cnt_o[...] = cnt


def columns_body(n_p, order, ids, x, *refs):
    outs = refs[-n_p:]
    T = x.shape[1] - 16
    wide = outs[0].shape[2]
    for k in range(x.shape[0]):
        rows = x.at[ids[0] ^ k if order else k]
        for s in range(n_p):
            at = pl.multiple_of((ids[2] ^ s) * wide, 128)
            outs[s][k, :T, :] = rows[:T, pl.ds(at, wide)]
    if len(refs) > n_p:
        for s in range(n_p):
            outs[s][:, T:, :] = refs[0][...]


def gelu_both(u):
    t = jnp.tanh(GELU_A * (u + GELU_B * u * u * u))
    value = 0.5 * u * (1.0 + t)
    slope = 0.5 * (1.0 + t) + 0.5 * u * (1.0 - t * t) * (GELU_A * (1.0 + 3.0 * GELU_B * u * u))
    return value, slope


def experts_body(S, eb, ids, *refs):
    x, c = views(*refs[:2]), views_from(ids, *refs[2:4])
    code, up, down, dx0, dx1, gy0, gy1, gr_o, du_o, ct, gts, dl, ps, xs, cs, gys, dxs = refs[4:]
    step = pl.program_id(0)
    pairs = S // 2
    R = 2 * MOST
    T = x[0].shape[0] - 16
    D = x[0].shape[1]
    ep = ct.shape[1]
    rows = pairs * R
    H = up.shape[2]

    @pl.when(step == 0)
    def _():
        e_id = iota((ep, T), 0).astype(f32)
        start = ids[3].astype(f32)
        dl[...] = jnp.zeros_like(dl)
        for pr in range(pairs):
            ct[pr] = code[pr].astype(f32)
        for k in range(S):
            r = c[k][T:, :T].astype(f32) * 32.0 + c[k][T:, T : 2 * T].astype(f32) - start
            g = x[k][T:, :T].astype(f32) + x[k][T:, T : 2 * T].astype(f32)
            dense = jnp.zeros((ep, T), f32)
            for i in range(r.shape[0]):
                dense = jnp.where(r[i : i + 1] == e_id, g[i : i + 1], dense)
            gts[:, k * T : (k + 1) * T] = dense

    slot = iota((R, 2 * T), 0).astype(f32)
    g_slot = [[None] * pairs for _ in range(eb)]
    onehot = [[None] * pairs for _ in range(eb)]
    for pr in range(pairs):
        blocks = []
        for j in range(eb):
            e = step * eb + j
            hot = jnp.where(ct[pr, pl.ds(e, 1), :] == slot, 1.0, 0.0)
            onehot[j][pr] = hot
            g_slot[j][pr] = jnp.sum(
                hot * gts[pl.ds(e, 1), pr * 2 * T : (pr + 1) * 2 * T], axis=-1, keepdims=True
            )
            blocks.append(hot.astype(bf16))
        block = jnp.concatenate(blocks, axis=0)
        ps[pr, pl.ds(pl.multiple_of(step * (eb * R), R), eb * R), :] = block
        for src, dst in ((x, xs), (c, cs)):
            both = jnp.concatenate([src[2 * pr][:T], src[2 * pr + 1][:T]], axis=0)
            got = mm(block, both, 1, 0).astype(bf16)
            for j in range(eb):
                dst[j * rows + pr * R : j * rows + (pr + 1) * R, :] = got[j * R : (j + 1) * R]
    units = [list(range(first, min(first + 2, eb))) for first in range(0, eb, 2)]
    every = range(len(units))
    spans = [slice(js[0] * rows, (js[-1] + 1) * rows) for js in units]

    def own(v, n):
        return jnp.concatenate([v[i * rows : (i + 1) * rows, i * H : (i + 1) * H] for i in range(n)], axis=0)

    def spread_out(v, n):
        if n == 1:
            return v
        zero = jnp.zeros((rows, H), v.dtype)
        return jnp.concatenate(
            [
                jnp.concatenate([v[i * rows : (i + 1) * rows] if i == b else zero for b in range(n)], axis=1)
                for i in range(n)
            ],
            axis=0,
        )

    gs = [jnp.concatenate([p for j in js for p in g_slot[j]], axis=0) for js in units]
    ups = [jnp.concatenate([up[j] for j in js], axis=1) for js in units]
    downs = [jnp.concatenate([down[j] for j in js], axis=0) for js in units]
    us = [own(mm(xs[spans[m], :], ups[m], 1, 0), len(units[m])) for m in every]
    drs = [
        own(mm((gs[m] * cs[spans[m], :].astype(f32)).astype(bf16), downs[m], 1, 1), len(units[m])) for m in every
    ]
    dus, rs = [], []
    for m in every:
        value, slope = gelu_both(us[m])
        rs.append(value.astype(bf16))
        dus.append((drs[m] * slope).astype(bf16))
    ys = [mm(spread_out(rs[m], len(units[m])), downs[m], 1, 0).astype(bf16) for m in every]
    dxu = [mm(spread_out(dus[m], len(units[m])), ups[m], 1, 1).astype(bf16) for m in every]
    for m in every:
        js = units[m]
        g = gs[m]
        r, du = rs[m], dus[m]
        y, dx = ys[m].astype(f32), dxu[m]
        dgate = jnp.sum(cs[spans[m], :].astype(f32) * y, axis=-1, keepdims=True)
        gy = (g * y).astype(bf16)
        gr = (g * r.astype(f32)).astype(bf16)
        dlog = dgate * g * (1.0 - g)
        for i, j in enumerate(js):
            e = step * eb + j
            gr_o[j] = gr[i * rows : (i + 1) * rows]
            du_o[j] = du[i * rows : (i + 1) * rows]
            for pr in range(pairs):
                at = pl.ds(pl.multiple_of(step * (eb * R) + j * R, R), R)
                cut = slice(i * rows + pr * R, i * rows + (pr + 1) * R)
                gys[pr, at, :] = gy[cut]
                dxs[pr, at, :] = dx[cut]
                dl[pl.ds(e, 1), pr * 2 * T : (pr + 1) * 2 * T] = jnp.sum(
                    onehot[j][pr] * dlog[cut], axis=0, keepdims=True
                )

    @pl.when(step == pl.num_programs(0) - 1)
    def _():
        for pr in range(pairs):
            for src, d0, d1 in ((dxs, dx0, dx1), (gys, gy0, gy1)):
                got = mm(ps[pr], src[pr], 0, 0).astype(bf16)
                d0[pr, :T] = got[:T]
                d1[pr, :T] = got[T:]
            for x_i, d in ((0, dx0), (1, dx1)):
                k = 2 * pr + x_i
                part = dl[:, k * T : (k + 1) * T].astype(bf16)
                d[pr, T:] = jnp.zeros((16, D), bf16)
                for b in range(ep // 16):
                    d[pr, T:, b * T : (b + 1) * T] = part[16 * b : 16 * b + 16]


def join_body(T, mine, recv, out):
    half = mine.shape[2] // 2
    for s in range(mine.shape[0]):
        out[s, :T] = (mine[s, :T].astype(f32) + recv[s, :T].astype(f32)).astype(bf16)
        if mine.shape[1] > T:
            out[s, T:, :half] = mine[s, T:, :half]
            out[s, T:, half:] = recv[s, T:, :half]


def join_apart_body(nz, ids, mine, recv, *outs):
    for s in range(nz):
        outs[s][...] = (mine[ids[0] ^ s].astype(f32) + recv[ids[0] ^ s].astype(f32)).astype(bf16)


def ffn_back_body(n_p, S, nz, ids, parts, h1, c, fsel, gain, froutes, cnt, dh1_o, db_o, mid_o, dlt, sl):
    T, D = h1.shape
    ep = dlt.shape[0] // S
    half = D // 2
    dxs = parts[0, :T].astype(f32)
    for s in range(1, nz):
        dxs += parts[s, :T].astype(f32)
    for s in range(nz):
        for x in range(2):
            for b in range(ep // 16):
                at = pl.multiple_of(device_of(ids, s, x) * ep + 16 * b, 16)
                dlt[pl.ds(at, 16), :] = parts[s, T:, x * half + b * T : x * half + (b + 1) * T].astype(f32)
    dl = dlt[...].T
    da2 = mm(dl.astype(bf16), fsel[...], 1, 0)
    hat, inv = centre(h1[...])
    dh1 = c[...].astype(f32) + dxs + centre_back(da2, hat, inv, gain[...])
    dh1_o[...] = dh1
    db = dh1.astype(bf16)
    db_o[...] = db
    low = db.astype(f32)
    for e in range(S):
        sl[e] = take_slices(low, n_p, S, e).astype(bf16)
    slot = iota(dlt.shape, 0)
    few = [
        jnp.sum(jnp.where(slot == froutes[i : i + 1, :], dlt[...], 0.0), axis=0, keepdims=True)
        for i in range(froutes.shape[0])
    ]
    few = jnp.concatenate(few, axis=0).astype(bf16)
    hi = cnt[...].astype(bf16)
    lo = (cnt[...] - hi.astype(f32)).astype(bf16)
    vectors = []
    for v in (jnp.sum(da2 * hat, axis=0, keepdims=True), jnp.sum(da2, axis=0, keepdims=True)):
        high = v.astype(bf16).astype(f32)
        for part in (high, v - high):
            vectors += [part[:, b * 256 : (b + 1) * 256] for b in range(D // 256)]
    vectors = jnp.concatenate(vectors, axis=0).astype(bf16)
    for s in range(nz):
        m = mid_o.at[s]
        m[:T, :128] = sl[device_of(ids, s, 1)]
        m[:T, 128:] = sl[device_of(ids, s, 0)]
        m[T : T + 16, :T] = few
        m[T : T + 16, T:] = jnp.zeros((16, 256 - T), bf16)
        m[T : T + 16, T : T + ep] = jnp.concatenate([hi, lo], axis=0)
        m[T + 16 :] = vectors


def attention_back_body(db, wo, gt, o, q, k, v, a, p, late_o, dp_o):
    T, D = db.shape
    heads = a.shape[0]
    dh = q.shape[1] // heads
    ea = p.shape[1] // (heads * dh)
    he, hd = heads * ea, heads * dh
    width = ea * dh
    scaling = 1.0 / math.sqrt(dh)
    gates = gt[...]
    lane = iota((T, 128), 1)
    every = range(heads)
    hs = [slice(h * dh, (h + 1) * dh) for h in every]
    dz = [mm(db[...], wo[h * width : (h + 1) * width, :], 1, 1) for h in every]
    do = []
    for h in every:
        total = jnp.zeros((T, dh), f32)
        for e in range(ea):
            c = he + h * ea + e
            total += gates[:, c : c + 1] * dz[h][:, e * dh : (e + 1) * dh]
        do.append(total.astype(bf16))
    da = [mm(do[h], v[:, hs[h]], 1, 1) for h in every]
    dv = [mm(a[h].astype(bf16), do[h], 0, 0).astype(bf16) for h in every]
    ds = [(a[h] * (da[h] - jnp.sum(a[h] * da[h], axis=-1, keepdims=True))).astype(bf16) for h in every]
    dq = [(mm(ds[h], k[:, hs[h]], 1, 0) * scaling).astype(bf16) for h in every]
    dk = [(mm(ds[h], q[:, hs[h]], 0, 0) * scaling).astype(bf16) for h in every]
    dgates = jnp.zeros((T, 128), f32)
    for h in every:
        oh, dvf = o[:, hs[h]], dv[h].astype(f32)
        for e in range(ea):
            c = h * ea + e
            es = slice(c * dh, (c + 1) * dh)
            dp_o[:, es] = (gates[:, c : c + 1] * dvf).astype(bf16)
            out_sum = jnp.sum(dz[h][:, e * dh : (e + 1) * dh] * oh, axis=-1, keepdims=True)
            in_sum = jnp.sum(dvf * p[:, es], axis=-1, keepdims=True)
            dgates = jnp.where(lane == he + c, out_sum, jnp.where(lane == c, in_sum, dgates))
    sel = (dgates * gates * (1.0 - gates)).astype(bf16)
    for s in range(late_o.shape[0]):
        for h in every:
            late_o[s, :, hs[h]] = dv[h]
            late_o[s, :, hd + h * dh : hd + (h + 1) * dh] = dq[h]
            late_o[s, :, 2 * hd + h * dh : 2 * hd + (h + 1) * dh] = dk[h]
        late_o[s, :, 3 * hd :] = sel


def input_back_body(late, dp, wq, wk, wv, selw, li, gain, dh1, ig_o):
    hd = wq.shape[1]
    da1 = mm(late[0, :, hd : 2 * hd], wq[...], 1, 1)
    da1 += mm(late[0, :, 2 * hd : 3 * hd], wk[...], 1, 1)
    da1 += mm(late[0, :, 3 * hd :], selw[...], 1, 1)
    hat, inv = centre(li[...].astype(f32))
    ig_o[...] = dh1[...] + mm(dp[...], wv[...], 1, 1) + centre_back(da1, hat, inv, gain[...])


def spread(values, gates, lo, heads, ea, dh):
    return jnp.concatenate(
        [
            (gates[:, lo + h * ea + e : lo + h * ea + e + 1] * values[:, h * dh : (h + 1) * dh]).astype(bf16)
            for h in range(heads)
            for e in range(ea)
        ],
        axis=1,
    )


def spread_body(S, n_p, w, heads, ea, ids, e0, e1, wq, wk, selw, z_o, a2_o, lia1_o, hat_o, gates_o, wsl_o):
    early = views(e0, e1)
    T = early[0].shape[0]
    D, hd = wq.shape
    for b in range(n_p):
        at = pl.ds(pl.multiple_of(b * (D // n_p) + (2 * ids[0] + ids[1]) * w, 16), w)
        bs = slice(b * w, (b + 1) * w)
        wsl_o[bs, :hd] = wq[at, :]
        wsl_o[bs, hd : 2 * hd] = wk[at, :]
        wsl_o[bs, 2 * hd :] = selw[at, :]
    for k in range(S):
        ts = slice(k * T, (k + 1) * T)
        m = early[k]
        both = m[:, hd : hd + 128].astype(f32)
        gates = both + pltpu.roll(both, 64, 1)
        gates_o[ts, :] = gates
        z_o[ts, :] = spread(m[:, :hd].astype(f32), gates, heads * ea, heads, ea, hd // heads)
        at = hd + 512 if k % 2 == 0 else hd + 128
        li = m[:, at : at + 128].astype(f32)
        he2 = 2 * heads * ea
        lia1_o[:128, ts] = li.T.astype(bf16)
        lia1_o[128:, ts] = m[:, at + 128 : at + 256].astype(f32).T.astype(bf16)
        hat_o[:, ts] = ((li - gates[:, he2 : he2 + 1]) * gates[:, he2 + 1 : he2 + 2]).T
        a2_o[ts, :] = m[:, at + 256 : at + 384]


def out_rows(acc, outs, ids, w):
    for s, ref in enumerate(outs):
        plane = ids[2] ^ s
        ref[:, : acc.shape[1]] = acc[pl.ds(pl.multiple_of(plane * w, 8), w), :].astype(ref.dtype)


def out_grads_body(S, n_p, w, ids, m0, m1, z, a2, routes, *refs):
    mid, outs = views(m0, m1), refs[:n_p]
    acc, lhs, dlt, cnt = refs[n_p:]
    T = z.shape[0] // S
    EP = dlt.shape[0]
    e_id = iota((EP, T), 0).astype(f32)
    norms = jnp.zeros((16, 256), f32)
    for k in range(S):
        n = mid[k]
        ts = slice(k * T, (k + 1) * T)
        at = 128 if k % 2 == 0 else 0
        lhs[ts, :] = n[:T, at : at + 128]
        few = n[T : T + 16, :T].astype(f32)
        route = routes[k * 16 : (k + 1) * 16, :]
        dense = jnp.zeros((EP, T), f32)
        for i in range(16):
            dense = jnp.where(route[i : i + 1] == e_id, few[i : i + 1], dense)
        dlt[:, ts] = dense.astype(bf16)
        tally = n[T : T + 16, T:].astype(f32)
        at = device_of(ids, k // 2, k % 2)
        cnt[pl.ds(at, 1), :] = tally[:1]
        cnt[pl.ds(at + 8, 1), :] = tally[8:9]
        norms += n[T + 16 :].astype(f32)
    wide = z.shape[1]
    acc[:, :wide] = mm(lhs[...], z[...], 0, 0)
    acc[:, wide:] = mm(dlt[...], a2[...], 1, 0).T
    out_rows(acc, outs, ids, w)
    norms = pltpu.roll(norms, lax.rem(256 - (2 * ids[0] + ids[1]) * w, 256), 1)
    norms = jnp.concatenate([norms[0:4] + norms[4:8], norms[8:12] + norms[12:16]], axis=0)
    extra = jnp.concatenate([cnt[...], norms[:, :128], jnp.zeros((w - 24, 128), f32)], axis=0)
    for ref in outs:
        ref[:, acc.shape[1] :] = extra.astype(ref.dtype)


def in_grads_body(n_p, heads, ea, w, hd, ids, l0, l1, lia1, hat, gates, wsl, *refs):
    outs, (acc, rhs, qk, sums) = refs[:n_p], refs[n_p:]
    step = pl.program_id(0)
    T = l0.shape[1]
    wide = rhs.shape[1]

    @pl.when(step == 0)
    def _():
        acc[...] = jnp.zeros_like(acc)
        sums[...] = jnp.zeros_like(sums)

    for x, n in enumerate((l0, l1)):
        ts = slice(x * T, (x + 1) * T)
        rhs[ts, :] = spread(n[0, :, :hd].astype(f32), gates[ts, :], 0, heads, ea, hd // heads)
        qk[ts, :] = n[0, :, hd:]
    acc[:, :wide] += mm(lia1[:128, :], rhs[...], 1, 0)
    acc[:, wide:] += mm(lia1[128:, :], qk[...], 1, 0)
    da1 = mm(wsl[...], qk[...], 1, 1)
    gain = jnp.sum(da1 * hat[...], axis=1, keepdims=True)
    shift = jnp.sum(da1, axis=1, keepdims=True)
    lane = iota((128, 128), 1)
    sums[...] += jnp.where(lane == 64, gain, jnp.where(lane == 65, shift, 0.0))

    @pl.when(step == pl.num_programs(0) - 1)
    def _():
        acc[:, wide + 2 * hd :] += sums[...]
        out_rows(acc, outs, ids, w)


def last_a_body(n_p, S, w, el, ids, *refs):
    parts, (og_o, fg_o, gain_o, shift_o, counts_o, rows) = refs[:n_p], refs[n_p:]
    total = parts[0][...]
    for m in parts[1:]:
        total += m[...].astype(f32)
    wide = og_o.shape[1]
    og_o[...] = total[:w, :wide]
    ep = (total.shape[1] - 128 - wide) // S
    sel = total[:, wide:]
    fg_o[...] = jnp.concatenate([sel[:, e * ep : e * ep + el] for e in range(S)], axis=1)[:, : fg_o.shape[1]]
    extra = total[:, wide + S * ep :]
    rows[...] = extra[16:24]
    gain_o[...] = rows[pl.ds(ids[2], 1), :w]
    shift_o[...] = rows[pl.ds(ids[2] + n_p, 1), :w]
    cnt = extra[0:8] + extra[8:16]
    counts_o[...] = jnp.concatenate([cnt[e : e + 1, :el] for e in range(S)], axis=1)[:, : counts_o.shape[1]]


def last_b_body(n_p, w, hd, he, *refs):
    parts, (vg_o, qg_o, kg_o, vs_o, os_o, gain_o, shift_o) = refs[:n_p], refs[n_p:]
    total = parts[0][...]
    for m in parts[1:]:
        total += m[...].astype(f32)
    wide = vg_o.shape[1]
    vg_o[...] = total[:w, :wide]
    qg_o[...] = total[:w, wide : wide + hd]
    kg_o[...] = total[:w, wide + hd : wide + 2 * hd]
    sel = total[:w, wide + 2 * hd :].T
    vs_o[...] = sel[:he]
    os_o[...] = sel[he : 2 * he]
    gain_o[...] = sel[64:65]
    shift_o[...] = sel[65:66]


def expert_grads_body(n_p, eb, first, xm, xo, cm, co, *refs):
    gr_in, du_in = refs[:n_p], refs[n_p : 2 * n_p]
    up_o, down_o, ct, got = refs[-4:]
    start = pl.program_id(0)
    step = start + first
    _, pairs, T, wide = cm.shape
    T2 = 2 * T
    R = 2 * MOST
    rows = pairs * R

    @pl.when(start == 0)
    def _():
        for s in range(n_p):
            for pr in range(pairs):
                ct[s * pairs + pr] = xm[s, pr, T:, :].astype(f32)

    slot = iota((R, T2), 0).astype(f32)
    for s in range(n_p):
        for pr in range(pairs):
            block = jnp.concatenate(
                [
                    jnp.where(ct[s * pairs + pr, pl.ds(step * eb + j, 1), :] == slot, 1.0, 0.0).astype(bf16)
                    for j in range(eb)
                ],
                axis=0,
            )
            both = jnp.concatenate(
                [jnp.concatenate([x[s, pr, :T], c[s, pr]], axis=1) for x, c in ((xm, cm), (xo, co))], axis=0
            )
            res = mm(block, both, 1, 0).astype(bf16)
            for j in range(eb):
                at = j * n_p * rows + s * rows + pr * R
                got[at : at + R, :] = res[j * R : (j + 1) * R]
    for j in range(eb):
        at = j * n_p * rows
        xj = got[at : at + n_p * rows, :wide]
        cj = got[at : at + n_p * rows, wide:]
        gr = jnp.concatenate([gr_in[s][j] for s in range(n_p)], axis=0)
        du = jnp.concatenate([du_in[s][j] for s in range(n_p)], axis=0)
        up_o[j] = mm(xj, du, 0, 0)
        down_o[j] = mm(gr, cj, 0, 0)


def after(values, *deps):
    return lax.optimization_barrier((values, deps))[0]


class Links:
    def __init__(self):
        self.n_e = lax.axis_size("expert")
        self.nz = self.n_e // 2
        self.n_p = lax.axis_size("dp")
        self.me = lax.axis_index("expert")
        self.z, self.c = self.me // 2, self.me % 2
        self.p = lax.axis_index("dp")

    def core(self, v):
        return lax.ppermute(v, "expert", [(e, e ^ 1) for e in range(self.n_e)])

    def chips(self, v):
        groups = [[2 * s + c for s in range(self.nz)] for c in range(2)]
        return lax.all_to_all(v, "expert", 0, 0, axis_index_groups=groups, tiled=True)

    def chip(self, v, s):
        return lax.ppermute(v, "expert", [(e, (e + 2 * s) % self.n_e) for e in range(self.n_e)])

    def plane(self, v, s):
        return lax.ppermute(v, "dp", [(p, p ^ s) for p in range(self.n_p)])

    def near(self, msgs):
        pairs = [[(e, e ^ (2 * s)) for e in range(self.n_e)] for s in range(self.nz)]
        return [msgs[0]] + [lax.ppermute(msgs[s], "expert", pairs[s]) for s in range(1, self.nz)]

    def relay(self, mine):
        return [mine, self.core(mine)]

    def planes_of(self, msgs):
        return [msgs[0]] + [self.plane(msgs[s], s) for s in range(1, self.n_p)]


def fast_path(
    layer_input, cotangent, lengths, value_routes, output_routes, ffn_routes, att_gain, att_shift,
    query_weight, key_weight, value_weight, output_weight, value_selector, output_selector,
    ffn_gain, ffn_shift, ffn_selector, up_weight, down_weight,
):
    L = Links()
    S, nz, n_p = L.n_e, L.nz, L.n_p
    pairs = S // 2
    T, D = layer_input.shape
    heads = value_routes.shape[1]
    dh = query_weight.shape[1] // heads
    ea = value_selector.shape[1] // heads
    hd, he, wide = heads * dh, heads * ea, heads * ea * dh
    el, _, H = up_weight.shape
    ep = -(-el // 16) * 16
    EP = ep * S
    w = D // (n_p * S)
    Dp = D // n_p
    R = 2 * MOST
    eb = max(d for d in (7, 4, 2, 1) if el % d == 0)

    ids = jnp.stack([L.z, L.c, L.p, L.me * ep]).astype(jnp.int32)
    raw = ffn_routes.T
    padded = (raw // el) * ep + raw % el

    rt = jnp.where(jnp.arange(T)[None, :] < lengths[0], padded, EP)
    tail = jnp.concatenate([rt // 32, rt % 32], axis=1).astype(bf16)
    cpack = jnp.concatenate([cotangent, jnp.pad(tail, ((0, 0), (0, D - 2 * T)))], axis=0)
    c_far = L.near([cpack] * nz)

    h1, xpack, q, k, v, proj, a, o, gt, a1, a2 = call(
        forward_body,
        [
            ((T, D), f32), ((nz, T + 16, D), bf16), ((T, hd), bf16), ((T, hd), bf16), ((T, hd), bf16),
            ((T, wide), f32), ((heads, T, T), f32), ((T, hd), f32), ((T, 128), f32),
            ((T, D), bf16), ((T, D), bf16),
        ],
        [
            layer_input, value_routes.transpose(1, 2, 0), output_routes.transpose(1, 2, 0), raw,
            att_gain[None], att_shift[None], query_weight, key_weight, value_weight, output_weight,
            value_selector.T, output_selector.T, ffn_gain[None], ffn_shift[None], ffn_selector.T,
        ],
        scratch=[pltpu.VMEM((T, wide), bf16)],
        smem=[lengths],
        name="forward",
    )
    x_far = L.chips(xpack)
    selectors = after((ffn_selector, value_selector, output_selector), xpack)
    fsel = jnp.pad(selectors[0].T, ((0, S * el - ffn_selector.shape[1]), (0, 0)))
    fsel = jnp.pad(fsel.reshape(S, el, D), ((0, 0), (0, ep - el), (0, 0))).reshape(EP, D)
    selw = jnp.pad(jnp.concatenate(selectors[1:], axis=1), ((0, 0), (0, 128 - 2 * he)))
    (early,) = call(
        partial(early_body, n_p, S),
        [((nz, T, hd + 896), bf16)],
        [layer_input, a1, a2, o, gt],
        scratch=[pltpu.VMEM((S, T, 384), bf16)],
        smem=[ids],
        name="early_slices",
    )
    c_msgs = L.relay(jnp.stack(after(c_far, early, fsel, selw)))
    ccols = call(
        partial(columns_body, n_p, True), [((nz, T, Dp), bf16)] * n_p, [after(c_msgs[0], c_msgs[1])], smem=[ids],
        name="cotangent_columns",
    )
    cc_all = [ccols[0], L.plane(ccols[1], 1), L.plane(ccols[2], 2)]
    tail_rows = pl.BlockSpec((nz, 16, 2 * T), lambda i: (0, T // 16, 0))
    code, cnt, routes = pl.pallas_call(
        partial(codes_body, S),
        grid=(1,),
        in_specs=[pl.BlockSpec(memory_space=pltpu.SMEM), tail_rows, tail_rows],
        out_specs=[pl.BlockSpec(memory_space=pltpu.VMEM)] * 3,
        out_shape=[
            jax.ShapeDtypeStruct((pairs, ep, 2 * T), bf16), jax.ShapeDtypeStruct((8, ep), f32),
            jax.ShapeDtypeStruct((S * 16, T), f32),
        ],
        compiler_params=pltpu.CompilerParams(vmem_limit_bytes=VMEM_LIMIT),
        cost_estimate=SHORT,
        name="codes",
    )(ids, *after(c_msgs, ccols))
    x_far = after(x_far, code, cc_all[1:])
    x_msgs = L.relay(x_far)
    xcols = call(
        partial(columns_body, n_p, False), [((nz, T + ep, Dp), bf16)] * n_p, [x_far, code],
        smem=[ids],
        name="token_columns",
    )
    xc_all = L.planes_of(xcols)
    early_far = L.chips(after(early, x_far))

    n_eb = el // eb
    whole = [pl.BlockSpec(memory_space=pltpu.VMEM)]
    dx0, dx1, gy0, gy1, gr, du = pl.pallas_call(
        partial(experts_body, S, eb),
        grid=(n_eb,),
        out_shape=[
            jax.ShapeDtypeStruct((pairs, T + 16, D), bf16), jax.ShapeDtypeStruct((pairs, T + 16, D), bf16),
            jax.ShapeDtypeStruct((pairs, T, D), bf16), jax.ShapeDtypeStruct((pairs, T, D), bf16),
            jax.ShapeDtypeStruct((el, pairs * R, H), bf16), jax.ShapeDtypeStruct((el, pairs * R, H), bf16),
        ],
        in_specs=[pl.BlockSpec(memory_space=pltpu.SMEM)]
        + whole * 5
        + [
            pl.BlockSpec((eb, D, H), lambda i: (i, 0, 0)),
            pl.BlockSpec((eb, H, D), lambda i: (i, 0, 0)),
        ],
        out_specs=whole * 4 + [pl.BlockSpec((eb, pairs * R, H), lambda i: (i, 0, 0))] * 2,
        scratch_shapes=[
            pltpu.VMEM((pairs, ep, 2 * T), f32), pltpu.VMEM((ep, S * T), f32), pltpu.VMEM((ep, S * T), f32),
            pltpu.VMEM((pairs, el * R, 2 * T), bf16),
            pltpu.VMEM((eb * pairs * R, D), bf16), pltpu.VMEM((eb * pairs * R, D), bf16),
            pltpu.VMEM((pairs, el * R, D), bf16), pltpu.VMEM((pairs, el * R, D), bf16),
        ],
        compiler_params=pltpu.CompilerParams(vmem_limit_bytes=VMEM_LIMIT),
        cost_estimate=SHORT,
        name="experts",
    )(after(ids, xcols), *x_msgs, *c_msgs, code, up_weight, down_weight)

    def join(mine, other, name):
        return call(partial(join_body, T), [(mine.shape, bf16)], [mine, L.core(other)], name=name)[0]

    def join_apart(mine, other, name):
        return call(
            partial(join_apart_body, nz), [(mine.shape[1:], bf16)] * nz, [mine, L.core(other)], smem=[ids], name=name
        )

    dx0, dx1, early_far, xc_all = lax.optimization_barrier((dx0, dx1, early_far, xc_all))
    dx_join = join(dx0, dx1, "join_dx")
    dx_parts = L.chips(dx_join)
    gr, du = after((gr, du), dx_join)
    gr1, du1 = L.plane(gr, 1), L.plane(du, 2)
    early_far, gy0, gy1, cc3, xc_all = after((early_far, gy0, gy1, ccols[3], xc_all), dx_join)
    xc_both = L.relay(jnp.stack(xc_all))
    cc_all += [L.plane(cc3, 3)]
    gy_join = join_apart(gy0, gy1, "join_out")
    z_all, a2_s, lia1, hat_s, gates, wsl = call(
        partial(spread_body, S, n_p, w, heads, ea),
        [
            ((S * T, wide), bf16), ((S * T, 128), bf16), ((256, S * T), bf16), ((128, S * T), f32),
            ((S * T, 128), f32), ((128, 2 * hd + 128), bf16),
        ],
        [*L.relay(early_far), query_weight, key_weight, selw],
        smem=[ids],
        cost=LONG,
        name="spread_tokens",
    )
    dx_parts, gr1, du1, z_all, gy_join, cc_all, xc_both = lax.optimization_barrier(
        (dx_parts, gr1, du1, z_all, gy_join, cc_all, xc_both)
    )
    cols_both = xc_both + L.relay(jnp.stack(cc_all))
    gr, du = after((gr, du), dx_parts)
    gr_all = [gr, gr1, L.plane(gr, 2)]
    du_all = [du, L.plane(du, 1), du1]

    dh1, db, mid = call(
        partial(ffn_back_body, n_p, S, nz),
        [((T, D), f32), ((T, D), bf16), ((nz, T + 32, 256), bf16)],
        [dx_parts, h1, cotangent, fsel, ffn_gain[None], padded, cnt],
        scratch=[pltpu.VMEM((EP, T), f32), pltpu.VMEM((S, T, 128), bf16)],
        smem=[ids],
        name="ffn_back",
    )
    mid_far = L.chips(mid)
    late, dp = call(
        attention_back_body,
        [((nz, T, 3 * hd + 128), bf16), ((T, wide), bf16)],
        [db, output_weight, gt, o, q, k, v, a, proj],
        cost=LONG,
        name="attention_back",
    )
    late = after(late, mid_far, gr_all[2], du_all[1])
    gr1, du1 = after((gr1, du1), late)
    gr_all += [L.plane(gr1, 2)]
    du_all += [L.plane(du1, 1)]
    late_far = L.chips(late)
    (input_grad,) = call(
        input_back_body,
        [((T, D), f32)],
        [late, dp, query_weight, key_weight, value_weight, selw, layer_input, att_gain[None], dh1],
        name="input_back",
    )
    mid_far = after(mid_far, input_grad)
    grads_a = call(
        partial(out_grads_body, S, n_p, w),
        [((w, wide + EP + 128), f32)] + [((w, wide + EP + 128), bf16)] * (n_p - 1),
        [*L.relay(mid_far), z_all, a2_s, routes],
        scratch=[
            pltpu.VMEM((128, wide + EP), f32), pltpu.VMEM((S * T, 128), bf16),
            pltpu.VMEM((EP, S * T), bf16), pltpu.VMEM((16, 128), f32),
        ],
        smem=[ids],
        name="out_grads",
    )
    a_parts = L.planes_of(grads_a)
    def expert_grads(first, last, args, so_far=()):
        n = len(args)
        return pl.pallas_call(
            partial(expert_grads_body, n_p, eb, first),
            grid=(last - first,),
            in_specs=whole * 4
            + [pl.BlockSpec((eb, pairs * R, H), lambda i: (i + first, 0, 0))] * (2 * n_p)
            + [pl.BlockSpec(memory_space=pl.ANY)] * len(so_far),
            out_specs=[
                pl.BlockSpec((eb, Dp, H), lambda i: (i + first, 0, 0)),
                pl.BlockSpec((eb, H, Dp), lambda i: (i + first, 0, 0)),
            ],
            scratch_shapes=[
                pltpu.VMEM((n_p * pairs, ep, 2 * T), f32),
                pltpu.VMEM((eb * n_p * pairs * R, 2 * Dp), bf16),
            ],
            out_shape=[jax.ShapeDtypeStruct((el, Dp, H), f32), jax.ShapeDtypeStruct((el, H, Dp), f32)],
            input_output_aliases={n + i: i for i in range(len(so_far))},
            compiler_params=pltpu.CompilerParams(vmem_limit_bytes=VMEM_LIMIT),
            cost_estimate=SHORT,
            name="expert_grads",
        )(*args, *so_far)

    cut = (n_eb + 1) // 2
    grads_in = (*cols_both, *after(gr_all + du_all, grads_a))
    half = expert_grads(0, cut, grads_in)
    late_far, a_parts, half = lax.optimization_barrier((late_far, a_parts, half))
    gy_parts = L.near(after(gy_join, late_far))
    late_block = pl.BlockSpec((1, T, 3 * hd + 128), lambda i: (i, 0, 0))
    grads_b = pl.pallas_call(
        partial(in_grads_body, n_p, heads, ea, w, hd),
        grid=(nz,),
        in_specs=[
            pl.BlockSpec(memory_space=pltpu.SMEM), late_block, late_block,
            pl.BlockSpec((256, 2 * T), lambda i: (0, i)), pl.BlockSpec((128, 2 * T), lambda i: (0, i)),
            pl.BlockSpec((2 * T, 128), lambda i: (i, 0)), whole[0],
        ],
        out_specs=whole * n_p,
        out_shape=[
            jax.ShapeDtypeStruct((w, wide + 2 * hd + 128), f32 if s == 0 else bf16) for s in range(n_p)
        ],
        scratch_shapes=[
            pltpu.VMEM((128, wide + 2 * hd + 128), f32), pltpu.VMEM((2 * T, wide), bf16),
            pltpu.VMEM((2 * T, 2 * hd + 128), bf16), pltpu.VMEM((128, 128), f32),
        ],
        compiler_params=pltpu.CompilerParams(vmem_limit_bytes=VMEM_LIMIT),
        cost_estimate=LONG,
        name="in_grads",
    )(ids, *L.relay(late_far), lia1, hat_s, gates, wsl)
    b_parts = L.planes_of(grads_b)
    up_grad, down_grad = expert_grads(cut, n_eb, after(grads_in, grads_b), half)

    output_grad, fgrad, ffn_gain_grad, ffn_shift_grad, counts = call(
        partial(last_a_body, n_p, S, w, el),
        [((w, wide), f32), ((w, EXPERTS), f32), ((1, w), f32), ((1, w), f32), ((1, EXPERTS), f32)],
        after(a_parts, up_grad),
        scratch=[pltpu.VMEM((8, 128), f32)],
        smem=[ids],
        name="last_sum_a",
    )
    gy_parts, b_parts = after((gy_parts, b_parts), fgrad)
    output = (h1 + sum(m.astype(f32) for m in gy_parts)).astype(bf16)
    value_grad, query_grad, key_grad, vsel, osel, att_gain_grad, att_shift_grad = call(
        partial(last_b_body, n_p, w, hd, he),
        [
            ((w, wide), f32), ((w, hd), f32), ((w, hd), f32), ((he, w), f32), ((he, w), f32),
            ((1, w), f32), ((1, w), f32),
        ],
        after(b_parts, output),
        name="last_sum_b",
    )
    return (
        output, input_grad, att_gain_grad[0], att_shift_grad[0], query_grad, key_grad, value_grad,
        output_grad.T, vsel.T, osel.T, ffn_gain_grad[0], ffn_shift_grad[0], fgrad, up_grad, down_grad, counts[0],
    )


def solution(mesh):
    path = fast_path if mesh.shape["expert"] == 8 and mesh.shape["dp"] == 4 else general_path
    placed = (
        P(("dp", "expert"), None),
        P(("dp", "expert"), None),
        P(("dp", "expert")),
        P(("dp", "expert"), None, None),
        P(("dp", "expert"), None, None),
        P(("dp", "expert"), None),
        P(),
        P(),
        P(),
        P(),
        P(),
        P(),
        P(),
        P(),
        P(),
        P(),
        P(),
        P("expert", None, None),
        P("expert", None, None),
    )
    return jax.shard_map(
        path,
        mesh=mesh,
        in_specs=placed,
        out_specs=(
            P(("dp", "expert"), None),
            P(("dp", "expert"), None),
            P(("dp", "expert")),
            P(("dp", "expert")),
            P(("dp", "expert"), None),
            P(("dp", "expert"), None),
            P(("dp", "expert"), None),
            P(None, ("dp", "expert")),
            P(("dp", "expert"), None),
            P(("dp", "expert"), None),
            P(("dp", "expert")),
            P(("dp", "expert")),
            P(("dp", "expert"), None),
            P("expert", "dp", None),
            P("expert", None, "dp"),
            P(),
        ),
        check_vma=False,
    )
```
